32 devices in a mesh: dp: 4 (over y, x), expert: 8 (over z, core).
Axes of the slice: x: 2, y: 2, z: 4, core: 2. Of those that a mesh axis runs over, the one named last changes fastest.
Arguments:
- tokens: bfloat16 [1024, 4096], P(('dp', 'expert')), may hold values from -6 to 6
- expert_ids: int32 [1024, 8], P(('dp', 'expert')), may hold values from 0 to 15, all different within a row; in each aligned block of 32 rows (0 to 31, 32 to 63, ...) at most 32 rows name the same one
- gate_vals: float32 [1024, 8], P(('dp', 'expert')), may hold values from 0.05 to 0.35
- gate_q: bfloat16 [4, 4096, 3072], P('dp', None, 'expert'), may hold values from -0.09375 to 0.09375
- up_q: bfloat16 [4, 4096, 3072], P('dp', None, 'expert'), may hold values from -0.09375 to 0.09375
- down_q: bfloat16 [4, 3072, 4096], P('dp', 'expert'), may hold values from -0.21875 to 0.21875
- gate_scale: float32 [4, 32, 24], P('dp', None, 'expert'), may hold values from 0.25 to 2
- up_scale: float32 [4, 32, 24], P('dp', None, 'expert'), may hold values from 0.25 to 2
- down_scale: float32 [4, 24, 32], P('dp', 'expert'), may hold values from 0.25 to 2
Outputs:
- mixed: bfloat16 [1024, 4096], P(('dp', 'expert'))
The draws below stay inside these ranges and needn't reach their ends.
Inputs may be any that keep to these rules, and one draw needn't show every extreme that they name: `expert_ids`: each token names 8 different experts; the 32 tokens of one device name any one expert at most 32 times, and some device names some expert exactly 32 times.
All inputs are finite; a program needn't handle non-finite values.
Results may differ from the reference program's by a relative error of at most 0.006.
Values may be sent and summed in bfloat16 or wider, within the bound.
No kernel may reach another device: no remote copies, remote signals or barrier semaphores. Data moves between devices by JAX's collectives and lax.ppermute only.
A program may use at most 128 MiB of HBM per device.

```python
import math
import jax
import jax.numpy as jnp
import numpy as np
from jax import lax

D = 4096
FF = 768
TOP = 8
BLOCK = 128
TOK_DEV = 32
PAIRS = 4
EXPERTS = 16
CAP = 32
TOKENS = 1024
N_DP = 4


def block_levels(key, extent, shards, least, largest):
    gain = 1.0
    for dim, shards_of in shards:
        draws = jax.random.uniform(jax.random.fold_in(jax.random.fold_in(key, 6), dim), (shards_of,), jnp.float32, least / len(shards), largest / len(shards))
        gain = gain * jnp.repeat(jnp.exp(draws), extent[dim] // shards_of).reshape((-1,) + (1,) * (len(extent) - 1 - dim))
    return gain


def deal_out(rng, own, number, rows, amount, top, limit, skew):
    sequence = jax.random.permutation(rng, amount)
    packed, ordinary = portions_of(amount, rows * top, limit, skew, True), portions_of(amount, rows * top, limit, skew, False)
    places = jnp.arange(amount)

    def named(sizes, turn):
        used = int((sizes > 0).sum())
        fixed = max(1, used // 4)
        moved = fixed + (places - fixed + turn * (used - fixed)) % max(1, amount - fixed)
        return jnp.zeros((amount,), jnp.int32).at[sequence[jnp.where(places < fixed, places, moved)]].set(jnp.asarray(sizes, jnp.int32))

    sizes = jnp.where(number % 4 == 0, named(packed, number // 4), named(ordinary, number - number // 4 - 1))
    mixed = jax.random.permutation(jax.random.fold_in(own, 3), amount)
    source_of, taker = mixed[0:amount // 2 * 2:2], mixed[1:amount // 2 * 2:2]
    margin = jnp.minimum(sizes[source_of] - 1, limit - sizes[taker]) // 2
    margin = jnp.where((source_of == sequence[0]) | (taker == sequence[0]) | (sizes[taker] == 0), 0, jnp.maximum(margin, 0))
    moved = jax.random.randint(jax.random.fold_in(own, 4), (amount // 2,), 0, 1 << 20) % (margin + 1)
    sizes = sizes.at[source_of].add(-moved).at[taker].add(moved)
    members = jnp.searchsorted(jnp.cumsum(sizes), jnp.arange(rows * top), side="right").astype(jnp.int32)
    listing = members.reshape(top, rows).T
    listing = listing[jax.random.permutation(jax.random.fold_in(own, 1), rows)]
    turn = jax.random.randint(jax.random.fold_in(own, 2), (rows, 1), 0, top)
    return jnp.take_along_axis(listing, (jnp.arange(top)[None, :] + turn) % top, axis=1)


def portions_of(amount, total, bound, lean, full):
    loads = [(1 << 20) // math.isqrt(standing ** lean) + 1 for standing in range(1, amount + 1)]
    largest = bound if full else min(bound, max(-(-total // amount), total * loads[0] // sum(loads)))
    least = 1 if total - largest >= amount - 1 else 0
    holding, surplus = [largest] + [least] * (amount - 1), total - largest - least * (amount - 1)
    while surplus > 0:
        candidates = [i for i in range(1, amount) if holding[i] < largest] or [i for i in range(1, amount) if holding[i] < bound]
        mass, budget = sum([loads[i] for i in candidates]), surplus
        for i in candidates:
            extra = min(bound - holding[i], max(1, budget * loads[i] // mass), surplus)
            holding[i] = holding[i] + extra
            surplus = surplus - extra
    return np.array(holding)


def bell_draw(rng, extent, width, bound, shards=(), kind=jnp.bfloat16):
    drawn = jax.random.normal(rng, extent, jnp.float32) * width
    if len(shards) > 0:
        drawn = block_levels(rng, extent, shards, -0.22, 0.18) * drawn
    return jnp.clip(drawn, min=-bound, max=bound).astype(kind)


def setup_inputs(seed: int = 0) -> dict:
    key_of = jax.random.split(jax.random.key(seed), 10)
    tokens = bell_draw(key_of[0], (TOKENS, D), 1.0, 6.0, ((0, 32),))
    expert_ids_keys = jax.random.split(jax.random.fold_in(key_of[1], 1), TOKENS // TOK_DEV)
    expert_ids_turns = jax.random.permutation(jax.random.fold_in(key_of[1], 3), TOKENS // TOK_DEV)
    expert_ids = jax.vmap(lambda own, number: deal_out(jax.random.fold_in(key_of[1], 2), own, number, TOK_DEV, EXPERTS, TOP, CAP, 2))(expert_ids_keys, expert_ids_turns).reshape((TOKENS, TOP))
    gate_vals = jnp.clip(0.05 + 0.29999999 * jax.random.uniform(key_of[2], (TOKENS, TOP), jnp.float32) ** block_levels(key_of[2], (TOKENS, TOP), ((0, 32),), -0.2, 0.2), 0.05, 0.35)
    gate_q = bell_draw(key_of[3], (N_DP, D, PAIRS * FF), D ** -0.5, 0.09375, ((0, 4), (2, 8)))
    up_q = bell_draw(key_of[4], (N_DP, D, PAIRS * FF), D ** -0.5, 0.09375, ((0, 4), (2, 8)))
    down_q = bell_draw(key_of[5], (N_DP, PAIRS * FF, D), FF ** -0.5, 0.21875, ((0, 4), (1, 8)))
    gate_scale = jnp.clip(jnp.exp(math.log(2.0) - 2.0794415 * jax.random.uniform(key_of[6], (N_DP, D // BLOCK, PAIRS * FF // BLOCK), jnp.float32) ** block_levels(key_of[6], (N_DP, D // BLOCK, PAIRS * FF // BLOCK), ((0, 4), (2, 8)), -0.2, 0.2)), 0.25, 2.0)
    up_scale = jnp.clip(jnp.exp(math.log(2.0) - 2.0794415 * jax.random.uniform(key_of[7], (N_DP, D // BLOCK, PAIRS * FF // BLOCK), jnp.float32) ** block_levels(key_of[7], (N_DP, D // BLOCK, PAIRS * FF // BLOCK), ((0, 4), (2, 8)), -0.2, 0.2)), 0.25, 2.0)
    down_scale = jnp.clip(jnp.exp(math.log(2.0) - 2.0794415 * jax.random.uniform(key_of[8], (N_DP, PAIRS * FF // BLOCK, D // BLOCK), jnp.float32) ** block_levels(key_of[8], (N_DP, PAIRS * FF // BLOCK, D // BLOCK), ((0, 4), (1, 8)), -0.2, 0.2)), 0.25, 2.0)
    return {"tokens": tokens, "expert_ids": expert_ids, "gate_vals": gate_vals, "gate_q": gate_q, "up_q": up_q, "down_q": down_q, "gate_scale": gate_scale, "up_scale": up_scale, "down_scale": down_scale}


def dequantize(quant_vals, block_scale):
    full_scale = jnp.repeat(jnp.repeat(block_scale, BLOCK, axis=0), BLOCK, axis=1)
    return (quant_vals.astype(jnp.float32) * full_scale).astype(jnp.bfloat16)


def expert_ffn(inputs, w_gate, w_up, w_down):
    gate_part = jnp.dot(inputs, w_gate, preferred_element_type=jnp.float32)
    up_part = jnp.dot(inputs, w_up, preferred_element_type=jnp.float32)
    hidden = (jax.nn.silu(gate_part) * up_part).astype(jnp.bfloat16)
    return jnp.dot(hidden, w_down, preferred_element_type=jnp.float32)


def reference(tokens, expert_ids, gate_vals, gate_q, up_q, down_q, gate_scale, up_scale, down_scale):
    row_total = (TOKENS // TOK_DEV) * CAP
    scale_cols = FF // BLOCK

    def per_expert(summed, expert):
        group_of = expert // PAIRS
        pair_of = expert % PAIRS
        gate_rows = lax.dynamic_index_in_dim(gate_q, group_of, 0, keepdims=False)
        up_rows = lax.dynamic_index_in_dim(up_q, group_of, 0, keepdims=False)
        down_rows = lax.dynamic_index_in_dim(down_q, group_of, 0, keepdims=False)
        gate_block = lax.dynamic_index_in_dim(gate_scale, group_of, 0, keepdims=False)
        up_block = lax.dynamic_index_in_dim(up_scale, group_of, 0, keepdims=False)
        down_block = lax.dynamic_index_in_dim(down_scale, group_of, 0, keepdims=False)
        w_gate = dequantize(lax.dynamic_slice_in_dim(gate_rows, pair_of * FF, FF, 1),
                            lax.dynamic_slice_in_dim(gate_block, pair_of * scale_cols, scale_cols, 1))
        w_up = dequantize(lax.dynamic_slice_in_dim(up_rows, pair_of * FF, FF, 1),
                          lax.dynamic_slice_in_dim(up_block, pair_of * scale_cols, scale_cols, 1))
        w_down = dequantize(lax.dynamic_slice_in_dim(down_rows, pair_of * FF, FF, 0),
                            lax.dynamic_slice_in_dim(down_block, pair_of * scale_cols, scale_cols, 0))
        matched = expert_ids == expert
        routed = jnp.any(matched, axis=1)
        position = jnp.cumsum(routed.astype(jnp.int32)) - 1
        target = jnp.where(routed, position, row_total).astype(jnp.int32)
        buffer = jnp.zeros((row_total, D), jnp.bfloat16).at[target].set(tokens, mode="drop")
        expert_out = expert_ffn(buffer, w_gate, w_up, w_down).astype(jnp.bfloat16)
        token_gate = jnp.sum(jnp.where(matched, gate_vals, 0.0), axis=1)
        picked = expert_out[jnp.minimum(target, row_total - 1)].astype(jnp.float32) * token_gate[:, None]
        return summed + picked, None

    summed, unused = lax.scan(per_expert, jnp.zeros((TOKENS, D), jnp.float32),
                              jnp.arange(EXPERTS, dtype=jnp.int32))
    return (tokens.astype(jnp.float32) + summed).astype(jnp.bfloat16)
```

```python
import jax
import jax.numpy as jnp
from jax import lax
from jax.sharding import PartitionSpec as P

BLOCK = 128


def from_partner(block, axis, bit):
    count = lax.axis_size(axis)
    route = []
    for low in range(count):
        high = low | 1 << bit
        if high != low and high < count:
            route += [(low, high), (high, low)]
    return lax.ppermute(block, axis, route)


def dequantize(quant_vals, block_scale):
    row_count, col_count = quant_vals.shape
    blocked = quant_vals.reshape(row_count // BLOCK, BLOCK, col_count // BLOCK, BLOCK).astype(
        jnp.float32
    )
    scaled = blocked * block_scale[:, None, :, None]
    return scaled.reshape(row_count, col_count).astype(jnp.bfloat16)


def expert_ffn(inputs, w_gate, w_up, w_down):
    gate_part = jnp.dot(inputs, w_gate, preferred_element_type=jnp.float32)
    up_part = jnp.dot(inputs, w_up, preferred_element_type=jnp.float32)
    hidden = (jax.nn.silu(gate_part) * up_part).astype(jnp.bfloat16)
    return jnp.dot(hidden, w_down, preferred_element_type=jnp.float32)


def across_groups(blocks):
    return lax.all_to_all(blocks, "dp", split_axis=1, concat_axis=1, tiled=True)


def across_owners(blocks):
    return lax.all_to_all(blocks, "expert", split_axis=0, concat_axis=0, tiled=True)


def by_rows(tokens, expert_ids, gate_vals, gate_q, up_q, down_q, gate_scale, up_scale, down_scale):
    group_count = lax.axis_size("dp")
    owner_count = lax.axis_size("expert")
    token_count, model_width = tokens.shape
    top_count = expert_ids.shape[1]
    pair_count = owner_count // 2
    expert_count = group_count * pair_count
    capacity = 2 * token_count * top_count // expert_count
    half_cap = capacity // 2
    slot_count = owner_count * group_count * half_cap
    routes = expert_ids.reshape(-1)
    onehot = (routes[:, None] == jnp.arange(expert_count, dtype=jnp.int32)[None, :]).astype(
        jnp.int32
    )
    earlier = jnp.cumsum(onehot, axis=0) - onehot
    route_slot = jnp.sum(earlier * onehot, axis=1)
    route_group = routes // pair_count
    route_pair = routes % pair_count
    route_owner = 2 * route_pair + route_slot // half_cap
    route_place = route_slot % half_cap
    route_index = (route_owner * group_count + route_group) * half_cap + route_place
    chosen = jnp.arange(slot_count, dtype=jnp.int32)[:, None] == route_index[None, :]
    chosen = jnp.any(chosen.reshape(slot_count, token_count, top_count), axis=2).astype(
        jnp.bfloat16
    )
    outgoing = jnp.dot(chosen, tokens, preferred_element_type=jnp.float32).astype(jnp.bfloat16)
    outgoing = outgoing.reshape(owner_count, group_count, half_cap, model_width)
    arrived = across_owners(across_groups(outgoing))
    own_rows = arrived.reshape(-1, model_width)
    row_count = own_rows.shape[0]
    w_gate = dequantize(gate_q[0], gate_scale[0])
    w_up = dequantize(up_q[0], up_scale[0])
    w_down = dequantize(down_q[0], down_scale[0])
    partner_rows = from_partner(own_rows, "expert", 0)
    both_rows = jnp.concatenate([own_rows, partner_rows], axis=0)
    partial_value = expert_ffn(both_rows, w_gate, w_up, w_down)
    returned = from_partner(partial_value[row_count:], "expert", 0)
    expert_out = (partial_value[:row_count] + returned).astype(jnp.bfloat16)
    expert_out = expert_out.reshape(owner_count, group_count, half_cap, model_width)
    returned_rows = across_groups(across_owners(expert_out))
    returned_rows = returned_rows.reshape(slot_count, model_width)
    picked = returned_rows[route_index].reshape(token_count, top_count, model_width)
    weighted = jnp.einsum("tkd,tk->td", picked.astype(jnp.float32), gate_vals)
    mixed = tokens.astype(jnp.float32) + weighted
    return mixed.astype(jnp.bfloat16)


def by_sums(tokens, expert_ids, gate_vals, gate_q, up_q, down_q, gate_scale, up_scale, down_scale):
    both = ("dp", "expert")
    pair_count = lax.axis_size("expert") // 2
    expert_count = lax.axis_size("dp") * pair_count
    own_expert = lax.axis_index("dp") * pair_count + lax.axis_index("expert") // 2
    named = expert_ids[:, :, None] == jnp.arange(expert_count, dtype=jnp.int32)[None, None, :]
    weight = jnp.sum(jnp.where(named, gate_vals[:, :, None], 0.0), axis=1)
    all_weights = lax.all_gather(weight, both, axis=0, tiled=True)
    own_weight = jnp.sum(
        jnp.where(jnp.arange(expert_count)[None, :] == own_expert, all_weights, 0.0), axis=1
    )
    all_tokens = lax.all_gather(tokens, both, axis=0, tiled=True)
    w_gate = dequantize(gate_q[0], gate_scale[0])
    w_up = dequantize(up_q[0], up_scale[0])
    w_down = dequantize(down_q[0], down_scale[0])
    partial_value = expert_ffn(all_tokens, w_gate, w_up, w_down) * own_weight[:, None]
    summed = lax.psum_scatter(
        partial_value.astype(jnp.bfloat16), both, scatter_dimension=0, tiled=True
    )
    mixed = tokens.astype(jnp.float32) + summed.astype(jnp.float32)
    return mixed.astype(jnp.bfloat16)


def shards(tokens, expert_ids, *weights):
    expert_count = lax.axis_size("dp") * lax.axis_size("expert") // 2
    token_count, top_count = expert_ids.shape
    capacity = 2 * token_count * top_count // expert_count
    plan = by_rows if capacity < token_count else by_sums
    return plan(tokens, expert_ids, *weights)


def solution(mesh):
    return jax.shard_map(
        shards,
        mesh=mesh,
        in_specs=(
            P(("dp", "expert"), None),
            P(("dp", "expert"), None),
            P(("dp", "expert"), None),
            P("dp", None, "expert"),
            P("dp", None, "expert"),
            P("dp", "expert", None),
            P("dp", None, "expert"),
            P("dp", None, "expert"),
            P("dp", "expert", None),
        ),
        out_specs=P(("dp", "expert"), None),
        check_vma=False,
    )
```

```python
import jax
import jax.numpy as jnp
from jax import lax
from jax.sharding import PartitionSpec as P

BLOCK = 128


def from_partner(block, axis, bit):
    count = lax.axis_size(axis)
    route = []
    for low in range(count):
        high = low | 1 << bit
        if high != low and high < count:
            route += [(low, high), (high, low)]
    return lax.ppermute(block, axis, route)


def dequantize(quant_vals, block_scale):
    row_count, col_count = quant_vals.shape
    blocked = quant_vals.reshape(row_count // BLOCK, BLOCK, col_count // BLOCK, BLOCK).astype(
        jnp.float32
    )
    scaled = blocked * block_scale[:, None, :, None]
    return scaled.reshape(row_count, col_count).astype(jnp.bfloat16)


def expert_ffn(inputs, w_gate, w_up, w_down):
    gate_part = jnp.dot(inputs, w_gate, preferred_element_type=jnp.float32)
    up_part = jnp.dot(inputs, w_up, preferred_element_type=jnp.float32)
    hidden = (jax.nn.silu(gate_part) * up_part).astype(jnp.bfloat16)
    return jnp.dot(hidden, w_down, preferred_element_type=jnp.float32)


def across_groups(blocks):
    return lax.all_to_all(blocks, "dp", split_axis=1, concat_axis=1, tiled=True)


def across_owners(blocks):
    return lax.all_to_all(blocks, "expert", split_axis=0, concat_axis=0, tiled=True)


def by_rows(tokens, expert_ids, gate_vals, gate_q, up_q, down_q, gate_scale, up_scale, down_scale):
    group_count = lax.axis_size("dp")
    owner_count = lax.axis_size("expert")
    token_count, model_width = tokens.shape
    top_count = expert_ids.shape[1]
    pair_count = owner_count // 2
    expert_count = group_count * pair_count
    capacity = 2 * token_count * top_count // expert_count
    half_cap = capacity // 2
    slot_count = owner_count * group_count * half_cap
    routes = expert_ids.reshape(-1)
    onehot = (routes[:, None] == jnp.arange(expert_count, dtype=jnp.int32)[None, :]).astype(
        jnp.int32
    )
    earlier = jnp.cumsum(onehot, axis=0) - onehot
    route_slot = jnp.sum(earlier * onehot, axis=1)
    route_group = routes // pair_count
    route_pair = routes % pair_count
    route_owner = 2 * route_pair + route_slot // half_cap
    route_place = route_slot % half_cap
    route_index = (route_owner * group_count + route_group) * half_cap + route_place
    chosen = jnp.arange(slot_count, dtype=jnp.int32)[:, None] == route_index[None, :]
    chosen = jnp.any(chosen.reshape(slot_count, token_count, top_count), axis=2).astype(
        jnp.bfloat16
    )
    outgoing = jnp.dot(chosen, tokens, preferred_element_type=jnp.float32).astype(jnp.bfloat16)
    outgoing = outgoing.reshape(owner_count, group_count, half_cap, model_width)
    arrived = across_owners(across_groups(outgoing))
    own_rows = arrived.reshape(-1, model_width)
    row_count = own_rows.shape[0]
    w_gate = dequantize(gate_q[0], gate_scale[0])
    w_up = dequantize(up_q[0], up_scale[0])
    w_down = dequantize(down_q[0], down_scale[0])
    partner_rows = from_partner(own_rows, "expert", 0)
    both_rows = jnp.concatenate([own_rows, partner_rows], axis=0)
    partial_value = expert_ffn(both_rows, w_gate, w_up, w_down)
    returned = from_partner(partial_value[row_count:], "expert", 0)
    expert_out = (partial_value[:row_count] + returned).astype(jnp.bfloat16)
    expert_out = expert_out.reshape(owner_count, group_count, half_cap, model_width)
    returned_rows = across_groups(across_owners(expert_out))
    returned_rows = returned_rows.reshape(slot_count, model_width)
    picked = returned_rows[route_index].reshape(token_count, top_count, model_width)
    weighted = jnp.einsum("tkd,tk->td", picked.astype(jnp.float32), gate_vals)
    mixed = tokens.astype(jnp.float32) + weighted
    return mixed.astype(jnp.bfloat16)


def gather_groups(block, order):
    for bit in order:
        block = jnp.concatenate([block, from_partner(block, "dp", bit)], axis=0)
    return block


def sum_groups(block, order):
    for bit in reversed(order):
        kept, sent = jnp.split(block, 2, axis=0)
        arrived = from_partner(sent, "dp", bit)
        block = (kept.astype(jnp.float32) + arrived.astype(jnp.float32)).astype(jnp.bfloat16)
    return block


def across_chips(block, far):
    count = lax.axis_size("expert")
    return lax.ppermute(block, "expert", [(low, low ^ 2 * far) for low in range(count)])


def by_sums(tokens, expert_ids, gate_vals, gate_q, up_q, down_q, gate_scale, up_scale, down_scale):
    token_count, model_width = tokens.shape
    group_count = lax.axis_size("dp")
    pair_count = lax.axis_size("expert") // 2
    expert_count = group_count * pair_count
    own_expert = lax.axis_index("dp") * pair_count + lax.axis_index("expert") // 2
    half = token_count // 2
    bits = list(range(group_count.bit_length() - 1))
    orders = (bits, bits[::-1])

    named = expert_ids[:, :, None] == jnp.arange(expert_count, dtype=jnp.int32)[None, None, :]
    weight = jnp.sum(jnp.where(named, gate_vals[:, :, None], 0.0), axis=1)
    high = weight.astype(jnp.bfloat16)
    low = (weight - high.astype(jnp.float32)).astype(jnp.bfloat16)
    extra = -(-2 * expert_count // BLOCK) * BLOCK
    pad = jnp.zeros((token_count, extra - 2 * expert_count), jnp.bfloat16)
    payload = jnp.concatenate([tokens, high, low, pad], axis=1)

    w_gate = dequantize(gate_q[0], gate_scale[0])
    w_up = dequantize(up_q[0], up_scale[0])
    w_down = dequantize(down_q[0], down_scale[0])
    in_own = jnp.concatenate([w_gate, w_up], axis=1)
    in_other = from_partner(in_own, "expert", 0)
    down_other = from_partner(w_down, "expert", 0)
    down_both = jnp.concatenate([w_down, down_other], axis=0)
    hidden_half = w_gate.shape[1]

    def ffn(rows):
        inputs = rows[:, :model_width]
        marks = rows[:, model_width:].astype(jnp.float32)
        column = jnp.arange(extra, dtype=jnp.int32)[None, :]
        chosen = (column == own_expert) | (column == own_expert + expert_count)
        row_weight = jnp.sum(jnp.where(chosen, marks, 0.0), axis=1)
        hidden = []
        for w_in in (in_own, in_other):
            parts = jnp.dot(inputs, w_in, preferred_element_type=jnp.float32)
            hidden.append(
                (jax.nn.silu(parts[:, :hidden_half]) * parts[:, hidden_half:]).astype(jnp.bfloat16)
            )
        hidden = jnp.concatenate(hidden, axis=1)
        value = jnp.dot(hidden, down_both, preferred_element_type=jnp.float32)
        return (value * row_weight[:, None]).astype(jnp.bfloat16)

    from_far = {far: across_chips(payload, far) for far in range(1, pair_count)}
    from_far[0] = payload
    total = tokens.astype(jnp.float32)
    step = 2
    for first in range(0, pair_count, step):
        fars = range(first, first + step)
        gathered = []
        for place, order in enumerate(orders):
            rows = slice(place * half, (place + 1) * half)
            block = jnp.stack([from_far[far][rows] for far in fars])[None]
            gathered.append(gather_groups(block, order))
        every = jnp.stack(gathered)
        out = ffn(every.reshape(-1, every.shape[-1]))
        out = out.reshape(every.shape[:-1] + (model_width,))
        sums = [sum_groups(out[place], order)[0] for place, order in enumerate(orders)]
        sums = jnp.concatenate(sums, axis=1)
        for place, far in enumerate(fars):
            block = sums[place]
            if far > 0:
                block = across_chips(block, far)
            total = total + block.astype(jnp.float32)
    return total.astype(jnp.bfloat16)


def shards(tokens, expert_ids, *weights):
    expert_count = lax.axis_size("dp") * lax.axis_size("expert") // 2
    token_count, top_count = expert_ids.shape
    capacity = 2 * token_count * top_count // expert_count
    plan = by_rows if capacity < token_count else by_sums
    return plan(tokens, expert_ids, *weights)


def solution(mesh):
    return jax.shard_map(
        shards,
        mesh=mesh,
        in_specs=(
            P(("dp", "expert"), None),
            P(("dp", "expert"), None),
            P(("dp", "expert"), None),
            P("dp", None, "expert"),
            P("dp", None, "expert"),
            P("dp", "expert", None),
            P("dp", None, "expert"),
            P("dp", None, "expert"),
            P("dp", "expert", None),
        ),
        out_specs=P(("dp", "expert"), None),
        check_vma=False,
    )
```

```python
import functools

import jax
import jax.numpy as jnp
from jax import lax
from jax.experimental import pallas as pl
from jax.experimental.pallas import tpu as pltpu
from jax.sharding import PartitionSpec as P

BLOCK = 128


def from_partner(block, axis, bit):
    count = lax.axis_size(axis)
    route = []
    for low in range(count):
        high = low | 1 << bit
        if high != low and high < count:
            route += [(low, high), (high, low)]
    return lax.ppermute(block, axis, route)


def dequantize(quant_vals, block_scale):
    row_count, col_count = quant_vals.shape
    blocked = quant_vals.reshape(row_count // BLOCK, BLOCK, col_count // BLOCK, BLOCK).astype(
        jnp.float32
    )
    scaled = blocked * block_scale[:, None, :, None]
    return scaled.reshape(row_count, col_count).astype(jnp.bfloat16)


def expert_ffn(inputs, w_gate, w_up, w_down):
    gate_part = jnp.dot(inputs, w_gate, preferred_element_type=jnp.float32)
    up_part = jnp.dot(inputs, w_up, preferred_element_type=jnp.float32)
    hidden = (jax.nn.silu(gate_part) * up_part).astype(jnp.bfloat16)
    return jnp.dot(hidden, w_down, preferred_element_type=jnp.float32)


def across_groups(blocks):
    return lax.all_to_all(blocks, "dp", split_axis=1, concat_axis=1, tiled=True)


def across_owners(blocks):
    return lax.all_to_all(blocks, "expert", split_axis=0, concat_axis=0, tiled=True)


def by_rows(tokens, expert_ids, gate_vals, gate_q, up_q, down_q, gate_scale, up_scale, down_scale):
    group_count = lax.axis_size("dp")
    owner_count = lax.axis_size("expert")
    token_count, model_width = tokens.shape
    top_count = expert_ids.shape[1]
    pair_count = owner_count // 2
    expert_count = group_count * pair_count
    capacity = 2 * token_count * top_count // expert_count
    half_cap = capacity // 2
    slot_count = owner_count * group_count * half_cap
    routes = expert_ids.reshape(-1)
    onehot = (routes[:, None] == jnp.arange(expert_count, dtype=jnp.int32)[None, :]).astype(
        jnp.int32
    )
    earlier = jnp.cumsum(onehot, axis=0) - onehot
    route_slot = jnp.sum(earlier * onehot, axis=1)
    route_group = routes // pair_count
    route_pair = routes % pair_count
    route_owner = 2 * route_pair + route_slot // half_cap
    route_place = route_slot % half_cap
    route_index = (route_owner * group_count + route_group) * half_cap + route_place
    chosen = jnp.arange(slot_count, dtype=jnp.int32)[:, None] == route_index[None, :]
    chosen = jnp.any(chosen.reshape(slot_count, token_count, top_count), axis=2).astype(
        jnp.bfloat16
    )
    outgoing = jnp.dot(chosen, tokens, preferred_element_type=jnp.float32).astype(jnp.bfloat16)
    outgoing = outgoing.reshape(owner_count, group_count, half_cap, model_width)
    arrived = across_owners(across_groups(outgoing))
    own_rows = arrived.reshape(-1, model_width)
    row_count = own_rows.shape[0]
    w_gate = dequantize(gate_q[0], gate_scale[0])
    w_up = dequantize(up_q[0], up_scale[0])
    w_down = dequantize(down_q[0], down_scale[0])
    partner_rows = from_partner(own_rows, "expert", 0)
    both_rows = jnp.concatenate([own_rows, partner_rows], axis=0)
    partial_value = expert_ffn(both_rows, w_gate, w_up, w_down)
    returned = from_partner(partial_value[row_count:], "expert", 0)
    expert_out = (partial_value[:row_count] + returned).astype(jnp.bfloat16)
    expert_out = expert_out.reshape(owner_count, group_count, half_cap, model_width)
    returned_rows = across_groups(across_owners(expert_out))
    returned_rows = returned_rows.reshape(slot_count, model_width)
    picked = returned_rows[route_index].reshape(token_count, top_count, model_width)
    weighted = jnp.einsum("tkd,tk->td", picked.astype(jnp.float32), gate_vals)
    mixed = tokens.astype(jnp.float32) + weighted
    return mixed.astype(jnp.bfloat16)


def gather_groups(block, order):
    for bit in order:
        block = jnp.concatenate([block, from_partner(block, "dp", bit)], axis=0)
    return block


def sum_groups(block, order):
    for bit in reversed(order):
        kept, sent = jnp.split(block, 2, axis=0)
        arrived = from_partner(sent, "dp", bit)
        block = (kept.astype(jnp.float32) + arrived.astype(jnp.float32)).astype(jnp.bfloat16)
    return block


def scaled(block, scale):
    return (block.astype(jnp.float32) * scale).astype(jnp.bfloat16)


def in_kernel(block_cols, scales, gate_ref, up_ref, out_ref):
    strip = gate_ref.shape[0] // BLOCK
    first = pl.program_id(0) * strip
    up_at = pl.num_programs(0) * strip * block_cols
    for row in range(strip):
        rows = slice(row * BLOCK, (row + 1) * BLOCK)
        for col in range(block_cols):
            cols = slice(col * BLOCK, (col + 1) * BLOCK)
            place = (first + row) * block_cols + col
            out_ref[rows, cols] = scaled(gate_ref[rows, cols], scales[place])
            cols_up = slice((block_cols + col) * BLOCK, (block_cols + col + 1) * BLOCK)
            out_ref[rows, cols_up] = scaled(up_ref[rows, cols], scales[up_at + place])


def dequantize_in(gate, up, scales):
    rows, cols = gate.shape
    strip = min(rows, 4 * BLOCK)
    block = pl.BlockSpec((strip, cols), lambda i: (i, 0))
    return pl.pallas_call(
        functools.partial(in_kernel, cols // BLOCK),
        grid=(rows // strip,),
        in_specs=[pl.BlockSpec(memory_space=pltpu.SMEM), block, block],
        out_specs=pl.BlockSpec((strip, 2 * cols), lambda i: (i, 0)),
        out_shape=jax.ShapeDtypeStruct((rows, 2 * cols), jnp.bfloat16),
        cost_estimate=pl.CostEstimate(
            flops=2 * rows * cols, bytes_accessed=8 * rows * cols, transcendentals=0
        ),
        name="dequantize_in",
    )(scales, gate, up)


def down_kernel(at, block_cols, scales_own, scales_other, own_ref, other_ref, out_ref):
    strip = own_ref.shape[1] // BLOCK
    block_rows = own_ref.shape[0] // BLOCK
    first = pl.program_id(0) * strip
    for half, (scales, ref) in enumerate(((scales_own, own_ref), (scales_other, other_ref))):
        for row in range(block_rows):
            rows = slice(row * BLOCK, (row + 1) * BLOCK)
            out_row = (half * block_rows + row) * BLOCK
            for col in range(strip):
                cols = slice(col * BLOCK, (col + 1) * BLOCK)
                scale = scales[at + row * block_cols + first + col]
                out_ref[out_row : out_row + BLOCK, cols] = scaled(ref[rows, cols], scale)


def dequantize_down(own, other, scales_own, scales_other, at):
    rows, cols = own.shape
    strip = min(cols, 4 * BLOCK)
    block = pl.BlockSpec((rows, strip), lambda i: (0, i))
    smem = pl.BlockSpec(memory_space=pltpu.SMEM)
    return pl.pallas_call(
        functools.partial(down_kernel, at, cols // BLOCK),
        grid=(cols // strip,),
        in_specs=[smem, smem, block, block],
        out_specs=pl.BlockSpec((2 * rows, strip), lambda i: (0, i)),
        out_shape=jax.ShapeDtypeStruct((2 * rows, cols), jnp.bfloat16),
        cost_estimate=pl.CostEstimate(
            flops=2 * rows * cols, bytes_accessed=8 * rows * cols, transcendentals=0
        ),
        name="dequantize_down",
    )(scales_own, scales_other, own, other)


def across_chips(block, far):
    count = lax.axis_size("expert")
    return lax.ppermute(block, "expert", [(low, low ^ 2 * far) for low in range(count)])


def by_sums(tokens, expert_ids, gate_vals, gate_q, up_q, down_q, gate_scale, up_scale, down_scale):
    token_count, model_width = tokens.shape
    group_count = lax.axis_size("dp")
    pair_count = lax.axis_size("expert") // 2
    expert_count = group_count * pair_count
    own_expert = lax.axis_index("dp") * pair_count + lax.axis_index("expert") // 2
    bits = list(range(group_count.bit_length() - 1))
    orders = (bits, bits[::-1])

    named = expert_ids[:, :, None] == jnp.arange(expert_count, dtype=jnp.int32)[None, None, :]
    weight = jnp.sum(jnp.where(named, gate_vals[:, :, None], 0.0), axis=1)
    high = weight.astype(jnp.bfloat16)
    low = (weight - high.astype(jnp.float32)).astype(jnp.bfloat16)
    extra = -(-2 * expert_count // BLOCK) * BLOCK
    pad = jnp.zeros((token_count, extra - 2 * expert_count), jnp.bfloat16)
    payload = jnp.concatenate([tokens, high, low, pad], axis=1)

    quant = [gate_q[0], up_q[0], down_q[0]]
    hidden_half = gate_q.shape[2]
    scales = jnp.concatenate([s.reshape(-1) for s in (gate_scale, up_scale, down_scale)])
    scales_other = from_partner(scales, "expert", 0)
    gate_other, up_other, down_other = [from_partner(q, "expert", 0) for q in quant]
    in_own = dequantize_in(quant[0], quant[1], scales)
    in_other = dequantize_in(gate_other, up_other, scales_other)
    down_at = gate_scale.size + up_scale.size
    down_both = dequantize_down(quant[2], down_other, scales, scales_other, down_at)

    def ffn(rows):
        inputs = rows[:, :model_width]
        marks = rows[:, model_width:].astype(jnp.float32)
        column = jnp.arange(extra, dtype=jnp.int32)[None, :]
        chosen = (column == own_expert) | (column == own_expert + expert_count)
        row_weight = jnp.sum(jnp.where(chosen, marks, 0.0), axis=1)
        hidden = []
        for w_in in (in_own, in_other):
            parts = jnp.dot(inputs, w_in, preferred_element_type=jnp.float32)
            hidden.append(
                (jax.nn.silu(parts[:, :hidden_half]) * parts[:, hidden_half:]).astype(jnp.bfloat16)
            )
        hidden = jnp.concatenate(hidden, axis=1)
        value = jnp.dot(hidden, down_both, preferred_element_type=jnp.float32)
        return (value * row_weight[:, None]).astype(jnp.bfloat16)

    outs = {}
    for far in range(pair_count):
        block = payload if far == 0 else across_chips(payload, far)
        every = gather_groups(block[None], orders[far % 2])
        outs[far] = ffn(every.reshape(-1, every.shape[-1]))
    total = tokens.astype(jnp.float32)
    for far in [*range(2, pair_count), 1, 0][-pair_count:]:
        out = outs[far].reshape(group_count, token_count, model_width)
        block = sum_groups(out, orders[far % 2])[0]
        if far > 0:
            block = across_chips(block, far)
        total = total + block.astype(jnp.float32)
    return total.astype(jnp.bfloat16)


def shards(tokens, expert_ids, *weights):
    expert_count = lax.axis_size("dp") * lax.axis_size("expert") // 2
    token_count, top_count = expert_ids.shape
    capacity = 2 * token_count * top_count // expert_count
    plan = by_rows if capacity < token_count else by_sums
    return plan(tokens, expert_ids, *weights)


def solution(mesh):
    return jax.shard_map(
        shards,
        mesh=mesh,
        in_specs=(
            P(("dp", "expert"), None),
            P(("dp", "expert"), None),
            P(("dp", "expert"), None),
            P("dp", None, "expert"),
            P("dp", None, "expert"),
            P("dp", "expert", None),
            P("dp", None, "expert"),
            P("dp", None, "expert"),
            P("dp", "expert", None),
        ),
        out_specs=P(("dp", "expert"), None),
        check_vma=False,
    )
```

```python
import functools

import jax
import jax.numpy as jnp
from jax import lax
from jax.experimental import pallas as pl
from jax.experimental.pallas import tpu as pltpu
from jax.sharding import PartitionSpec as P

BLOCK = 128


def from_partner(block, axis, bit):
    count = lax.axis_size(axis)
    route = []
    for low in range(count):
        high = low | 1 << bit
        if high != low and high < count:
            route += [(low, high), (high, low)]
    return lax.ppermute(block, axis, route)


def dequantize(quant_vals, block_scale):
    row_count, col_count = quant_vals.shape
    blocked = quant_vals.reshape(row_count // BLOCK, BLOCK, col_count // BLOCK, BLOCK).astype(
        jnp.float32
    )
    scaled = blocked * block_scale[:, None, :, None]
    return scaled.reshape(row_count, col_count).astype(jnp.bfloat16)


def expert_ffn(inputs, w_gate, w_up, w_down):
    gate_part = jnp.dot(inputs, w_gate, preferred_element_type=jnp.float32)
    up_part = jnp.dot(inputs, w_up, preferred_element_type=jnp.float32)
    hidden = (jax.nn.silu(gate_part) * up_part).astype(jnp.bfloat16)
    return jnp.dot(hidden, w_down, preferred_element_type=jnp.float32)


def across_groups(blocks):
    return lax.all_to_all(blocks, "dp", split_axis=1, concat_axis=1, tiled=True)


def across_owners(blocks):
    return lax.all_to_all(blocks, "expert", split_axis=0, concat_axis=0, tiled=True)


def by_rows(tokens, expert_ids, gate_vals, gate_q, up_q, down_q, gate_scale, up_scale, down_scale):
    group_count = lax.axis_size("dp")
    owner_count = lax.axis_size("expert")
    token_count, model_width = tokens.shape
    top_count = expert_ids.shape[1]
    pair_count = owner_count // 2
    expert_count = group_count * pair_count
    capacity = 2 * token_count * top_count // expert_count
    half_cap = capacity // 2
    slot_count = owner_count * group_count * half_cap
    routes = expert_ids.reshape(-1)
    onehot = (routes[:, None] == jnp.arange(expert_count, dtype=jnp.int32)[None, :]).astype(
        jnp.int32
    )
    earlier = jnp.cumsum(onehot, axis=0) - onehot
    route_slot = jnp.sum(earlier * onehot, axis=1)
    route_group = routes // pair_count
    route_pair = routes % pair_count
    route_owner = 2 * route_pair + route_slot // half_cap
    route_place = route_slot % half_cap
    route_index = (route_owner * group_count + route_group) * half_cap + route_place
    chosen = jnp.arange(slot_count, dtype=jnp.int32)[:, None] == route_index[None, :]
    chosen = jnp.any(chosen.reshape(slot_count, token_count, top_count), axis=2).astype(
        jnp.bfloat16
    )
    outgoing = jnp.dot(chosen, tokens, preferred_element_type=jnp.float32).astype(jnp.bfloat16)
    outgoing = outgoing.reshape(owner_count, group_count, half_cap, model_width)
    arrived = across_owners(across_groups(outgoing))
    own_rows = arrived.reshape(-1, model_width)
    row_count = own_rows.shape[0]
    w_gate = dequantize(gate_q[0], gate_scale[0])
    w_up = dequantize(up_q[0], up_scale[0])
    w_down = dequantize(down_q[0], down_scale[0])
    partner_rows = from_partner(own_rows, "expert", 0)
    both_rows = jnp.concatenate([own_rows, partner_rows], axis=0)
    partial_value = expert_ffn(both_rows, w_gate, w_up, w_down)
    returned = from_partner(partial_value[row_count:], "expert", 0)
    expert_out = (partial_value[:row_count] + returned).astype(jnp.bfloat16)
    expert_out = expert_out.reshape(owner_count, group_count, half_cap, model_width)
    returned_rows = across_groups(across_owners(expert_out))
    returned_rows = returned_rows.reshape(slot_count, model_width)
    picked = returned_rows[route_index].reshape(token_count, top_count, model_width)
    weighted = jnp.einsum("tkd,tk->td", picked.astype(jnp.float32), gate_vals)
    mixed = tokens.astype(jnp.float32) + weighted
    return mixed.astype(jnp.bfloat16)


def gather_groups(block, order):
    for bit in order:
        block = jnp.concatenate([block, from_partner(block, "dp", bit)], axis=0)
    return block


def sum_groups(block, order):
    for bit in reversed(order):
        kept, sent = jnp.split(block, 2, axis=0)
        arrived = from_partner(sent, "dp", bit)
        block = (kept.astype(jnp.float32) + arrived.astype(jnp.float32)).astype(jnp.bfloat16)
    return block


def scaled(block, scale):
    return (block.astype(jnp.float32) * scale).astype(jnp.bfloat16)


def in_kernel(block_cols, gate_scales, up_scales, gate_ref, up_ref, out_ref):
    strip = gate_ref.shape[0] // BLOCK
    first = pl.program_id(0) * strip
    for row in range(strip):
        rows = slice(row * BLOCK, (row + 1) * BLOCK)
        for col in range(block_cols):
            cols = slice(col * BLOCK, (col + 1) * BLOCK)
            place = (first + row) * block_cols + col
            out_ref[rows, cols] = scaled(gate_ref[rows, cols], gate_scales[place])
            cols_up = slice((block_cols + col) * BLOCK, (block_cols + col + 1) * BLOCK)
            out_ref[rows, cols_up] = scaled(up_ref[rows, cols], up_scales[place])


def dequantize_in(gate, up, gate_scales, up_scales):
    rows, cols = gate.shape
    strip = min(rows, 8 * BLOCK)
    block = pl.BlockSpec((strip, cols), lambda i: (i, 0))
    smem = pl.BlockSpec(memory_space=pltpu.SMEM)
    return pl.pallas_call(
        functools.partial(in_kernel, cols // BLOCK),
        grid=(rows // strip,),
        in_specs=[smem, smem, block, block],
        out_specs=pl.BlockSpec((strip, 2 * cols), lambda i: (i, 0)),
        out_shape=jax.ShapeDtypeStruct((rows, 2 * cols), jnp.bfloat16),
        cost_estimate=pl.CostEstimate(
            flops=2 * rows * cols, bytes_accessed=8 * rows * cols, transcendentals=0
        ),
        name="dequantize_in",
    )(gate_scales, up_scales, gate, up)


def down_kernel(block_cols, scales, down_ref, out_ref):
    strip = down_ref.shape[1] // BLOCK
    first = pl.program_id(0) * strip
    for row in range(down_ref.shape[0] // BLOCK):
        rows = slice(row * BLOCK, (row + 1) * BLOCK)
        for col in range(strip):
            cols = slice(col * BLOCK, (col + 1) * BLOCK)
            scale = scales[row * block_cols + first + col]
            out_ref[rows, cols] = scaled(down_ref[rows, cols], scale)


def dequantize_down(down, scales):
    rows, cols = down.shape
    strip = min(cols, 8 * BLOCK)
    block = pl.BlockSpec((rows, strip), lambda i: (0, i))
    return pl.pallas_call(
        functools.partial(down_kernel, cols // BLOCK),
        grid=(cols // strip,),
        in_specs=[pl.BlockSpec(memory_space=pltpu.SMEM), block],
        out_specs=block,
        out_shape=jax.ShapeDtypeStruct((rows, cols), jnp.bfloat16),
        cost_estimate=pl.CostEstimate(
            flops=rows * cols, bytes_accessed=4 * rows * cols, transcendentals=0
        ),
        name="dequantize_down",
    )(scales, down)


def across_chips(block, far):
    count = lax.axis_size("expert")
    return lax.ppermute(block, "expert", [(low, low ^ 2 * far) for low in range(count)])


def by_sums(tokens, expert_ids, gate_vals, gate_q, up_q, down_q, gate_scale, up_scale, down_scale):
    token_count, model_width = tokens.shape
    group_count = lax.axis_size("dp")
    pair_count = lax.axis_size("expert") // 2
    expert_count = group_count * pair_count
    own_expert = lax.axis_index("dp") * pair_count + lax.axis_index("expert") // 2
    bits = list(range(group_count.bit_length() - 1))
    orders = (bits, bits[::-1])

    named = expert_ids[:, :, None] == jnp.arange(expert_count, dtype=jnp.int32)[None, None, :]
    weight = jnp.sum(jnp.where(named, gate_vals[:, :, None], 0.0), axis=1)
    high = weight.astype(jnp.bfloat16)
    low = (weight - high.astype(jnp.float32)).astype(jnp.bfloat16)
    extra = -(-2 * expert_count // BLOCK) * BLOCK
    pad = jnp.zeros((token_count, extra - 2 * expert_count), jnp.bfloat16)
    payload = jnp.concatenate([tokens, high, low, pad], axis=1)

    route = [0, *range(2, pair_count), 1][:pair_count]
    order_of = {far: orders[place % 2] for place, far in enumerate(route)}
    step = 2
    blocks = {0: payload[None]}
    for far in route[1:step]:
        blocks[far] = across_chips(payload, far)[None]
    blocks[0] = gather_groups(blocks[0], order_of[0][:1])

    gate_own, up_own, payload = lax.optimization_barrier((gate_q[0], up_q[0], payload))
    hidden_half = gate_q.shape[2]
    in_own = dequantize_in(gate_own, up_own, gate_scale.reshape(-1), up_scale.reshape(-1))
    blocks, payload, in_own, down_half = lax.optimization_barrier(
        (blocks, payload, in_own, down_q[0])
    )
    in_other = from_partner(in_own, "expert", 0)
    for far in route[step:]:
        blocks[far] = across_chips(payload, far)[None]
    down_own = dequantize_down(down_half, down_scale.reshape(-1))
    down_other = from_partner(down_own, "expert", 0)
    down_both = jnp.concatenate([down_own, down_other], axis=0)

    def ffn(rows):
        inputs = rows[:, :model_width]
        marks = rows[:, model_width:].astype(jnp.float32)
        column = jnp.arange(extra, dtype=jnp.int32)[None, :]
        chosen = (column == own_expert) | (column == own_expert + expert_count)
        row_weight = jnp.sum(jnp.where(chosen, marks, 0.0), axis=1)
        hidden = []
        for w_in in (in_own, in_other):
            parts = jnp.dot(inputs, w_in, preferred_element_type=jnp.float32)
            hidden.append(
                (jax.nn.silu(parts[:, :hidden_half]) * parts[:, hidden_half:]).astype(jnp.bfloat16)
            )
        hidden = jnp.concatenate(hidden, axis=1)
        value = jnp.dot(hidden, down_both, preferred_element_type=jnp.float32)
        return (value * row_weight[:, None]).astype(jnp.bfloat16)

    outs = {}
    for first in range(0, pair_count, step):
        fars = route[first : first + step]
        for far in fars:
            blocks[far] = gather_groups(blocks[far], order_of[far][int(far == 0) : -1])
        if outs:
            tied = [blocks[far] for far in fars]
            outs[0], tied = lax.optimization_barrier((outs[0], tied))
            for far, block in zip(fars, tied):
                blocks[far] = block
        for far in fars:
            blocks[far] = gather_groups(blocks[far], order_of[far][-1:])
        for far in fars:
            outs[far] = ffn(blocks[far].reshape(-1, blocks[far].shape[-1]))
    outs[0], outs[1] = lax.optimization_barrier((outs[0], outs[1]))
    total = tokens.astype(jnp.float32)
    for far in route[1:] + route[:1]:
        out = outs[far].reshape(group_count, token_count, model_width)
        block = sum_groups(out, order_of[far])[0]
        if far > 0:
            block = across_chips(block, far)
        total = total + block.astype(jnp.float32)
    return total.astype(jnp.bfloat16)


def shards(tokens, expert_ids, *weights):
    expert_count = lax.axis_size("dp") * lax.axis_size("expert") // 2
    token_count, top_count = expert_ids.shape
    capacity = 2 * token_count * top_count // expert_count
    plan = by_rows if capacity < token_count else by_sums
    return plan(tokens, expert_ids, *weights)


def solution(mesh):
    return jax.shard_map(
        shards,
        mesh=mesh,
        in_specs=(
            P(("dp", "expert"), None),
            P(("dp", "expert"), None),
            P(("dp", "expert"), None),
            P("dp", None, "expert"),
            P("dp", None, "expert"),
            P("dp", "expert", None),
            P("dp", None, "expert"),
            P("dp", None, "expert"),
            P("dp", "expert", None),
        ),
        out_specs=P(("dp", "expert"), None),
        check_vma=False,
    )
```

```python
import functools

import jax
import jax.numpy as jnp
from jax import lax
from jax.experimental import pallas as pl
from jax.experimental.pallas import tpu as pltpu
from jax.sharding import PartitionSpec as P

BLOCK = 128


def from_partner(block, axis, bit):
    count = lax.axis_size(axis)
    route = []
    for low in range(count):
        high = low | 1 << bit
        if high != low and high < count:
            route += [(low, high), (high, low)]
    return lax.ppermute(block, axis, route)


def dequantize(quant_vals, block_scale):
    row_count, col_count = quant_vals.shape
    blocked = quant_vals.reshape(row_count // BLOCK, BLOCK, col_count // BLOCK, BLOCK).astype(
        jnp.float32
    )
    scaled = blocked * block_scale[:, None, :, None]
    return scaled.reshape(row_count, col_count).astype(jnp.bfloat16)


def expert_ffn(inputs, w_gate, w_up, w_down):
    gate_part = jnp.dot(inputs, w_gate, preferred_element_type=jnp.float32)
    up_part = jnp.dot(inputs, w_up, preferred_element_type=jnp.float32)
    hidden = (jax.nn.silu(gate_part) * up_part).astype(jnp.bfloat16)
    return jnp.dot(hidden, w_down, preferred_element_type=jnp.float32)


def across_groups(blocks):
    return lax.all_to_all(blocks, "dp", split_axis=1, concat_axis=1, tiled=True)


def across_owners(blocks):
    return lax.all_to_all(blocks, "expert", split_axis=0, concat_axis=0, tiled=True)


def by_rows(tokens, expert_ids, gate_vals, gate_q, up_q, down_q, gate_scale, up_scale, down_scale):
    group_count = lax.axis_size("dp")
    owner_count = lax.axis_size("expert")
    token_count, model_width = tokens.shape
    top_count = expert_ids.shape[1]
    pair_count = owner_count // 2
    expert_count = group_count * pair_count
    capacity = 2 * token_count * top_count // expert_count
    half_cap = capacity // 2
    slot_count = owner_count * group_count * half_cap
    routes = expert_ids.reshape(-1)
    onehot = (routes[:, None] == jnp.arange(expert_count, dtype=jnp.int32)[None, :]).astype(
        jnp.int32
    )
    earlier = jnp.cumsum(onehot, axis=0) - onehot
    route_slot = jnp.sum(earlier * onehot, axis=1)
    route_group = routes // pair_count
    route_pair = routes % pair_count
    route_owner = 2 * route_pair + route_slot // half_cap
    route_place = route_slot % half_cap
    route_index = (route_owner * group_count + route_group) * half_cap + route_place
    chosen = jnp.arange(slot_count, dtype=jnp.int32)[:, None] == route_index[None, :]
    chosen = jnp.any(chosen.reshape(slot_count, token_count, top_count), axis=2).astype(
        jnp.bfloat16
    )
    outgoing = jnp.dot(chosen, tokens, preferred_element_type=jnp.float32).astype(jnp.bfloat16)
    outgoing = outgoing.reshape(owner_count, group_count, half_cap, model_width)
    arrived = across_owners(across_groups(outgoing))
    own_rows = arrived.reshape(-1, model_width)
    row_count = own_rows.shape[0]
    w_gate = dequantize(gate_q[0], gate_scale[0])
    w_up = dequantize(up_q[0], up_scale[0])
    w_down = dequantize(down_q[0], down_scale[0])
    partner_rows = from_partner(own_rows, "expert", 0)
    both_rows = jnp.concatenate([own_rows, partner_rows], axis=0)
    partial_value = expert_ffn(both_rows, w_gate, w_up, w_down)
    returned = from_partner(partial_value[row_count:], "expert", 0)
    expert_out = (partial_value[:row_count] + returned).astype(jnp.bfloat16)
    expert_out = expert_out.reshape(owner_count, group_count, half_cap, model_width)
    returned_rows = across_groups(across_owners(expert_out))
    returned_rows = returned_rows.reshape(slot_count, model_width)
    picked = returned_rows[route_index].reshape(token_count, top_count, model_width)
    weighted = jnp.einsum("tkd,tk->td", picked.astype(jnp.float32), gate_vals)
    mixed = tokens.astype(jnp.float32) + weighted
    return mixed.astype(jnp.bfloat16)


def gather_step(block, bit):
    return jnp.concatenate([block, from_partner(block, "dp", bit)], axis=0)


def sum_step(block, bit):
    kept, sent = jnp.split(block, 2, axis=0)
    arrived = from_partner(sent, "dp", bit)
    return (kept.astype(jnp.float32) + arrived.astype(jnp.float32)).astype(jnp.bfloat16)


def scaled(block, scale):
    return (block.astype(jnp.float32) * scale).astype(jnp.bfloat16)


def in_kernel(block_cols, gate_scales, up_scales, gate_ref, up_ref, out_ref):
    strip = gate_ref.shape[0] // BLOCK
    first = pl.program_id(0) * strip
    for row in range(strip):
        rows = slice(row * BLOCK, (row + 1) * BLOCK)
        for col in range(block_cols):
            cols = slice(col * BLOCK, (col + 1) * BLOCK)
            place = (first + row) * block_cols + col
            out_ref[rows, cols] = scaled(gate_ref[rows, cols], gate_scales[place])
            cols_up = slice((block_cols + col) * BLOCK, (block_cols + col + 1) * BLOCK)
            out_ref[rows, cols_up] = scaled(up_ref[rows, cols], up_scales[place])


def dequantize_in(gate, up, gate_scales, up_scales):
    rows, cols = gate.shape
    strip = min(rows, 8 * BLOCK)
    block = pl.BlockSpec((strip, cols), lambda i: (i, 0))
    smem = pl.BlockSpec(memory_space=pltpu.SMEM)
    return pl.pallas_call(
        functools.partial(in_kernel, cols // BLOCK),
        grid=(rows // strip,),
        in_specs=[smem, smem, block, block],
        out_specs=pl.BlockSpec((strip, 2 * cols), lambda i: (i, 0)),
        out_shape=jax.ShapeDtypeStruct((rows, 2 * cols), jnp.bfloat16),
        cost_estimate=pl.CostEstimate(
            flops=2 * rows * cols, bytes_accessed=8 * rows * cols, transcendentals=0
        ),
        name="dequantize_in",
    )(gate_scales, up_scales, gate, up)


def down_kernel(block_cols, scales, down_ref, out_ref):
    strip = down_ref.shape[1] // BLOCK
    first = pl.program_id(0) * strip
    for row in range(down_ref.shape[0] // BLOCK):
        rows = slice(row * BLOCK, (row + 1) * BLOCK)
        for col in range(strip):
            cols = slice(col * BLOCK, (col + 1) * BLOCK)
            scale = scales[row * block_cols + first + col]
            out_ref[rows, cols] = scaled(down_ref[rows, cols], scale)


def dequantize_down(down, scales):
    rows, cols = down.shape
    strip = min(cols, 8 * BLOCK)
    block = pl.BlockSpec((rows, strip), lambda i: (0, i))
    return pl.pallas_call(
        functools.partial(down_kernel, cols // BLOCK),
        grid=(cols // strip,),
        in_specs=[pl.BlockSpec(memory_space=pltpu.SMEM), block],
        out_specs=block,
        out_shape=jax.ShapeDtypeStruct((rows, cols), jnp.bfloat16),
        cost_estimate=pl.CostEstimate(
            flops=rows * cols, bytes_accessed=4 * rows * cols, transcendentals=0
        ),
        name="dequantize_down",
    )(scales, down)


def silu(v):
    return v / (1 + jnp.exp(-v))


def ffn_kernel(count, experts, in_steps, *refs):
    own_expert, refs = refs[0], refs[1:]
    rows_refs, refs = refs[:count], refs[count:]
    in_own, in_other, down_own, down_other = refs[:4]
    out_refs, (parts, hidden, weight) = refs[4 : 4 + count], refs[4 + count :]
    step = pl.program_id(0)
    depth, width = in_own.shape
    half = width // 2
    model_width = in_steps * depth

    def strip(first, size):
        cols = pl.ds(first, size)
        return jnp.concatenate([ref[:, cols] for ref in rows_refs], axis=0)

    @pl.when(step < in_steps)
    def _():
        rows = strip(pl.multiple_of(step * depth, depth), depth)
        for place, w_in in enumerate((in_own, in_other)):
            part = jnp.dot(rows, w_in[...], preferred_element_type=jnp.float32)
            before = jnp.where(step == 0, 0.0, parts[place])
            parts[place] = before + part

    @pl.when(step == in_steps)
    def _():
        for place in range(2):
            gate_part, up_part = parts[place][:, :half], parts[place][:, half:]
            value = (silu(gate_part) * up_part).astype(jnp.bfloat16)
            hidden[:, place * half : (place + 1) * half] = value
        marks = strip(model_width, rows_refs[0].shape[1] - model_width).astype(jnp.float32)
        column = lax.broadcasted_iota(jnp.int32, marks.shape, 1)
        chosen = (column == own_expert[0]) | (column == own_expert[0] + experts)
        weight[...] = jnp.sum(jnp.where(chosen, marks, 0.0), axis=1, keepdims=True)

    @pl.when(step >= in_steps)
    def _():
        value = jnp.dot(hidden[:, :half], down_own[...], preferred_element_type=jnp.float32)
        value += jnp.dot(hidden[:, half:], down_other[...], preferred_element_type=jnp.float32)
        value = (value * weight[...]).astype(jnp.bfloat16)
        size = out_refs[0].shape[0]
        for place, out_ref in enumerate(out_refs):
            out_ref[...] = value[place * size : (place + 1) * size]


def expert_layer(rows, own_expert, experts, in_own, in_other, down_own, down_other):
    count, (size, payload_width) = len(rows), rows[0].shape
    model_width, width = in_own.shape
    half = width // 2
    depth, strip = min(4 * BLOCK, model_width), min(8 * BLOCK, model_width)
    in_steps, out_steps = model_width // depth, model_width // strip
    whole = pl.BlockSpec((size, payload_width), lambda i: (0, 0))
    w_in = pl.BlockSpec((depth, width), lambda i: (jnp.minimum(i, in_steps - 1), 0))
    at_strip = lambda i: (0, jnp.maximum(i - in_steps, 0))
    w_down = pl.BlockSpec((half, strip), at_strip)
    total = count * size
    return pl.pallas_call(
        functools.partial(ffn_kernel, count, experts, in_steps),
        grid=(in_steps + out_steps,),
        in_specs=[pl.BlockSpec(memory_space=pltpu.SMEM)]
        + [whole] * count
        + [w_in, w_in, w_down, w_down],
        out_specs=[pl.BlockSpec((size, strip), at_strip)] * count,
        out_shape=[jax.ShapeDtypeStruct((size, model_width), jnp.bfloat16)] * count,
        scratch_shapes=[
            pltpu.VMEM((2, total, width), jnp.float32),
            pltpu.VMEM((total, width), jnp.bfloat16),
            pltpu.VMEM((total, 1), jnp.float32),
        ],
        cost_estimate=pl.CostEstimate(
            flops=6 * total * model_width * width,
            bytes_accessed=6 * model_width * width + 4 * total * model_width,
            transcendentals=total * width,
        ),
        compiler_params=pltpu.CompilerParams(vmem_limit_bytes=40 * 1024 * 1024),
        name="expert_layer",
    )(own_expert, *rows, in_own, in_other, down_own, down_other)


def across_chips(block, far):
    count = lax.axis_size("expert")
    return lax.ppermute(block, "expert", [(low, low ^ 2 * far) for low in range(count)])


def by_sums(tokens, expert_ids, gate_vals, gate_q, up_q, down_q, gate_scale, up_scale, down_scale):
    token_count, model_width = tokens.shape
    group_count = lax.axis_size("dp")
    pair_count = lax.axis_size("expert") // 2
    expert_count = group_count * pair_count
    own_expert = lax.axis_index("dp") * pair_count + lax.axis_index("expert") // 2
    bits = list(range(group_count.bit_length() - 1))
    orders = (bits, bits[::-1])

    named = expert_ids[:, :, None] == jnp.arange(expert_count, dtype=jnp.int32)[None, None, :]
    weight = jnp.sum(jnp.where(named, gate_vals[:, :, None], 0.0), axis=1)
    high = weight.astype(jnp.bfloat16)
    low = (weight - high.astype(jnp.float32)).astype(jnp.bfloat16)
    extra = -(-2 * expert_count // BLOCK) * BLOCK
    pad = jnp.zeros((token_count, extra - 2 * expert_count), jnp.bfloat16)
    payload = jnp.concatenate([tokens, high, low, pad], axis=1)

    together = lax.optimization_barrier
    step = 2
    pairs = [range(first, min(first + step, pair_count)) for first in range(0, pair_count, step)]
    near = {0: payload[None]}
    for far in pairs[0][1:]:
        near[far] = across_chips(payload, far)[None]

    gate_own, up_own, payload = together((gate_q[0], up_q[0], payload))
    hidden_half = gate_q.shape[2]
    in_own = dequantize_in(gate_own, up_own, gate_scale.reshape(-1), up_scale.reshape(-1))
    near, payload, in_own, down_half = together((near, payload, in_own, down_q[0]))
    in_other = from_partner(in_own, "expert", 0)
    down_own = dequantize_down(down_half, down_scale.reshape(-1))

    place = jnp.reshape(own_expert, (1,)).astype(jnp.int32)
    outs, weights = {}, None
    for number, pair in enumerate(pairs):
        following = list(pairs[number + 1]) if number + 1 < len(pairs) else []
        later, rows_before = {}, None
        for turn in range(len(bits)):
            if turn == 0:
                for far in following:
                    low = far & -far
                    block = payload if far == low else later[far ^ low][0]
                    later[far] = across_chips(block, low)[None]
            near = {far: gather_step(near[far], orders[far % 2][turn]) for far in pair}
            if number == 0 and turn == 0:
                near, down_own = together((near, down_own))
            elif number == 0 and turn == len(bits) - 1:
                near, later, in_other, down_own = together((near, later, in_other, down_own))
            elif number == 1 and turn == 0:
                down_other = from_partner(down_own, "expert", 0)
                near, waiting, down_other = together((near, waiting, down_other))
                weights = (in_own, in_other, down_own, down_other)
        if number == 0:
            waiting = near
        else:
            for held in ([waiting, near] if number == 1 else [near]):
                if number == 1 and held is near:
                    near, outs = together((near, outs))
                rows = [held[far].reshape(-1, held[far].shape[-1]) for far in held]
                for far, out in zip(held, expert_layer(rows, place, expert_count, *weights)):
                    outs[far] = out
        near = later

    total = tokens.astype(jnp.float32)
    sums = {far: out.reshape(group_count, token_count, model_width) for far, out in outs.items()}
    for pair in pairs[::-1]:
        for turn in reversed(range(len(bits))):
            for far in pair:
                sums[far] = sum_step(sums[far], orders[far % 2][turn])
            sums = together(sums)
        for far in reversed(pair):
            block, low = sums.pop(far), far & -far
            if far == 0:
                total = total + block[0].astype(jnp.float32)
            elif far == low:
                total = total + across_chips(block[0], low).astype(jnp.float32)
            else:
                arrived = across_chips(block, low)
                block = sums[far ^ low]
                sums[far ^ low] = (block.astype(jnp.float32) + arrived.astype(jnp.float32)).astype(jnp.bfloat16)
    return total.astype(jnp.bfloat16)


def shards(tokens, expert_ids, *weights):
    expert_count = lax.axis_size("dp") * lax.axis_size("expert") // 2
    token_count, top_count = expert_ids.shape
    capacity = 2 * token_count * top_count // expert_count
    group_count, pair_count = lax.axis_size("dp"), lax.axis_size("expert") // 2
    powers = all(count & (count - 1) == 0 for count in (group_count, pair_count))
    dense = capacity >= token_count and powers and min(group_count, pair_count) >= 4
    plan = by_sums if dense else by_rows
    return plan(tokens, expert_ids, *weights)


def solution(mesh):
    return jax.shard_map(
        shards,
        mesh=mesh,
        in_specs=(
            P(("dp", "expert"), None),
            P(("dp", "expert"), None),
            P(("dp", "expert"), None),
            P("dp", None, "expert"),
            P("dp", None, "expert"),
            P("dp", "expert", None),
            P("dp", None, "expert"),
            P("dp", None, "expert"),
            P("dp", "expert", None),
        ),
        out_specs=P(("dp", "expert"), None),
        check_vma=False,
    )
```

```python
import functools

import jax
import jax.numpy as jnp
from jax import lax
from jax.experimental import pallas as pl
from jax.experimental.pallas import tpu as pltpu
from jax.sharding import PartitionSpec as P

BLOCK = 128


def from_partner(block, axis, bit):
    count = lax.axis_size(axis)
    route = []
    for low in range(count):
        high = low | 1 << bit
        if high != low and high < count:
            route += [(low, high), (high, low)]
    return lax.ppermute(block, axis, route)


def dequantize(quant_vals, block_scale):
    row_count, col_count = quant_vals.shape
    blocked = quant_vals.reshape(row_count // BLOCK, BLOCK, col_count // BLOCK, BLOCK).astype(
        jnp.float32
    )
    scaled = blocked * block_scale[:, None, :, None]
    return scaled.reshape(row_count, col_count).astype(jnp.bfloat16)


def expert_ffn(inputs, w_gate, w_up, w_down):
    gate_part = jnp.dot(inputs, w_gate, preferred_element_type=jnp.float32)
    up_part = jnp.dot(inputs, w_up, preferred_element_type=jnp.float32)
    hidden = (jax.nn.silu(gate_part) * up_part).astype(jnp.bfloat16)
    return jnp.dot(hidden, w_down, preferred_element_type=jnp.float32)


def across_groups(blocks):
    return lax.all_to_all(blocks, "dp", split_axis=1, concat_axis=1, tiled=True)


def across_owners(blocks):
    return lax.all_to_all(blocks, "expert", split_axis=0, concat_axis=0, tiled=True)


def by_rows(tokens, expert_ids, gate_vals, gate_q, up_q, down_q, gate_scale, up_scale, down_scale):
    group_count = lax.axis_size("dp")
    owner_count = lax.axis_size("expert")
    token_count, model_width = tokens.shape
    top_count = expert_ids.shape[1]
    pair_count = owner_count // 2
    expert_count = group_count * pair_count
    capacity = 2 * token_count * top_count // expert_count
    half_cap = capacity // 2
    slot_count = owner_count * group_count * half_cap
    routes = expert_ids.reshape(-1)
    onehot = (routes[:, None] == jnp.arange(expert_count, dtype=jnp.int32)[None, :]).astype(
        jnp.int32
    )
    earlier = jnp.cumsum(onehot, axis=0) - onehot
    route_slot = jnp.sum(earlier * onehot, axis=1)
    route_group = routes // pair_count
    route_pair = routes % pair_count
    route_owner = 2 * route_pair + route_slot // half_cap
    route_place = route_slot % half_cap
    route_index = (route_owner * group_count + route_group) * half_cap + route_place
    chosen = jnp.arange(slot_count, dtype=jnp.int32)[:, None] == route_index[None, :]
    chosen = jnp.any(chosen.reshape(slot_count, token_count, top_count), axis=2).astype(
        jnp.bfloat16
    )
    outgoing = jnp.dot(chosen, tokens, preferred_element_type=jnp.float32).astype(jnp.bfloat16)
    outgoing = outgoing.reshape(owner_count, group_count, half_cap, model_width)
    arrived = across_owners(across_groups(outgoing))
    own_rows = arrived.reshape(-1, model_width)
    row_count = own_rows.shape[0]
    w_gate = dequantize(gate_q[0], gate_scale[0])
    w_up = dequantize(up_q[0], up_scale[0])
    w_down = dequantize(down_q[0], down_scale[0])
    partner_rows = from_partner(own_rows, "expert", 0)
    both_rows = jnp.concatenate([own_rows, partner_rows], axis=0)
    partial_value = expert_ffn(both_rows, w_gate, w_up, w_down)
    returned = from_partner(partial_value[row_count:], "expert", 0)
    expert_out = (partial_value[:row_count] + returned).astype(jnp.bfloat16)
    expert_out = expert_out.reshape(owner_count, group_count, half_cap, model_width)
    returned_rows = across_groups(across_owners(expert_out))
    returned_rows = returned_rows.reshape(slot_count, model_width)
    picked = returned_rows[route_index].reshape(token_count, top_count, model_width)
    weighted = jnp.einsum("tkd,tk->td", picked.astype(jnp.float32), gate_vals)
    mixed = tokens.astype(jnp.float32) + weighted
    return mixed.astype(jnp.bfloat16)


def added(block, arrived):
    return (block.astype(jnp.float32) + arrived.astype(jnp.float32)).astype(jnp.bfloat16)


def scaled(block, scale):
    return (block.astype(jnp.float32) * scale).astype(jnp.bfloat16)


def in_kernel(gate_scales, up_scales, gate_ref, up_ref, out_ref):
    strip, cols = gate_ref.shape
    first = pl.program_id(0) * (strip // BLOCK)
    for row in range(strip // BLOCK):
        rows = slice(row * BLOCK, (row + 1) * BLOCK)
        for col in range(cols // BLOCK):
            at = slice(col * BLOCK, (col + 1) * BLOCK)
            to = 2 * col * BLOCK
            out_ref[rows, to : to + BLOCK] = scaled(gate_ref[rows, at], gate_scales[col, first + row])
            to += BLOCK
            out_ref[rows, to : to + BLOCK] = scaled(up_ref[rows, at], up_scales[col, first + row])


def dequantize_in(gate, up, gate_scales, up_scales):
    rows, cols = gate.shape
    strip = min(rows, 8 * BLOCK)
    block = pl.BlockSpec((strip, cols), lambda i: (i, 0))
    smem = pl.BlockSpec(memory_space=pltpu.SMEM)
    return pl.pallas_call(
        in_kernel,
        grid=(rows // strip,),
        in_specs=[smem, smem, block, block],
        out_specs=pl.BlockSpec((strip, 2 * cols), lambda i: (i, 0)),
        out_shape=jax.ShapeDtypeStruct((rows, 2 * cols), jnp.bfloat16),
        cost_estimate=pl.CostEstimate(
            flops=2 * rows * cols, bytes_accessed=8 * rows * cols, transcendentals=0
        ),
        name="dequantize_in",
    )(gate_scales.T, up_scales.T, gate, up)


def down_kernel(scales, down_ref, out_ref):
    strip = down_ref.shape[1] // BLOCK
    first = pl.program_id(0) * strip
    for row in range(down_ref.shape[0] // BLOCK):
        rows = slice(row * BLOCK, (row + 1) * BLOCK)
        for col in range(strip):
            cols = slice(col * BLOCK, (col + 1) * BLOCK)
            out_ref[rows, cols] = scaled(down_ref[rows, cols], scales[row, first + col])


def dequantize_down(down, scales):
    rows, cols = down.shape
    strip = min(cols, 8 * BLOCK)
    block = pl.BlockSpec((rows, strip), lambda i: (0, i))
    return pl.pallas_call(
        down_kernel,
        grid=(cols // strip,),
        in_specs=[pl.BlockSpec(memory_space=pltpu.SMEM), block],
        out_specs=block,
        out_shape=jax.ShapeDtypeStruct((rows, cols), jnp.bfloat16),
        cost_estimate=pl.CostEstimate(
            flops=rows * cols, bytes_accessed=4 * rows * cols, transcendentals=0
        ),
        name="dequantize_down",
    )(scales, down)


def silu(v):
    return v / (1 + jnp.exp(-v))


def expert_kernel(count, experts, own_expert, *refs):
    pieces, refs = refs[:count], refs[count:]
    in_refs, down_refs, refs = refs[:2], refs[2:4], refs[4:]
    outs, (rows, w_in, w_down, hidden, in_sems, down_sems) = refs[:count], refs[count:]
    size = pieces[0].shape[0]
    model_width = rows.shape[1]
    strips, full, strip = w_down.shape
    half = full // 2
    columns = range(half // BLOCK)

    def in_copy(part, col):
        source = in_refs[part].at[:, pl.ds(2 * col * BLOCK, 2 * BLOCK)]
        return pltpu.make_async_copy(source, w_in.at[part, col], in_sems.at[part, col])

    def down_copy(part, at):
        source = down_refs[part].at[:, pl.ds(at * strip, strip)]
        target = w_down.at[at, pl.ds(part * half, half)]
        return pltpu.make_async_copy(source, target, down_sems.at[part, at])

    for part in range(2):
        for col in columns:
            in_copy(part, col).start()
    for at in range(strips):
        for part in range(2):
            down_copy(part, at).start()

    weights = []
    for place, piece in enumerate(pieces):
        rows[place * size : (place + 1) * size, :] = piece[:, :model_width]
        marks = piece[:, model_width:].astype(jnp.float32)
        column = lax.broadcasted_iota(jnp.int32, marks.shape, 1)
        chosen = (column == own_expert[0]) | (column == own_expert[0] + experts)
        weights.append(jnp.sum(jnp.where(chosen, marks, 0.0), axis=1, keepdims=True))
    for part in range(2):
        for col in columns:
            in_copy(part, col).wait()
            both = jnp.dot(rows[...], w_in[part, col], preferred_element_type=jnp.float32)
            value = (silu(both[:, :BLOCK]) * both[:, BLOCK:]).astype(jnp.bfloat16)
            to = part * half + col * BLOCK
            hidden[:, to : to + BLOCK] = value
    for at in range(strips):
        for part in range(2):
            down_copy(part, at).wait()
        value = jnp.dot(hidden[...], w_down[at], preferred_element_type=jnp.float32)
        for place, out in enumerate(outs):
            weighted = value[place * size : (place + 1) * size] * weights[place]
            out[:, at * strip : (at + 1) * strip] = weighted.astype(jnp.bfloat16)


def expert_layer(pieces, own_expert, experts, in_own, in_other, down_own, down_other):
    count, size = len(pieces), pieces[0].shape[0]
    model_width, width = in_own.shape
    half = width // 2
    strip = min(8 * BLOCK, model_width)
    strips, columns = model_width // strip, half // BLOCK
    total = count * size
    whole = pl.BlockSpec(memory_space=pltpu.VMEM)
    anywhere = pl.BlockSpec(memory_space=pl.ANY)
    return pl.pallas_call(
        functools.partial(expert_kernel, count, experts),
        in_specs=[pl.BlockSpec(memory_space=pltpu.SMEM)] + [whole] * count + [anywhere] * 4,
        out_specs=[whole] * count,
        out_shape=[jax.ShapeDtypeStruct((size, model_width), jnp.bfloat16)] * count,
        scratch_shapes=[
            pltpu.VMEM((total, model_width), jnp.bfloat16),
            pltpu.VMEM((2, columns, model_width, 2 * BLOCK), jnp.bfloat16),
            pltpu.VMEM((strips, width, strip), jnp.bfloat16),
            pltpu.VMEM((total, width), jnp.bfloat16),
            pltpu.SemaphoreType.DMA((2, columns)),
            pltpu.SemaphoreType.DMA((2, strips)),
        ],
        cost_estimate=pl.CostEstimate(
            flops=6 * total * model_width * width,
            bytes_accessed=6 * model_width * width + 4 * total * model_width,
            transcendentals=total * width,
        ),
        compiler_params=pltpu.CompilerParams(vmem_limit_bytes=32 * 1024 * 1024),
        name="expert_layer",
    )(own_expert, *pieces, in_own, in_other, down_own, down_other)


def across_chips(block, far):
    count = lax.axis_size("expert")
    return lax.ppermute(block, "expert", [(low, low ^ 2 * far) for low in range(count)])


def by_sums(tokens, expert_ids, gate_vals, gate_q, up_q, down_q, gate_scale, up_scale, down_scale):
    token_count, model_width = tokens.shape
    group_count = lax.axis_size("dp")
    pair_count = lax.axis_size("expert") // 2
    expert_count = group_count * pair_count
    own_expert = lax.axis_index("dp") * pair_count + lax.axis_index("expert") // 2
    bits = list(range(group_count.bit_length() - 1))
    orders = (bits, bits[::-1])

    named = expert_ids[:, :, None] == jnp.arange(expert_count, dtype=jnp.int32)[None, None, :]
    weight = jnp.sum(jnp.where(named, gate_vals[:, :, None], 0.0), axis=1)
    high = weight.astype(jnp.bfloat16)
    low = (weight - high.astype(jnp.float32)).astype(jnp.bfloat16)
    extra = -(-2 * expert_count // BLOCK) * BLOCK
    pad = jnp.zeros((token_count, extra - 2 * expert_count), jnp.bfloat16)
    payload = jnp.concatenate([tokens, high, low, pad], axis=1)

    together = lax.optimization_barrier
    place = jnp.reshape(own_expert, (1,)).astype(jnp.int32)
    last = len(bits) - 1
    pairs = [(first, first + 1) for first in range(0, pair_count, 2)]
    came = {0: payload, 1: across_chips(payload, 1)}

    def along_z(far):
        low = far & -far
        came[far] = across_chips(came[far ^ low], low)

    gate_own, up_own, came = together((gate_q[0], up_q[0], came))
    pieces, outs, in_other, down_other = {}, {}, None, None
    for number, pair in enumerate(pairs):
        following = pairs[number + 1] if number + 1 < len(pairs) else ()
        blocks = {far: came[far] for far in pair}
        for turn in range(len(bits)):
            if turn < len(following):
                along_z(following[turn])
            arrived = {far: from_partner(blocks[far], "dp", orders[far % 2][turn]) for far in pair}
            if turn == last:
                pieces[pair] = [part for far in pair for part in (blocks[far], arrived[far])]
            else:
                blocks = {
                    far: jnp.concatenate([blocks[far], arrived[far]], axis=0) for far in pair
                }
            if number == 0 and turn == 0:
                in_own = dequantize_in(gate_own, up_own, gate_scale[0], up_scale[0])
                blocks, came, in_own, down_own = together((blocks, came, in_own, down_q[0]))
                in_other = from_partner(in_own, "expert", 0)
                down_own = dequantize_down(down_own, down_scale[0])
            elif number == 0 and turn == last:
                tied = (pieces[pair], came, in_other, down_own)
                pieces[pair], came, in_other, down_own = together(tied)
                down_other = from_partner(down_own, "expert", 0)
                weights = (in_own, in_other, down_own)
            elif number == 1 and turn == 0:
                blocks, pieces, down_other = together((blocks, pieces, down_other))
                held = pieces[pairs[0]]
                outs[pairs[0]] = expert_layer(held, place, expert_count, *weights, down_other)
        if number > 0:
            pieces[pair], outs = together((pieces[pair], outs))
            outs[pair] = expert_layer(pieces[pair], place, expert_count, *weights, down_other)

    total = tokens.astype(jnp.float32)
    sums = {}
    for pair in pairs[::-1]:
        for turn in range(last, -1, -1):
            for where, far in enumerate(pair):
                if turn == last:
                    kept, sent = outs[pair][2 * where : 2 * where + 2]
                else:
                    kept, sent = jnp.split(sums[far], 2, axis=0)
                sums[far] = added(kept, from_partner(sent, "dp", orders[far % 2][turn]))
            sums, outs = together((sums, outs))
        for far in reversed(pair):
            block, low = sums.pop(far), far & -far
            if far == 0:
                total = total + block.astype(jnp.float32)
            elif far == low:
                total = total + across_chips(block, low).astype(jnp.float32)
            else:
                sums[far ^ low] = added(sums[far ^ low], across_chips(block, low))
    return total.astype(jnp.bfloat16)


def shards(tokens, expert_ids, *weights):
    expert_count = lax.axis_size("dp") * lax.axis_size("expert") // 2
    token_count, top_count = expert_ids.shape
    capacity = 2 * token_count * top_count // expert_count
    group_count, pair_count = lax.axis_size("dp"), lax.axis_size("expert") // 2
    powers = all(count & (count - 1) == 0 for count in (group_count, pair_count))
    dense = capacity >= token_count and powers and min(group_count, pair_count) >= 4
    plan = by_sums if dense else by_rows
    return plan(tokens, expert_ids, *weights)


def solution(mesh):
    return jax.shard_map(
        shards,
        mesh=mesh,
        in_specs=(
            P(("dp", "expert"), None),
            P(("dp", "expert"), None),
            P(("dp", "expert"), None),
            P("dp", None, "expert"),
            P("dp", None, "expert"),
            P("dp", "expert", None),
            P("dp", None, "expert"),
            P("dp", None, "expert"),
            P("dp", "expert", None),
        ),
        out_specs=P(("dp", "expert"), None),
        check_vma=False,
    )
```

```python
import functools

import jax
import jax.numpy as jnp
from jax import lax
from jax.experimental import pallas as pl
from jax.experimental.pallas import tpu as pltpu
from jax.sharding import PartitionSpec as P

BLOCK = 128


def from_partner(block, axis, bit):
    count = lax.axis_size(axis)
    route = []
    for low in range(count):
        high = low | 1 << bit
        if high != low and high < count:
            route += [(low, high), (high, low)]
    return lax.ppermute(block, axis, route)


def dequantize(quant_vals, block_scale):
    row_count, col_count = quant_vals.shape
    blocked = quant_vals.reshape(row_count // BLOCK, BLOCK, col_count // BLOCK, BLOCK).astype(
        jnp.float32
    )
    scaled = blocked * block_scale[:, None, :, None]
    return scaled.reshape(row_count, col_count).astype(jnp.bfloat16)


def expert_ffn(inputs, w_gate, w_up, w_down):
    gate_part = jnp.dot(inputs, w_gate, preferred_element_type=jnp.float32)
    up_part = jnp.dot(inputs, w_up, preferred_element_type=jnp.float32)
    hidden = (jax.nn.silu(gate_part) * up_part).astype(jnp.bfloat16)
    return jnp.dot(hidden, w_down, preferred_element_type=jnp.float32)


def across_groups(blocks):
    return lax.all_to_all(blocks, "dp", split_axis=1, concat_axis=1, tiled=True)


def across_owners(blocks):
    return lax.all_to_all(blocks, "expert", split_axis=0, concat_axis=0, tiled=True)


def by_rows(tokens, expert_ids, gate_vals, gate_q, up_q, down_q, gate_scale, up_scale, down_scale):
    group_count = lax.axis_size("dp")
    owner_count = lax.axis_size("expert")
    token_count, model_width = tokens.shape
    top_count = expert_ids.shape[1]
    pair_count = owner_count // 2
    expert_count = group_count * pair_count
    capacity = 2 * token_count * top_count // expert_count
    half_cap = capacity // 2
    slot_count = owner_count * group_count * half_cap
    routes = expert_ids.reshape(-1)
    onehot = (routes[:, None] == jnp.arange(expert_count, dtype=jnp.int32)[None, :]).astype(
        jnp.int32
    )
    earlier = jnp.cumsum(onehot, axis=0) - onehot
    route_slot = jnp.sum(earlier * onehot, axis=1)
    route_group = routes // pair_count
    route_pair = routes % pair_count
    route_owner = 2 * route_pair + route_slot // half_cap
    route_place = route_slot % half_cap
    route_index = (route_owner * group_count + route_group) * half_cap + route_place
    chosen = jnp.arange(slot_count, dtype=jnp.int32)[:, None] == route_index[None, :]
    chosen = jnp.any(chosen.reshape(slot_count, token_count, top_count), axis=2).astype(
        jnp.bfloat16
    )
    outgoing = jnp.dot(chosen, tokens, preferred_element_type=jnp.float32).astype(jnp.bfloat16)
    outgoing = outgoing.reshape(owner_count, group_count, half_cap, model_width)
    arrived = across_owners(across_groups(outgoing))
    own_rows = arrived.reshape(-1, model_width)
    row_count = own_rows.shape[0]
    w_gate = dequantize(gate_q[0], gate_scale[0])
    w_up = dequantize(up_q[0], up_scale[0])
    w_down = dequantize(down_q[0], down_scale[0])
    partner_rows = from_partner(own_rows, "expert", 0)
    both_rows = jnp.concatenate([own_rows, partner_rows], axis=0)
    partial_value = expert_ffn(both_rows, w_gate, w_up, w_down)
    returned = from_partner(partial_value[row_count:], "expert", 0)
    expert_out = (partial_value[:row_count] + returned).astype(jnp.bfloat16)
    expert_out = expert_out.reshape(owner_count, group_count, half_cap, model_width)
    returned_rows = across_groups(across_owners(expert_out))
    returned_rows = returned_rows.reshape(slot_count, model_width)
    picked = returned_rows[route_index].reshape(token_count, top_count, model_width)
    weighted = jnp.einsum("tkd,tk->td", picked.astype(jnp.float32), gate_vals)
    mixed = tokens.astype(jnp.float32) + weighted
    return mixed.astype(jnp.bfloat16)


def added(block, arrived):
    return (block.astype(jnp.float32) + arrived.astype(jnp.float32)).astype(jnp.bfloat16)


def scaled(block, scale):
    return (block.astype(jnp.float32) * scale).astype(jnp.bfloat16)


def in_kernel(gate_scales, up_scales, gate_ref, up_ref, out_ref):
    strip, cols = gate_ref.shape
    first = pl.program_id(0) * (strip // BLOCK)
    for row in range(strip // BLOCK):
        rows = slice(row * BLOCK, (row + 1) * BLOCK)
        for col in range(cols // BLOCK):
            at = slice(col * BLOCK, (col + 1) * BLOCK)
            to = 2 * col * BLOCK
            out_ref[rows, to : to + BLOCK] = scaled(gate_ref[rows, at], gate_scales[col, first + row])
            to += BLOCK
            out_ref[rows, to : to + BLOCK] = scaled(up_ref[rows, at], up_scales[col, first + row])


def dequantize_in(gate, up, gate_scales, up_scales):
    rows, cols = gate.shape
    strip = min(rows, 8 * BLOCK)
    block = pl.BlockSpec((strip, cols), lambda i: (i, 0))
    smem = pl.BlockSpec(memory_space=pltpu.SMEM)
    return pl.pallas_call(
        in_kernel,
        grid=(rows // strip,),
        in_specs=[smem, smem, block, block],
        out_specs=pl.BlockSpec((strip, 2 * cols), lambda i: (i, 0)),
        out_shape=jax.ShapeDtypeStruct((rows, 2 * cols), jnp.bfloat16),
        cost_estimate=pl.CostEstimate(
            flops=2 * rows * cols, bytes_accessed=8 * rows * cols, transcendentals=0
        ),
        compiler_params=pltpu.CompilerParams(vmem_limit_bytes=8 * 1024 * 1024),
        name="dequantize_in",
    )(gate_scales.T, up_scales.T, gate, up)


def down_kernel(scales, down_ref, out_ref):
    strip = down_ref.shape[1] // BLOCK
    first = pl.program_id(0) * strip
    for row in range(down_ref.shape[0] // BLOCK):
        rows = slice(row * BLOCK, (row + 1) * BLOCK)
        for col in range(strip):
            cols = slice(col * BLOCK, (col + 1) * BLOCK)
            out_ref[rows, cols] = scaled(down_ref[rows, cols], scales[row, first + col])


def dequantize_down(down, scales):
    rows, cols = down.shape
    strip = min(cols, 8 * BLOCK)
    block = pl.BlockSpec((rows, strip), lambda i: (0, i))
    return pl.pallas_call(
        down_kernel,
        grid=(cols // strip,),
        in_specs=[pl.BlockSpec(memory_space=pltpu.SMEM), block],
        out_specs=block,
        out_shape=jax.ShapeDtypeStruct((rows, cols), jnp.bfloat16),
        cost_estimate=pl.CostEstimate(
            flops=rows * cols, bytes_accessed=4 * rows * cols, transcendentals=0
        ),
        compiler_params=pltpu.CompilerParams(vmem_limit_bytes=8 * 1024 * 1024),
        name="dequantize_down",
    )(scales, down)


def silu(v):
    return v / (1 + jnp.exp(-v))


def expert_kernel(count, experts, own_expert, *refs):
    pieces, refs = refs[:count], refs[count:]
    in_refs, down_refs, refs = refs[:2], refs[2:4], refs[4:]
    outs, (rows, hidden) = refs[:count], refs[count:]
    size, (half, model_width) = pieces[0].shape[0], down_refs[0].shape
    strip = min(4 * BLOCK, model_width)

    weights = []
    for place, piece in enumerate(pieces):
        rows[place * size : (place + 1) * size, :] = piece[:, :model_width]
        marks = piece[:, model_width:].astype(jnp.float32)
        column = lax.broadcasted_iota(jnp.int32, marks.shape, 1)
        chosen = (column == own_expert[0]) | (column == own_expert[0] + experts)
        weights.append(jnp.sum(jnp.where(chosen, marks, 0.0), axis=1, keepdims=True))
    for part, in_ref in enumerate(in_refs):
        for col in range(half // BLOCK):
            at = slice(2 * col * BLOCK, 2 * (col + 1) * BLOCK)
            both = jnp.dot(rows[...], in_ref[:, at], preferred_element_type=jnp.float32)
            value = (silu(both[:, :BLOCK]) * both[:, BLOCK:]).astype(jnp.bfloat16)
            to = part * half + col * BLOCK
            hidden[:, to : to + BLOCK] = value
    for first in range(0, model_width, strip):
        at = slice(first, first + strip)
        value = jnp.dot(hidden[:, :half], down_refs[0][:, at], preferred_element_type=jnp.float32)
        value += jnp.dot(hidden[:, half:], down_refs[1][:, at], preferred_element_type=jnp.float32)
        for place, out in enumerate(outs):
            weighted = value[place * size : (place + 1) * size] * weights[place]
            out[:, at] = weighted.astype(jnp.bfloat16)


def expert_layer(pieces, own_expert, experts, *weights):
    count, size = len(pieces), pieces[0].shape[0]
    model_width, width = weights[0].shape
    total = count * size
    whole = pl.BlockSpec(memory_space=pltpu.VMEM)
    weights = [pltpu.with_memory_space_constraint(weight, pltpu.VMEM) for weight in weights]
    return pl.pallas_call(
        functools.partial(expert_kernel, count, experts),
        in_specs=[pl.BlockSpec(memory_space=pltpu.SMEM)] + [whole] * (count + len(weights)),
        out_specs=[whole] * count,
        out_shape=[jax.ShapeDtypeStruct((size, model_width), jnp.bfloat16)] * count,
        scratch_shapes=[
            pltpu.VMEM((total, model_width), jnp.bfloat16),
            pltpu.VMEM((total, width), jnp.bfloat16),
        ],
        cost_estimate=pl.CostEstimate(
            flops=6 * total * model_width * width,
            bytes_accessed=6 * model_width * width + 4 * total * model_width,
            transcendentals=total * width,
        ),
        compiler_params=pltpu.CompilerParams(vmem_limit_bytes=16 * 1024 * 1024),
        name="expert_layer",
    )(own_expert, *pieces, *weights)


def across_chips(block, far):
    count = lax.axis_size("expert")
    return lax.ppermute(block, "expert", [(low, low ^ 2 * far) for low in range(count)])


def by_sums(tokens, expert_ids, gate_vals, gate_q, up_q, down_q, gate_scale, up_scale, down_scale):
    token_count, model_width = tokens.shape
    group_count = lax.axis_size("dp")
    pair_count = lax.axis_size("expert") // 2
    expert_count = group_count * pair_count
    own_expert = lax.axis_index("dp") * pair_count + lax.axis_index("expert") // 2
    bits = list(range(group_count.bit_length() - 1))
    orders = (bits, bits[::-1])

    named = expert_ids[:, :, None] == jnp.arange(expert_count, dtype=jnp.int32)[None, None, :]
    weight = jnp.sum(jnp.where(named, gate_vals[:, :, None], 0.0), axis=1)
    high = weight.astype(jnp.bfloat16)
    low = (weight - high.astype(jnp.float32)).astype(jnp.bfloat16)
    extra = -(-2 * expert_count // BLOCK) * BLOCK
    pad = jnp.zeros((token_count, extra - 2 * expert_count), jnp.bfloat16)
    payload = jnp.concatenate([tokens, high, low, pad], axis=1)

    together = lax.optimization_barrier
    place = jnp.reshape(own_expert, (1,)).astype(jnp.int32)
    last = len(bits) - 1
    pairs = [(first, first + 1) for first in range(0, pair_count, 2)]
    came = {0: payload, 1: across_chips(payload, 1)}

    def along_z(far):
        low = far & -far
        came[far] = across_chips(came[far ^ low], low)

    gate_own, up_own, came = together((gate_q[0], up_q[0], came))
    pieces, outs, in_other, down_other = {}, {}, None, None
    for number, pair in enumerate(pairs):
        following = pairs[number + 1] if number + 1 < len(pairs) else ()
        blocks = {far: came[far] for far in pair}
        for turn in range(len(bits)):
            if turn < len(following):
                along_z(following[turn])
            arrived = {far: from_partner(blocks[far], "dp", orders[far % 2][turn]) for far in pair}
            if turn == last:
                pieces[pair] = [part for far in pair for part in (blocks[far], arrived[far])]
            else:
                blocks = {
                    far: jnp.concatenate([blocks[far], arrived[far]], axis=0) for far in pair
                }
            if number == 0 and turn == 0:
                in_own = dequantize_in(gate_own, up_own, gate_scale[0], up_scale[0])
                blocks, came, in_own, down_own = together((blocks, came, in_own, down_q[0]))
                in_other = from_partner(in_own, "expert", 0)
                down_own = dequantize_down(down_own, down_scale[0])
            elif number == 0 and turn == last:
                tied = (pieces[pair], came, in_other, down_own)
                pieces[pair], came, in_other, down_own = together(tied)
                down_other = from_partner(down_own, "expert", 0)
                weights = (in_own, in_other, down_own)
            elif number == 1 and turn == 0:
                blocks, pieces, down_other = together((blocks, pieces, down_other))
                held = pieces[pairs[0]]
                outs[pairs[0]] = expert_layer(held, place, expert_count, *weights, down_other)
        if number > 0:
            pieces[pair], outs = together((pieces[pair], outs))
            outs[pair] = expert_layer(pieces[pair], place, expert_count, *weights, down_other)

    total = tokens.astype(jnp.float32)
    sums = {}
    for pair in pairs[::-1]:
        for turn in range(last, -1, -1):
            for where, far in enumerate(pair):
                if turn == last:
                    kept, sent = outs[pair][2 * where : 2 * where + 2]
                else:
                    kept, sent = jnp.split(sums[far], 2, axis=0)
                sums[far] = added(kept, from_partner(sent, "dp", orders[far % 2][turn]))
            sums, outs = together((sums, outs))
        for far in reversed(pair):
            block, low = sums.pop(far), far & -far
            if far == 0:
                total = total + block.astype(jnp.float32)
            elif far == low:
                total = total + across_chips(block, low).astype(jnp.float32)
            else:
                sums[far ^ low] = added(sums[far ^ low], across_chips(block, low))
    return total.astype(jnp.bfloat16)


def shards(tokens, expert_ids, *weights):
    expert_count = lax.axis_size("dp") * lax.axis_size("expert") // 2
    token_count, top_count = expert_ids.shape
    capacity = 2 * token_count * top_count // expert_count
    group_count, pair_count = lax.axis_size("dp"), lax.axis_size("expert") // 2
    powers = all(count & (count - 1) == 0 for count in (group_count, pair_count))
    dense = capacity >= token_count and powers and min(group_count, pair_count) >= 4
    plan = by_sums if dense else by_rows
    return plan(tokens, expert_ids, *weights)


def solution(mesh):
    return jax.shard_map(
        shards,
        mesh=mesh,
        in_specs=(
            P(("dp", "expert"), None),
            P(("dp", "expert"), None),
            P(("dp", "expert"), None),
            P("dp", None, "expert"),
            P("dp", None, "expert"),
            P("dp", "expert", None),
            P("dp", None, "expert"),
            P("dp", None, "expert"),
            P("dp", "expert", None),
        ),
        out_specs=P(("dp", "expert"), None),
        check_vma=False,
    )
```

```python
import functools

import jax
import jax.numpy as jnp
from jax import lax
from jax.experimental import pallas as pl
from jax.experimental.pallas import tpu as pltpu
from jax.sharding import PartitionSpec as P

BLOCK = 128


def from_partner(block, axis, bit):
    count = lax.axis_size(axis)
    route = []
    for low in range(count):
        high = low | 1 << bit
        if high != low and high < count:
            route += [(low, high), (high, low)]
    return lax.ppermute(block, axis, route)


def dequantize(quant_vals, block_scale):
    row_count, col_count = quant_vals.shape
    blocked = quant_vals.reshape(row_count // BLOCK, BLOCK, col_count // BLOCK, BLOCK).astype(
        jnp.float32
    )
    scaled = blocked * block_scale[:, None, :, None]
    return scaled.reshape(row_count, col_count).astype(jnp.bfloat16)


def expert_ffn(inputs, w_gate, w_up, w_down):
    gate_part = jnp.dot(inputs, w_gate, preferred_element_type=jnp.float32)
    up_part = jnp.dot(inputs, w_up, preferred_element_type=jnp.float32)
    hidden = (jax.nn.silu(gate_part) * up_part).astype(jnp.bfloat16)
    return jnp.dot(hidden, w_down, preferred_element_type=jnp.float32)


def across_groups(blocks):
    return lax.all_to_all(blocks, "dp", split_axis=1, concat_axis=1, tiled=True)


def across_owners(blocks):
    return lax.all_to_all(blocks, "expert", split_axis=0, concat_axis=0, tiled=True)


def by_rows(tokens, expert_ids, gate_vals, gate_q, up_q, down_q, gate_scale, up_scale, down_scale):
    group_count = lax.axis_size("dp")
    owner_count = lax.axis_size("expert")
    token_count, model_width = tokens.shape
    top_count = expert_ids.shape[1]
    pair_count = owner_count // 2
    expert_count = group_count * pair_count
    capacity = 2 * token_count * top_count // expert_count
    half_cap = capacity // 2
    slot_count = owner_count * group_count * half_cap
    routes = expert_ids.reshape(-1)
    onehot = (routes[:, None] == jnp.arange(expert_count, dtype=jnp.int32)[None, :]).astype(
        jnp.int32
    )
    earlier = jnp.cumsum(onehot, axis=0) - onehot
    route_slot = jnp.sum(earlier * onehot, axis=1)
    route_group = routes // pair_count
    route_pair = routes % pair_count
    route_owner = 2 * route_pair + route_slot // half_cap
    route_place = route_slot % half_cap
    route_index = (route_owner * group_count + route_group) * half_cap + route_place
    chosen = jnp.arange(slot_count, dtype=jnp.int32)[:, None] == route_index[None, :]
    chosen = jnp.any(chosen.reshape(slot_count, token_count, top_count), axis=2).astype(
        jnp.bfloat16
    )
    outgoing = jnp.dot(chosen, tokens, preferred_element_type=jnp.float32).astype(jnp.bfloat16)
    outgoing = outgoing.reshape(owner_count, group_count, half_cap, model_width)
    arrived = across_owners(across_groups(outgoing))
    own_rows = arrived.reshape(-1, model_width)
    row_count = own_rows.shape[0]
    w_gate = dequantize(gate_q[0], gate_scale[0])
    w_up = dequantize(up_q[0], up_scale[0])
    w_down = dequantize(down_q[0], down_scale[0])
    partner_rows = from_partner(own_rows, "expert", 0)
    both_rows = jnp.concatenate([own_rows, partner_rows], axis=0)
    partial_value = expert_ffn(both_rows, w_gate, w_up, w_down)
    returned = from_partner(partial_value[row_count:], "expert", 0)
    expert_out = (partial_value[:row_count] + returned).astype(jnp.bfloat16)
    expert_out = expert_out.reshape(owner_count, group_count, half_cap, model_width)
    returned_rows = across_groups(across_owners(expert_out))
    returned_rows = returned_rows.reshape(slot_count, model_width)
    picked = returned_rows[route_index].reshape(token_count, top_count, model_width)
    weighted = jnp.einsum("tkd,tk->td", picked.astype(jnp.float32), gate_vals)
    mixed = tokens.astype(jnp.float32) + weighted
    return mixed.astype(jnp.bfloat16)


def added(block, arrived):
    return (block.astype(jnp.float32) + arrived.astype(jnp.float32)).astype(jnp.bfloat16)


def scaled(block, scale):
    return (block.astype(jnp.float32) * scale).astype(jnp.bfloat16)


def in_kernel(gate_scales, up_scales, gate_ref, up_ref, out_ref):
    strip, cols = gate_ref.shape
    first = pl.program_id(0) * (strip // BLOCK)
    for row in range(strip // BLOCK):
        rows = slice(row * BLOCK, (row + 1) * BLOCK)
        for col in range(cols // BLOCK):
            at = slice(col * BLOCK, (col + 1) * BLOCK)
            to = 2 * col * BLOCK
            out_ref[rows, to : to + BLOCK] = scaled(gate_ref[rows, at], gate_scales[col, first + row])
            to += BLOCK
            out_ref[rows, to : to + BLOCK] = scaled(up_ref[rows, at], up_scales[col, first + row])


def dequantize_in(gate, up, gate_scales, up_scales):
    rows, cols = gate.shape
    strip = min(rows, 8 * BLOCK)
    block = pl.BlockSpec((strip, cols), lambda i: (i, 0))
    smem = pl.BlockSpec(memory_space=pltpu.SMEM)
    return pl.pallas_call(
        in_kernel,
        grid=(rows // strip,),
        in_specs=[smem, smem, block, block],
        out_specs=pl.BlockSpec((strip, 2 * cols), lambda i: (i, 0)),
        out_shape=jax.ShapeDtypeStruct((rows, 2 * cols), jnp.bfloat16),
        cost_estimate=pl.CostEstimate(
            flops=2 * rows * cols, bytes_accessed=8 * rows * cols, transcendentals=0
        ),
        compiler_params=pltpu.CompilerParams(vmem_limit_bytes=8 * 1024 * 1024),
        name="dequantize_in",
    )(gate_scales.T, up_scales.T, gate, up)


def down_kernel(scales, down_ref, out_ref):
    strip = down_ref.shape[1] // BLOCK
    first = pl.program_id(0) * strip
    for row in range(down_ref.shape[0] // BLOCK):
        rows = slice(row * BLOCK, (row + 1) * BLOCK)
        for col in range(strip):
            cols = slice(col * BLOCK, (col + 1) * BLOCK)
            out_ref[rows, cols] = scaled(down_ref[rows, cols], scales[row, first + col])


def dequantize_down(down, scales):
    rows, cols = down.shape
    strip = min(cols, 8 * BLOCK)
    block = pl.BlockSpec((rows, strip), lambda i: (0, i))
    return pl.pallas_call(
        down_kernel,
        grid=(cols // strip,),
        in_specs=[pl.BlockSpec(memory_space=pltpu.SMEM), block],
        out_specs=block,
        out_shape=jax.ShapeDtypeStruct((rows, cols), jnp.bfloat16),
        cost_estimate=pl.CostEstimate(
            flops=rows * cols, bytes_accessed=4 * rows * cols, transcendentals=0
        ),
        compiler_params=pltpu.CompilerParams(vmem_limit_bytes=8 * 1024 * 1024),
        name="dequantize_down",
    )(scales, down)


def silu(v):
    return v / (1 + jnp.exp(-v))


def expert_kernel(count, experts, own_expert, *refs):
    pieces, refs = refs[:count], refs[count:]
    in_refs, down_refs, refs = refs[:2], refs[2:4], refs[4:]
    outs, (rows, hidden) = refs[:count], refs[count:]
    size, (half, model_width) = pieces[0].shape[0], down_refs[0].shape
    strip = min(4 * BLOCK, model_width)

    weights = []
    for place, piece in enumerate(pieces):
        rows[place * size : (place + 1) * size, :] = piece[:, :model_width]
        marks = piece[:, model_width:].astype(jnp.float32)
        column = lax.broadcasted_iota(jnp.int32, marks.shape, 1)
        chosen = (column == own_expert[0]) | (column == own_expert[0] + experts)
        weights.append(jnp.sum(jnp.where(chosen, marks, 0.0), axis=1, keepdims=True))
    for part, in_ref in enumerate(in_refs):
        for col in range(half // BLOCK):
            at = slice(2 * col * BLOCK, 2 * (col + 1) * BLOCK)
            both = jnp.dot(rows[...], in_ref[:, at], preferred_element_type=jnp.float32)
            value = (silu(both[:, :BLOCK]) * both[:, BLOCK:]).astype(jnp.bfloat16)
            to = part * half + col * BLOCK
            hidden[:, to : to + BLOCK] = value
    for first in range(0, model_width, strip):
        at = slice(first, first + strip)
        value = jnp.dot(hidden[:, :half], down_refs[0][:, at], preferred_element_type=jnp.float32)
        value += jnp.dot(hidden[:, half:], down_refs[1][:, at], preferred_element_type=jnp.float32)
        for place, out in enumerate(outs):
            weighted = value[place * size : (place + 1) * size] * weights[place]
            out[:, at] = weighted.astype(jnp.bfloat16)


def expert_layer(pieces, own_expert, experts, *weights):
    count, size = len(pieces), pieces[0].shape[0]
    model_width, width = weights[0].shape
    total = count * size
    whole = pl.BlockSpec(memory_space=pltpu.VMEM)
    weights = [pltpu.with_memory_space_constraint(weight, pltpu.VMEM) for weight in weights]
    return pl.pallas_call(
        functools.partial(expert_kernel, count, experts),
        in_specs=[pl.BlockSpec(memory_space=pltpu.SMEM)] + [whole] * (count + len(weights)),
        out_specs=[whole] * count,
        out_shape=[jax.ShapeDtypeStruct((size, model_width), jnp.bfloat16)] * count,
        scratch_shapes=[
            pltpu.VMEM((total, model_width), jnp.bfloat16),
            pltpu.VMEM((total, width), jnp.bfloat16),
        ],
        cost_estimate=pl.CostEstimate(
            flops=6 * total * model_width * width,
            bytes_accessed=6 * model_width * width + 4 * total * model_width,
            transcendentals=total * width,
        ),
        compiler_params=pltpu.CompilerParams(vmem_limit_bytes=16 * 1024 * 1024),
        name="expert_layer",
    )(own_expert, *pieces, *weights)


def across_chips(block, far):
    count = lax.axis_size("expert")
    return lax.ppermute(block, "expert", [(low, low ^ 2 * far) for low in range(count)])


def by_sums(tokens, expert_ids, gate_vals, gate_q, up_q, down_q, gate_scale, up_scale, down_scale):
    token_count, model_width = tokens.shape
    group_count = lax.axis_size("dp")
    pair_count = lax.axis_size("expert") // 2
    expert_count = group_count * pair_count
    own_expert = lax.axis_index("dp") * pair_count + lax.axis_index("expert") // 2
    bits = list(range(group_count.bit_length() - 1))
    orders = (bits, bits[::-1])

    named = expert_ids[:, :, None] == jnp.arange(expert_count, dtype=jnp.int32)[None, None, :]
    weight = jnp.sum(jnp.where(named, gate_vals[:, :, None], 0.0), axis=1)
    high = weight.astype(jnp.bfloat16)
    low = (weight - high.astype(jnp.float32)).astype(jnp.bfloat16)
    extra = -(-2 * expert_count // BLOCK) * BLOCK
    pad = jnp.zeros((token_count, extra - 2 * expert_count), jnp.bfloat16)
    payload = jnp.concatenate([tokens, high, low, pad], axis=1)

    together = lax.optimization_barrier
    place = jnp.reshape(own_expert, (1,)).astype(jnp.int32)
    last = len(bits) - 1
    pairs = [(first, first + 1) for first in range(0, pair_count, 2)]
    place, payload = together((place, payload))
    came = {0: payload, 1: across_chips(payload, 1)}

    def along_z(far):
        low = far & -far
        came[far] = across_chips(came[far ^ low], low)

    in_own = dequantize_in(gate_q[0], up_q[0], gate_scale[0], up_scale[0])
    down_own = dequantize_down(down_q[0], down_scale[0])
    came, in_own, down_own = together((came, in_own, down_own))
    in_other, down_other = from_partner(in_own, "expert", 0), None
    pieces, outs, weights = {}, {}, None
    for number, pair in enumerate(pairs):
        following = pairs[number + 1] if number + 1 < len(pairs) else ()
        blocks = {far: came[far] for far in pair}
        for turn in range(len(bits)):
            if turn < len(following):
                along_z(following[turn])
            arrived = {far: from_partner(blocks[far], "dp", orders[far % 2][turn]) for far in pair}
            if turn == last:
                pieces[pair] = [part for far in pair for part in (blocks[far], arrived[far])]
            else:
                blocks = {
                    far: jnp.concatenate([blocks[far], arrived[far]], axis=0) for far in pair
                }
                if number == 0 and turn == 0:
                    blocks, came, down_own = together((blocks, came, down_own))
                    down_other = from_partner(down_own, "expert", 0)
                elif number == 1 and turn == 0:
                    blocks, outs = together((blocks, outs))
        if number == 0:
            tied = (pieces[pair], came, in_other, down_other)
            pieces[pair], came, in_other, down_other = together(tied)
            weights = (in_own, in_other, down_own, down_other)
        else:
            pieces[pair], outs = together((pieces[pair], outs))
        outs[pair] = expert_layer(pieces[pair], place, expert_count, *weights)

    total = tokens.astype(jnp.float32)
    sums = {}
    for pair in pairs[::-1]:
        for turn in range(last, -1, -1):
            for where, far in enumerate(pair):
                if turn == last:
                    kept, sent = outs[pair][2 * where : 2 * where + 2]
                else:
                    kept, sent = jnp.split(sums[far], 2, axis=0)
                sums[far] = added(kept, from_partner(sent, "dp", orders[far % 2][turn]))
            sums, outs = together((sums, outs))
        for far in reversed(pair):
            block, low = sums.pop(far), far & -far
            if far == 0:
                total = total + block.astype(jnp.float32)
            elif far == low:
                total = total + across_chips(block, low).astype(jnp.float32)
            else:
                sums[far ^ low] = added(sums[far ^ low], across_chips(block, low))
    return total.astype(jnp.bfloat16)


def shards(tokens, expert_ids, *weights):
    expert_count = lax.axis_size("dp") * lax.axis_size("expert") // 2
    token_count, top_count = expert_ids.shape
    capacity = 2 * token_count * top_count // expert_count
    group_count, pair_count = lax.axis_size("dp"), lax.axis_size("expert") // 2
    powers = all(count & (count - 1) == 0 for count in (group_count, pair_count))
    dense = capacity >= token_count and powers and min(group_count, pair_count) >= 4
    plan = by_sums if dense else by_rows
    return plan(tokens, expert_ids, *weights)


def solution(mesh):
    return jax.shard_map(
        shards,
        mesh=mesh,
        in_specs=(
            P(("dp", "expert"), None),
            P(("dp", "expert"), None),
            P(("dp", "expert"), None),
            P("dp", None, "expert"),
            P("dp", None, "expert"),
            P("dp", "expert", None),
            P("dp", None, "expert"),
            P("dp", None, "expert"),
            P("dp", "expert", None),
        ),
        out_specs=P(("dp", "expert"), None),
        check_vma=False,
    )
```

```python
import functools

import jax
import jax.numpy as jnp
from jax import lax
from jax.experimental import pallas as pl
from jax.experimental.pallas import tpu as pltpu
from jax.sharding import PartitionSpec as P

BLOCK = 128


def from_partner(block, axis, bit):
    count = lax.axis_size(axis)
    route = []
    for low in range(count):
        high = low | 1 << bit
        if high != low and high < count:
            route += [(low, high), (high, low)]
    return lax.ppermute(block, axis, route)


def dequantize(quant_vals, block_scale):
    row_count, col_count = quant_vals.shape
    blocked = quant_vals.reshape(row_count // BLOCK, BLOCK, col_count // BLOCK, BLOCK).astype(
        jnp.float32
    )
    scaled = blocked * block_scale[:, None, :, None]
    return scaled.reshape(row_count, col_count).astype(jnp.bfloat16)


def expert_ffn(inputs, w_gate, w_up, w_down):
    gate_part = jnp.dot(inputs, w_gate, preferred_element_type=jnp.float32)
    up_part = jnp.dot(inputs, w_up, preferred_element_type=jnp.float32)
    hidden = (jax.nn.silu(gate_part) * up_part).astype(jnp.bfloat16)
    return jnp.dot(hidden, w_down, preferred_element_type=jnp.float32)


def across_groups(blocks):
    return lax.all_to_all(blocks, "dp", split_axis=1, concat_axis=1, tiled=True)


def across_owners(blocks):
    return lax.all_to_all(blocks, "expert", split_axis=0, concat_axis=0, tiled=True)


def by_rows(tokens, expert_ids, gate_vals, gate_q, up_q, down_q, gate_scale, up_scale, down_scale):
    group_count = lax.axis_size("dp")
    owner_count = lax.axis_size("expert")
    token_count, model_width = tokens.shape
    top_count = expert_ids.shape[1]
    pair_count = owner_count // 2
    expert_count = group_count * pair_count
    capacity = 2 * token_count * top_count // expert_count
    half_cap = capacity // 2
    slot_count = owner_count * group_count * half_cap
    routes = expert_ids.reshape(-1)
    onehot = (routes[:, None] == jnp.arange(expert_count, dtype=jnp.int32)[None, :]).astype(
        jnp.int32
    )
    earlier = jnp.cumsum(onehot, axis=0) - onehot
    route_slot = jnp.sum(earlier * onehot, axis=1)
    route_group = routes // pair_count
    route_pair = routes % pair_count
    route_owner = 2 * route_pair + route_slot // half_cap
    route_place = route_slot % half_cap
    route_index = (route_owner * group_count + route_group) * half_cap + route_place
    chosen = jnp.arange(slot_count, dtype=jnp.int32)[:, None] == route_index[None, :]
    chosen = jnp.any(chosen.reshape(slot_count, token_count, top_count), axis=2).astype(
        jnp.bfloat16
    )
    outgoing = jnp.dot(chosen, tokens, preferred_element_type=jnp.float32).astype(jnp.bfloat16)
    outgoing = outgoing.reshape(owner_count, group_count, half_cap, model_width)
    arrived = across_owners(across_groups(outgoing))
    own_rows = arrived.reshape(-1, model_width)
    row_count = own_rows.shape[0]
    w_gate = dequantize(gate_q[0], gate_scale[0])
    w_up = dequantize(up_q[0], up_scale[0])
    w_down = dequantize(down_q[0], down_scale[0])
    partner_rows = from_partner(own_rows, "expert", 0)
    both_rows = jnp.concatenate([own_rows, partner_rows], axis=0)
    partial_value = expert_ffn(both_rows, w_gate, w_up, w_down)
    returned = from_partner(partial_value[row_count:], "expert", 0)
    expert_out = (partial_value[:row_count] + returned).astype(jnp.bfloat16)
    expert_out = expert_out.reshape(owner_count, group_count, half_cap, model_width)
    returned_rows = across_groups(across_owners(expert_out))
    returned_rows = returned_rows.reshape(slot_count, model_width)
    picked = returned_rows[route_index].reshape(token_count, top_count, model_width)
    weighted = jnp.einsum("tkd,tk->td", picked.astype(jnp.float32), gate_vals)
    mixed = tokens.astype(jnp.float32) + weighted
    return mixed.astype(jnp.bfloat16)


def added(block, arrived):
    return (block.astype(jnp.float32) + arrived.astype(jnp.float32)).astype(jnp.bfloat16)


def scaled(block, scale):
    return (block.astype(jnp.float32) * scale).astype(jnp.bfloat16)


def in_kernel(gate_scales, up_scales, gate_ref, up_ref, out_ref):
    strip, cols = gate_ref.shape
    first = pl.program_id(0) * (strip // BLOCK)
    for row in range(strip // BLOCK):
        rows = slice(row * BLOCK, (row + 1) * BLOCK)
        for col in range(cols // BLOCK):
            at = slice(col * BLOCK, (col + 1) * BLOCK)
            to = 2 * col * BLOCK
            out_ref[rows, to : to + BLOCK] = scaled(gate_ref[rows, at], gate_scales[col, first + row])
            to += BLOCK
            out_ref[rows, to : to + BLOCK] = scaled(up_ref[rows, at], up_scales[col, first + row])


def dequantize_in(gate, up, gate_scales, up_scales):
    rows, cols = gate.shape
    strip = min(rows, 8 * BLOCK)
    block = pl.BlockSpec((strip, cols), lambda i: (i, 0))
    smem = pl.BlockSpec(memory_space=pltpu.SMEM)
    return pl.pallas_call(
        in_kernel,
        grid=(rows // strip,),
        in_specs=[smem, smem, block, block],
        out_specs=pl.BlockSpec((strip, 2 * cols), lambda i: (i, 0)),
        out_shape=jax.ShapeDtypeStruct((rows, 2 * cols), jnp.bfloat16),
        cost_estimate=pl.CostEstimate(
            flops=2 * rows * cols, bytes_accessed=8 * rows * cols, transcendentals=0
        ),
        compiler_params=pltpu.CompilerParams(vmem_limit_bytes=8 * 1024 * 1024),
        name="dequantize_in",
    )(gate_scales.T, up_scales.T, gate, up)


def down_kernel(scales, down_ref, out_ref):
    strip = down_ref.shape[1] // BLOCK
    first = pl.program_id(0) * strip
    for row in range(down_ref.shape[0] // BLOCK):
        rows = slice(row * BLOCK, (row + 1) * BLOCK)
        for col in range(strip):
            cols = slice(col * BLOCK, (col + 1) * BLOCK)
            out_ref[rows, cols] = scaled(down_ref[rows, cols], scales[row, first + col])


def dequantize_down(down, scales):
    rows, cols = down.shape
    strip = min(cols, 8 * BLOCK)
    block = pl.BlockSpec((rows, strip), lambda i: (0, i))
    return pl.pallas_call(
        down_kernel,
        grid=(cols // strip,),
        in_specs=[pl.BlockSpec(memory_space=pltpu.SMEM), block],
        out_specs=block,
        out_shape=jax.ShapeDtypeStruct((rows, cols), jnp.bfloat16),
        cost_estimate=pl.CostEstimate(
            flops=rows * cols, bytes_accessed=4 * rows * cols, transcendentals=0
        ),
        compiler_params=pltpu.CompilerParams(vmem_limit_bytes=8 * 1024 * 1024),
        name="dequantize_down",
    )(scales, down)


def silu(v):
    return v / (1 + jnp.exp(-v))


def expert_kernel(count, experts, own_expert, *refs):
    pieces, refs = refs[:count], refs[count:]
    in_refs, down_refs, refs = refs[:2], refs[2:4], refs[4:]
    outs, (rows, hidden) = refs[:count], refs[count:]
    size, (half, model_width) = pieces[0].shape[0], down_refs[0].shape
    strip = min(4 * BLOCK, model_width)

    weights = []
    for place, piece in enumerate(pieces):
        rows[place * size : (place + 1) * size, :] = piece[:, :model_width]
        marks = piece[:, model_width:].astype(jnp.float32)
        column = lax.broadcasted_iota(jnp.int32, marks.shape, 1)
        chosen = (column == own_expert[0]) | (column == own_expert[0] + experts)
        weights.append(jnp.sum(jnp.where(chosen, marks, 0.0), axis=1, keepdims=True))
    for part, in_ref in enumerate(in_refs):
        for col in range(half // BLOCK):
            at = slice(2 * col * BLOCK, 2 * (col + 1) * BLOCK)
            both = jnp.dot(rows[...], in_ref[:, at], preferred_element_type=jnp.float32)
            value = (silu(both[:, :BLOCK]) * both[:, BLOCK:]).astype(jnp.bfloat16)
            to = part * half + col * BLOCK
            hidden[:, to : to + BLOCK] = value
    for first in range(0, model_width, strip):
        at = slice(first, first + strip)
        value = jnp.dot(hidden[:, :half], down_refs[0][:, at], preferred_element_type=jnp.float32)
        value += jnp.dot(hidden[:, half:], down_refs[1][:, at], preferred_element_type=jnp.float32)
        for place, out in enumerate(outs):
            weighted = value[place * size : (place + 1) * size] * weights[place]
            out[:, at] = weighted.astype(jnp.bfloat16)


def expert_layer(pieces, own_expert, experts, *weights):
    count, size = len(pieces), pieces[0].shape[0]
    model_width, width = weights[0].shape
    total = count * size
    whole = pl.BlockSpec(memory_space=pltpu.VMEM)
    weights = [pltpu.with_memory_space_constraint(weight, pltpu.VMEM) for weight in weights]
    return pl.pallas_call(
        functools.partial(expert_kernel, count, experts),
        in_specs=[pl.BlockSpec(memory_space=pltpu.SMEM)] + [whole] * (count + len(weights)),
        out_specs=[whole] * count,
        out_shape=[jax.ShapeDtypeStruct((size, model_width), jnp.bfloat16)] * count,
        scratch_shapes=[
            pltpu.VMEM((total, model_width), jnp.bfloat16),
            pltpu.VMEM((total, width), jnp.bfloat16),
        ],
        cost_estimate=pl.CostEstimate(
            flops=6 * total * model_width * width,
            bytes_accessed=6 * model_width * width + 4 * total * model_width,
            transcendentals=total * width,
        ),
        compiler_params=pltpu.CompilerParams(vmem_limit_bytes=16 * 1024 * 1024),
        name="expert_layer",
    )(own_expert, *pieces, *weights)


def across_chips(block, far):
    count = lax.axis_size("expert")
    return lax.ppermute(block, "expert", [(low, low ^ 2 * far) for low in range(count)])


def by_sums(tokens, expert_ids, gate_vals, gate_q, up_q, down_q, gate_scale, up_scale, down_scale):
    token_count, model_width = tokens.shape
    group_count = lax.axis_size("dp")
    pair_count = lax.axis_size("expert") // 2
    expert_count = group_count * pair_count
    own_expert = lax.axis_index("dp") * pair_count + lax.axis_index("expert") // 2
    bits = list(range(group_count.bit_length() - 1))
    orders = (bits, bits[::-1])

    named = expert_ids[:, :, None] == jnp.arange(expert_count, dtype=jnp.int32)[None, None, :]
    weight = jnp.sum(jnp.where(named, gate_vals[:, :, None], 0.0), axis=1)
    high = weight.astype(jnp.bfloat16)
    low = (weight - high.astype(jnp.float32)).astype(jnp.bfloat16)
    extra = -(-2 * expert_count // BLOCK) * BLOCK
    pad = jnp.zeros((token_count, extra - 2 * expert_count), jnp.bfloat16)
    half = token_count // 2
    halves = [slice(0, half), slice(half, token_count)]
    payload = [
        jnp.concatenate([part[rows] for part in (tokens, high, low, pad)], axis=1)
        for rows in halves
    ]

    together = lax.optimization_barrier
    place = jnp.reshape(own_expert, (1,)).astype(jnp.int32)
    turns = len(bits)
    groups = [(0,), *((far, far + 1) for far in range(1, pair_count - 1, 2)), (pair_count - 1,)]

    def lanes_of(group):
        if len(group) == 2:
            return [came[far] for far in group]
        return [came[group[0]][:half], came[group[0]][half:]]

    def along_z(far):
        low = far & -far
        came[far] = across_chips(came[far ^ low], low)

    def gather_turn(number, turn):
        blocks = lanes[number]
        arrived = [from_partner(block, "dp", orders[lane][turn]) for lane, block in enumerate(blocks)]
        if turn == turns - 1:
            lanes[number] = [part for pair in zip(blocks, arrived) for part in pair]
        else:
            lanes[number] = [jnp.concatenate(pair, axis=0) for pair in zip(blocks, arrived)]

    def layer(number):
        return expert_layer(lanes[number], place, expert_count, *weights)

    place, payload = together((place, payload))
    lanes, outs = {0: payload}, {}
    near = [{far: across_chips(payload[0], far) for far in groups[1]}]
    gather_turn(0, 0)
    lanes, near, payload, gate_own, up_own, down_own = together(
        (lanes, near, payload, gate_q[0], up_q[0], down_q[0])
    )
    in_own = dequantize_in(gate_own, up_own, gate_scale[0], up_scale[0])
    in_other = from_partner(in_own, "expert", 0)
    down_own = dequantize_down(down_own, down_scale[0])
    near.append({far: across_chips(payload[1], far) for far in groups[1]})
    for turn in range(1, turns):
        gather_turn(0, turn)
    lanes, near, down_own = together((lanes, near, down_own))
    came = {far: jnp.concatenate([part[far] for part in near], axis=0) for far in groups[1]}
    down_other = from_partner(down_own, "expert", 0)
    lanes[1] = lanes_of(groups[1])
    for number in range(1, len(groups)):
        following = groups[number + 1] if number + 1 < len(groups) else ()
        for turn in range(int(number > 1), turns - 1):
            gather_turn(number, turn)
            if turn == int(number > 1):
                for far in following:
                    along_z(far)
            tied = (lanes, came, outs, in_other, down_other)
            lanes, came, outs, in_other, down_other = together(tied)
        weights = (in_own, in_other, down_own, down_other)
        gather_turn(number, turns - 1)
        if following:
            if turns - 1 == int(number > 1):
                for far in following:
                    along_z(far)
            lanes[number + 1] = lanes_of(following)
            gather_turn(number + 1, 0)
        outs[number - 1] = layer(number - 1)
        lanes, outs, came = together((lanes, outs, came))
    final = len(groups) - 1
    outs[final] = layer(final)

    def sum_turn(number, turn):
        result = []
        for lane in range(2):
            if turn == turns - 1:
                kept, sent = outs[number][2 * lane : 2 * lane + 2]
            else:
                kept, sent = jnp.split(sums[number][lane], 2, axis=0)
            result.append(added(kept, from_partner(sent, "dp", orders[lane][turn])))
        sums[number] = result

    def leave(number):
        group, done = groups[number], sums.pop(number)
        done = done if len(group) == 2 else [jnp.concatenate(done, axis=0)]
        ready = dict(zip(group, done))
        for far in reversed(group):
            block, low = ready[far], far & -far
            if far in merged:
                block = added(block, merged.pop(far))
            if far != low:
                came_back = across_chips(block, low)
                into = far ^ low
                merged[into] = added(merged[into], came_back) if into in merged else came_back
            elif number > 1:
                whole = across_chips(block, low)
                parts.append([whole[rows] for rows in halves])
            else:
                leaving[far] = [block[rows] for rows in halves]

    sums, merged, parts, leaving = {}, {}, [], {}
    for number in range(final, 0, -1):
        for turn in range(turns - 1 - int(number < final), -1, -1):
            sum_turn(number, turn)
            if turn == 0 and number > 1:
                sum_turn(number - 1, turns - 1)
            sums, outs, merged = together((sums, outs, merged))
        leave(number)
    back = [{far: across_chips(leaving[far][0], far) for far in groups[1]}]
    for turn in range(turns - 1, 0, -1):
        sum_turn(0, turn)
    sums, back, leaving = together((sums, back, leaving))
    back.append({far: across_chips(leaving[far][1], far) for far in groups[1]})
    sum_turn(0, 0)
    result = []
    for lane, rows in enumerate(halves):
        total = tokens[rows].astype(jnp.float32) + sums[0][lane].astype(jnp.float32)
        for part in [*back[lane].values(), *(part[lane] for part in parts)]:
            total = total + part.astype(jnp.float32)
        result.append(total.astype(jnp.bfloat16))
    return jnp.concatenate(result, axis=0)


def shards(tokens, expert_ids, *weights):
    expert_count = lax.axis_size("dp") * lax.axis_size("expert") // 2
    token_count, top_count = expert_ids.shape
    capacity = 2 * token_count * top_count // expert_count
    group_count, pair_count = lax.axis_size("dp"), lax.axis_size("expert") // 2
    powers = all(count & (count - 1) == 0 for count in (group_count, pair_count))
    dense = capacity >= token_count and powers and min(group_count, pair_count) >= 4
    plan = by_sums if dense else by_rows
    return plan(tokens, expert_ids, *weights)


def solution(mesh):
    return jax.shard_map(
        shards,
        mesh=mesh,
        in_specs=(
            P(("dp", "expert"), None),
            P(("dp", "expert"), None),
            P(("dp", "expert"), None),
            P("dp", None, "expert"),
            P("dp", None, "expert"),
            P("dp", "expert", None),
            P("dp", None, "expert"),
            P("dp", None, "expert"),
            P("dp", "expert", None),
        ),
        out_specs=P(("dp", "expert"), None),
        check_vma=False,
    )
```

```python
import functools

import jax
import jax.numpy as jnp
from jax import lax
from jax.experimental import pallas as pl
from jax.experimental.pallas import tpu as pltpu
from jax.sharding import PartitionSpec as P

BLOCK = 128


def from_partner(block, axis, bit):
    count = lax.axis_size(axis)
    route = []
    for low in range(count):
        high = low | 1 << bit
        if high != low and high < count:
            route += [(low, high), (high, low)]
    return lax.ppermute(block, axis, route)


def dequantize(quant_vals, block_scale):
    row_count, col_count = quant_vals.shape
    blocked = quant_vals.reshape(row_count // BLOCK, BLOCK, col_count // BLOCK, BLOCK).astype(
        jnp.float32
    )
    scaled = blocked * block_scale[:, None, :, None]
    return scaled.reshape(row_count, col_count).astype(jnp.bfloat16)


def expert_ffn(inputs, w_gate, w_up, w_down):
    gate_part = jnp.dot(inputs, w_gate, preferred_element_type=jnp.float32)
    up_part = jnp.dot(inputs, w_up, preferred_element_type=jnp.float32)
    hidden = (jax.nn.silu(gate_part) * up_part).astype(jnp.bfloat16)
    return jnp.dot(hidden, w_down, preferred_element_type=jnp.float32)


def across_groups(blocks):
    return lax.all_to_all(blocks, "dp", split_axis=1, concat_axis=1, tiled=True)


def across_owners(blocks):
    return lax.all_to_all(blocks, "expert", split_axis=0, concat_axis=0, tiled=True)


def by_rows(tokens, expert_ids, gate_vals, gate_q, up_q, down_q, gate_scale, up_scale, down_scale):
    group_count = lax.axis_size("dp")
    owner_count = lax.axis_size("expert")
    token_count, model_width = tokens.shape
    top_count = expert_ids.shape[1]
    pair_count = owner_count // 2
    expert_count = group_count * pair_count
    capacity = 2 * token_count * top_count // expert_count
    half_cap = capacity // 2
    slot_count = owner_count * group_count * half_cap
    routes = expert_ids.reshape(-1)
    onehot = (routes[:, None] == jnp.arange(expert_count, dtype=jnp.int32)[None, :]).astype(
        jnp.int32
    )
    earlier = jnp.cumsum(onehot, axis=0) - onehot
    route_slot = jnp.sum(earlier * onehot, axis=1)
    route_group = routes // pair_count
    route_pair = routes % pair_count
    route_owner = 2 * route_pair + route_slot // half_cap
    route_place = route_slot % half_cap
    route_index = (route_owner * group_count + route_group) * half_cap + route_place
    chosen = jnp.arange(slot_count, dtype=jnp.int32)[:, None] == route_index[None, :]
    chosen = jnp.any(chosen.reshape(slot_count, token_count, top_count), axis=2).astype(
        jnp.bfloat16
    )
    outgoing = jnp.dot(chosen, tokens, preferred_element_type=jnp.float32).astype(jnp.bfloat16)
    outgoing = outgoing.reshape(owner_count, group_count, half_cap, model_width)
    arrived = across_owners(across_groups(outgoing))
    own_rows = arrived.reshape(-1, model_width)
    row_count = own_rows.shape[0]
    w_gate = dequantize(gate_q[0], gate_scale[0])
    w_up = dequantize(up_q[0], up_scale[0])
    w_down = dequantize(down_q[0], down_scale[0])
    partner_rows = from_partner(own_rows, "expert", 0)
    both_rows = jnp.concatenate([own_rows, partner_rows], axis=0)
    partial_value = expert_ffn(both_rows, w_gate, w_up, w_down)
    returned = from_partner(partial_value[row_count:], "expert", 0)
    expert_out = (partial_value[:row_count] + returned).astype(jnp.bfloat16)
    expert_out = expert_out.reshape(owner_count, group_count, half_cap, model_width)
    returned_rows = across_groups(across_owners(expert_out))
    returned_rows = returned_rows.reshape(slot_count, model_width)
    picked = returned_rows[route_index].reshape(token_count, top_count, model_width)
    weighted = jnp.einsum("tkd,tk->td", picked.astype(jnp.float32), gate_vals)
    mixed = tokens.astype(jnp.float32) + weighted
    return mixed.astype(jnp.bfloat16)


def added(block, arrived):
    return (block.astype(jnp.float32) + arrived.astype(jnp.float32)).astype(jnp.bfloat16)


def scaled(block, scale):
    return (block.astype(jnp.float32) * scale).astype(jnp.bfloat16)


def in_kernel(gate_scales, up_scales, gate_ref, up_ref, out_ref):
    strip, cols = gate_ref.shape
    first = pl.program_id(0) * (strip // BLOCK)
    for row in range(strip // BLOCK):
        rows = slice(row * BLOCK, (row + 1) * BLOCK)
        for col in range(cols // BLOCK):
            at = slice(col * BLOCK, (col + 1) * BLOCK)
            to = 2 * col * BLOCK
            out_ref[rows, to : to + BLOCK] = scaled(gate_ref[rows, at], gate_scales[col, first + row])
            to += BLOCK
            out_ref[rows, to : to + BLOCK] = scaled(up_ref[rows, at], up_scales[col, first + row])


def dequantize_in(gate, up, gate_scales, up_scales):
    rows, cols = gate.shape
    strip = min(rows, 8 * BLOCK)
    block = pl.BlockSpec((strip, cols), lambda i: (i, 0))
    smem = pl.BlockSpec(memory_space=pltpu.SMEM)
    return pl.pallas_call(
        in_kernel,
        grid=(rows // strip,),
        in_specs=[smem, smem, block, block],
        out_specs=pl.BlockSpec((strip, 2 * cols), lambda i: (i, 0)),
        out_shape=jax.ShapeDtypeStruct((rows, 2 * cols), jnp.bfloat16),
        cost_estimate=pl.CostEstimate(
            flops=2 * rows * cols, bytes_accessed=8 * rows * cols, transcendentals=0
        ),
        compiler_params=pltpu.CompilerParams(vmem_limit_bytes=8 * 1024 * 1024),
        name="dequantize_in",
    )(gate_scales.T, up_scales.T, gate, up)


def down_kernel(scales, down_ref, out_ref):
    strip = down_ref.shape[1] // BLOCK
    first = pl.program_id(0) * strip
    for row in range(down_ref.shape[0] // BLOCK):
        rows = slice(row * BLOCK, (row + 1) * BLOCK)
        for col in range(strip):
            cols = slice(col * BLOCK, (col + 1) * BLOCK)
            out_ref[rows, cols] = scaled(down_ref[rows, cols], scales[row, first + col])


def dequantize_down(down, scales):
    rows, cols = down.shape
    strip = min(cols, 8 * BLOCK)
    block = pl.BlockSpec((rows, strip), lambda i: (0, i))
    return pl.pallas_call(
        down_kernel,
        grid=(cols // strip,),
        in_specs=[pl.BlockSpec(memory_space=pltpu.SMEM), block],
        out_specs=block,
        out_shape=jax.ShapeDtypeStruct((rows, cols), jnp.bfloat16),
        cost_estimate=pl.CostEstimate(
            flops=rows * cols, bytes_accessed=4 * rows * cols, transcendentals=0
        ),
        compiler_params=pltpu.CompilerParams(vmem_limit_bytes=8 * 1024 * 1024),
        name="dequantize_down",
    )(scales, down)


def silu(v):
    return v / (1 + jnp.exp(-v))


def expert_kernel(count, experts, own_expert, *refs):
    pieces, refs = refs[:count], refs[count:]
    in_refs, down_refs, refs = refs[:2], refs[2:4], refs[4:]
    outs, (rows, hidden) = refs[:count], refs[count:]
    size, (half, model_width) = pieces[0].shape[0], down_refs[0].shape
    strip = min(4 * BLOCK, model_width)

    weights = []
    for place, piece in enumerate(pieces):
        rows[place * size : (place + 1) * size, :] = piece[:, :model_width]
        marks = piece[:, model_width:].astype(jnp.float32)
        column = lax.broadcasted_iota(jnp.int32, marks.shape, 1)
        chosen = (column == own_expert[0]) | (column == own_expert[0] + experts)
        weights.append(jnp.sum(jnp.where(chosen, marks, 0.0), axis=1, keepdims=True))
    for part, in_ref in enumerate(in_refs):
        for col in range(half // BLOCK):
            at = slice(2 * col * BLOCK, 2 * (col + 1) * BLOCK)
            both = jnp.dot(rows[...], in_ref[:, at], preferred_element_type=jnp.float32)
            value = (silu(both[:, :BLOCK]) * both[:, BLOCK:]).astype(jnp.bfloat16)
            to = part * half + col * BLOCK
            hidden[:, to : to + BLOCK] = value
    for first in range(0, model_width, strip):
        at = slice(first, first + strip)
        value = jnp.dot(hidden[:, :half], down_refs[0][:, at], preferred_element_type=jnp.float32)
        value += jnp.dot(hidden[:, half:], down_refs[1][:, at], preferred_element_type=jnp.float32)
        for place, out in enumerate(outs):
            weighted = value[place * size : (place + 1) * size] * weights[place]
            out[:, at] = weighted.astype(jnp.bfloat16)


def expert_layer(pieces, own_expert, experts, *weights):
    count, size = len(pieces), pieces[0].shape[0]
    model_width, width = weights[0].shape
    total = count * size
    whole = pl.BlockSpec(memory_space=pltpu.VMEM)
    weights = [pltpu.with_memory_space_constraint(weight, pltpu.VMEM) for weight in weights]
    return pl.pallas_call(
        functools.partial(expert_kernel, count, experts),
        in_specs=[pl.BlockSpec(memory_space=pltpu.SMEM)] + [whole] * (count + len(weights)),
        out_specs=[whole] * count,
        out_shape=[jax.ShapeDtypeStruct((size, model_width), jnp.bfloat16)] * count,
        scratch_shapes=[
            pltpu.VMEM((total, model_width), jnp.bfloat16),
            pltpu.VMEM((total, width), jnp.bfloat16),
        ],
        cost_estimate=pl.CostEstimate(
            flops=6 * total * model_width * width,
            bytes_accessed=6 * model_width * width + 4 * total * model_width,
            transcendentals=total * width,
        ),
        compiler_params=pltpu.CompilerParams(vmem_limit_bytes=16 * 1024 * 1024),
        name="expert_layer",
    )(own_expert, *pieces, *weights)


def across_chips(block, far):
    count = lax.axis_size("expert")
    return lax.ppermute(block, "expert", [(low, low ^ 2 * far) for low in range(count)])


def by_sums(tokens, expert_ids, gate_vals, gate_q, up_q, down_q, gate_scale, up_scale, down_scale):
    token_count, model_width = tokens.shape
    group_count = lax.axis_size("dp")
    pair_count = lax.axis_size("expert") // 2
    expert_count = group_count * pair_count
    own_expert = lax.axis_index("dp") * pair_count + lax.axis_index("expert") // 2
    bits = list(range(group_count.bit_length() - 1))
    orders = (bits, bits[::-1])

    named = expert_ids[:, :, None] == jnp.arange(expert_count, dtype=jnp.int32)[None, None, :]
    weight = jnp.sum(jnp.where(named, gate_vals[:, :, None], 0.0), axis=1)
    high = weight.astype(jnp.bfloat16)
    low = (weight - high.astype(jnp.float32)).astype(jnp.bfloat16)
    extra = -(-2 * expert_count // BLOCK) * BLOCK
    pad = jnp.zeros((token_count, extra - 2 * expert_count), jnp.bfloat16)
    half = token_count // 2
    halves = [slice(0, half), slice(half, token_count)]
    payload = [
        jnp.concatenate([part[rows] for part in (tokens, high, low, pad)], axis=1)
        for rows in halves
    ]

    together = lax.optimization_barrier
    place = jnp.reshape(own_expert, (1,)).astype(jnp.int32)
    turns = len(bits)
    groups = [(0,), *((far, far + 1) for far in range(1, pair_count - 1, 2)), (pair_count - 1,)]

    def lanes_of(group):
        if len(group) == 2:
            return [came[far] for far in group]
        return [came[group[0]][:half], came[group[0]][half:]]

    def along_z(far):
        low = far & -far
        came[far] = across_chips(came[far ^ low], low)

    def gather_turn(number, turn):
        blocks = lanes[number]
        arrived = [from_partner(block, "dp", orders[lane][turn]) for lane, block in enumerate(blocks)]
        if turn == turns - 1:
            lanes[number] = [part for pair in zip(blocks, arrived) for part in pair]
        else:
            lanes[number] = [jnp.concatenate(pair, axis=0) for pair in zip(blocks, arrived)]

    def layer(number):
        return expert_layer(lanes[number], place, expert_count, *weights)

    place, payload = together((place, payload))
    lanes, outs = {0: payload}, {}
    near = [{far: across_chips(payload[0], far) for far in groups[1]}]
    gather_turn(0, 0)
    in_own = dequantize_in(gate_q[0], up_q[0], gate_scale[0], up_scale[0])
    down_own = dequantize_down(down_q[0], down_scale[0])
    lanes, near, payload, in_own, down_own = together((lanes, near, payload, in_own, down_own))
    in_other = from_partner(in_own, "expert", 0)
    near.append({far: across_chips(payload[1], far) for far in groups[1]})
    for turn in range(1, turns):
        gather_turn(0, turn)
    lanes, near, down_own = together((lanes, near, down_own))
    came = {far: jnp.concatenate([part[far] for part in near], axis=0) for far in groups[1]}
    down_other = from_partner(down_own, "expert", 0)
    lanes[1] = lanes_of(groups[1])
    for number in range(1, len(groups)):
        following = groups[number + 1] if number + 1 < len(groups) else ()
        for turn in range(int(number > 1), turns - 1):
            gather_turn(number, turn)
            if turn == int(number > 1):
                for far in following:
                    along_z(far)
            tied = (lanes, came, outs, in_other, down_other)
            lanes, came, outs, in_other, down_other = together(tied)
        weights = (in_own, in_other, down_own, down_other)
        gather_turn(number, turns - 1)
        if following:
            if turns - 1 == int(number > 1):
                for far in following:
                    along_z(far)
            lanes[number + 1] = lanes_of(following)
            gather_turn(number + 1, 0)
        outs[number - 1] = layer(number - 1)
        lanes, outs, came = together((lanes, outs, came))
    final = len(groups) - 1
    outs[final] = layer(final)

    def sum_turn(number, turn):
        result = []
        for lane in range(2):
            if turn == turns - 1:
                kept, sent = outs[number][2 * lane : 2 * lane + 2]
            else:
                kept, sent = jnp.split(sums[number][lane], 2, axis=0)
            result.append(added(kept, from_partner(sent, "dp", orders[lane][turn])))
        sums[number] = result

    def leave(number):
        group, done = groups[number], sums.pop(number)
        done = done if len(group) == 2 else [jnp.concatenate(done, axis=0)]
        ready = dict(zip(group, done))
        for far in reversed(group):
            block, low = ready[far], far & -far
            if far in merged:
                block = added(block, merged.pop(far))
            if far != low:
                came_back = across_chips(block, low)
                into = far ^ low
                merged[into] = added(merged[into], came_back) if into in merged else came_back
            elif number > 1:
                whole = across_chips(block, low)
                parts.append([whole[rows] for rows in halves])
            else:
                leaving[far] = [block[rows] for rows in halves]

    sums, merged, parts, leaving = {}, {}, [], {}
    for number in range(final, 0, -1):
        for turn in range(turns - 1 - int(number < final), -1, -1):
            sum_turn(number, turn)
            if turn == 0 and number > 1:
                sum_turn(number - 1, turns - 1)
            if turn == 0 and number > 1:
                leave(number)
            sums, outs, merged = together((sums, outs, merged))
    leave(1)
    back = [{far: across_chips(leaving[far][0], far) for far in groups[1]}]
    for turn in range(turns - 1, 0, -1):
        sum_turn(0, turn)
    sums, back, leaving = together((sums, back, leaving))
    back.append({far: across_chips(leaving[far][1], far) for far in groups[1]})
    sum_turn(0, 0)
    result = []
    for lane, rows in enumerate(halves):
        total = tokens[rows].astype(jnp.float32) + sums[0][lane].astype(jnp.float32)
        for part in [*back[lane].values(), *(part[lane] for part in parts)]:
            total = total + part.astype(jnp.float32)
        result.append(total.astype(jnp.bfloat16))
    return jnp.concatenate(result, axis=0)


def shards(tokens, expert_ids, *weights):
    expert_count = lax.axis_size("dp") * lax.axis_size("expert") // 2
    token_count, top_count = expert_ids.shape
    capacity = 2 * token_count * top_count // expert_count
    group_count, pair_count = lax.axis_size("dp"), lax.axis_size("expert") // 2
    powers = all(count & (count - 1) == 0 for count in (group_count, pair_count))
    dense = capacity >= token_count and powers and min(group_count, pair_count) >= 4
    plan = by_sums if dense else by_rows
    return plan(tokens, expert_ids, *weights)


def solution(mesh):
    return jax.shard_map(
        shards,
        mesh=mesh,
        in_specs=(
            P(("dp", "expert"), None),
            P(("dp", "expert"), None),
            P(("dp", "expert"), None),
            P("dp", None, "expert"),
            P("dp", None, "expert"),
            P("dp", "expert", None),
            P("dp", None, "expert"),
            P("dp", None, "expert"),
            P("dp", "expert", None),
        ),
        out_specs=P(("dp", "expert"), None),
        check_vma=False,
    )
```

```python
import functools

import jax
import jax.numpy as jnp
from jax import lax
from jax.experimental import pallas as pl
from jax.experimental.pallas import tpu as pltpu
from jax.sharding import PartitionSpec as P

BLOCK = 128


def from_partner(block, axis, bit):
    count = lax.axis_size(axis)
    route = []
    for low in range(count):
        high = low | 1 << bit
        if high != low and high < count:
            route += [(low, high), (high, low)]
    return lax.ppermute(block, axis, route)


def dequantize(quant_vals, block_scale):
    row_count, col_count = quant_vals.shape
    blocked = quant_vals.reshape(row_count // BLOCK, BLOCK, col_count // BLOCK, BLOCK).astype(
        jnp.float32
    )
    scaled = blocked * block_scale[:, None, :, None]
    return scaled.reshape(row_count, col_count).astype(jnp.bfloat16)


def expert_ffn(inputs, w_gate, w_up, w_down):
    gate_part = jnp.dot(inputs, w_gate, preferred_element_type=jnp.float32)
    up_part = jnp.dot(inputs, w_up, preferred_element_type=jnp.float32)
    hidden = (jax.nn.silu(gate_part) * up_part).astype(jnp.bfloat16)
    return jnp.dot(hidden, w_down, preferred_element_type=jnp.float32)


def across_groups(blocks):
    return lax.all_to_all(blocks, "dp", split_axis=1, concat_axis=1, tiled=True)


def across_owners(blocks):
    return lax.all_to_all(blocks, "expert", split_axis=0, concat_axis=0, tiled=True)


def by_rows(tokens, expert_ids, gate_vals, gate_q, up_q, down_q, gate_scale, up_scale, down_scale):
    group_count = lax.axis_size("dp")
    owner_count = lax.axis_size("expert")
    token_count, model_width = tokens.shape
    top_count = expert_ids.shape[1]
    pair_count = owner_count // 2
    expert_count = group_count * pair_count
    capacity = 2 * token_count * top_count // expert_count
    half_cap = capacity // 2
    slot_count = owner_count * group_count * half_cap
    routes = expert_ids.reshape(-1)
    onehot = (routes[:, None] == jnp.arange(expert_count, dtype=jnp.int32)[None, :]).astype(
        jnp.int32
    )
    earlier = jnp.cumsum(onehot, axis=0) - onehot
    route_slot = jnp.sum(earlier * onehot, axis=1)
    route_group = routes // pair_count
    route_pair = routes % pair_count
    route_owner = 2 * route_pair + route_slot // half_cap
    route_place = route_slot % half_cap
    route_index = (route_owner * group_count + route_group) * half_cap + route_place
    chosen = jnp.arange(slot_count, dtype=jnp.int32)[:, None] == route_index[None, :]
    chosen = jnp.any(chosen.reshape(slot_count, token_count, top_count), axis=2).astype(
        jnp.bfloat16
    )
    outgoing = jnp.dot(chosen, tokens, preferred_element_type=jnp.float32).astype(jnp.bfloat16)
    outgoing = outgoing.reshape(owner_count, group_count, half_cap, model_width)
    arrived = across_owners(across_groups(outgoing))
    own_rows = arrived.reshape(-1, model_width)
    row_count = own_rows.shape[0]
    w_gate = dequantize(gate_q[0], gate_scale[0])
    w_up = dequantize(up_q[0], up_scale[0])
    w_down = dequantize(down_q[0], down_scale[0])
    partner_rows = from_partner(own_rows, "expert", 0)
    both_rows = jnp.concatenate([own_rows, partner_rows], axis=0)
    partial_value = expert_ffn(both_rows, w_gate, w_up, w_down)
    returned = from_partner(partial_value[row_count:], "expert", 0)
    expert_out = (partial_value[:row_count] + returned).astype(jnp.bfloat16)
    expert_out = expert_out.reshape(owner_count, group_count, half_cap, model_width)
    returned_rows = across_groups(across_owners(expert_out))
    returned_rows = returned_rows.reshape(slot_count, model_width)
    picked = returned_rows[route_index].reshape(token_count, top_count, model_width)
    weighted = jnp.einsum("tkd,tk->td", picked.astype(jnp.float32), gate_vals)
    mixed = tokens.astype(jnp.float32) + weighted
    return mixed.astype(jnp.bfloat16)


def added(block, arrived):
    return (block.astype(jnp.float32) + arrived.astype(jnp.float32)).astype(jnp.bfloat16)


def scaled(block, scale):
    return (block.astype(jnp.float32) * scale).astype(jnp.bfloat16)


def in_kernel(gate_scales, up_scales, gate_ref, up_ref, out_ref):
    strip, cols = gate_ref.shape
    first = pl.program_id(0) * (strip // BLOCK)
    for row in range(strip // BLOCK):
        rows = slice(row * BLOCK, (row + 1) * BLOCK)
        for col in range(cols // BLOCK):
            at = slice(col * BLOCK, (col + 1) * BLOCK)
            to = 2 * col * BLOCK
            out_ref[rows, to : to + BLOCK] = scaled(gate_ref[rows, at], gate_scales[col, first + row])
            to += BLOCK
            out_ref[rows, to : to + BLOCK] = scaled(up_ref[rows, at], up_scales[col, first + row])


def dequantize_in(gate, up, gate_scales, up_scales):
    rows, cols = gate.shape
    strip = min(rows, 8 * BLOCK)
    block = pl.BlockSpec((strip, cols), lambda i: (i, 0))
    smem = pl.BlockSpec(memory_space=pltpu.SMEM)
    return pl.pallas_call(
        in_kernel,
        grid=(rows // strip,),
        in_specs=[smem, smem, block, block],
        out_specs=pl.BlockSpec((strip, 2 * cols), lambda i: (i, 0)),
        out_shape=jax.ShapeDtypeStruct((rows, 2 * cols), jnp.bfloat16),
        cost_estimate=pl.CostEstimate(
            flops=2 * rows * cols, bytes_accessed=8 * rows * cols, transcendentals=0
        ),
        compiler_params=pltpu.CompilerParams(vmem_limit_bytes=8 * 1024 * 1024),
        name="dequantize_in",
    )(gate_scales.T, up_scales.T, gate, up)


def down_kernel(scales, down_ref, out_ref):
    strip = down_ref.shape[1] // BLOCK
    first = pl.program_id(0) * strip
    for row in range(down_ref.shape[0] // BLOCK):
        rows = slice(row * BLOCK, (row + 1) * BLOCK)
        for col in range(strip):
            cols = slice(col * BLOCK, (col + 1) * BLOCK)
            out_ref[rows, cols] = scaled(down_ref[rows, cols], scales[row, first + col])


def dequantize_down(down, scales):
    rows, cols = down.shape
    strip = min(cols, 8 * BLOCK)
    block = pl.BlockSpec((rows, strip), lambda i: (0, i))
    return pl.pallas_call(
        down_kernel,
        grid=(cols // strip,),
        in_specs=[pl.BlockSpec(memory_space=pltpu.SMEM), block],
        out_specs=block,
        out_shape=jax.ShapeDtypeStruct((rows, cols), jnp.bfloat16),
        cost_estimate=pl.CostEstimate(
            flops=rows * cols, bytes_accessed=4 * rows * cols, transcendentals=0
        ),
        compiler_params=pltpu.CompilerParams(vmem_limit_bytes=8 * 1024 * 1024),
        name="dequantize_down",
    )(scales, down)


def silu(v):
    return v / (1 + jnp.exp(-v))


def expert_kernel(count, experts, own_expert, *refs):
    pieces, refs = refs[:count], refs[count:]
    in_refs, down_refs, refs = refs[:2], refs[2:4], refs[4:]
    outs, (rows, hidden) = refs[:-2], refs[-2:]
    half, model_width = down_refs[0].shape
    strip = min(4 * BLOCK, model_width)

    weights, first = [], 0
    for piece in pieces:
        size = piece.shape[0]
        rows[first : first + size, :] = piece[:, :model_width]
        marks = piece[:, model_width:].astype(jnp.float32)
        column = lax.broadcasted_iota(jnp.int32, marks.shape, 1)
        chosen = (column == own_expert[0]) | (column == own_expert[0] + experts)
        weights.append(jnp.sum(jnp.where(chosen, marks, 0.0), axis=1, keepdims=True))
        first += size
    weights = jnp.concatenate(weights, axis=0)
    for part, in_ref in enumerate(in_refs):
        for col in range(half // BLOCK):
            at = slice(2 * col * BLOCK, 2 * (col + 1) * BLOCK)
            both = jnp.dot(rows[...], in_ref[:, at], preferred_element_type=jnp.float32)
            value = (silu(both[:, :BLOCK]) * both[:, BLOCK:]).astype(jnp.bfloat16)
            to = part * half + col * BLOCK
            hidden[:, to : to + BLOCK] = value
    for start in range(0, model_width, strip):
        at = slice(start, start + strip)
        value = jnp.dot(hidden[:, :half], down_refs[0][:, at], preferred_element_type=jnp.float32)
        value += jnp.dot(hidden[:, half:], down_refs[1][:, at], preferred_element_type=jnp.float32)
        value, first = (value * weights).astype(jnp.bfloat16), 0
        for out in outs:
            out[:, at] = value[first : first + out.shape[0]]
            first += out.shape[0]


def expert_layer(pieces, out_sizes, own_expert, experts, *weights):
    count, total = len(pieces), sum(out_sizes)
    model_width, width = weights[0].shape
    whole = pl.BlockSpec(memory_space=pltpu.VMEM)
    weights = [pltpu.with_memory_space_constraint(weight, pltpu.VMEM) for weight in weights]
    return pl.pallas_call(
        functools.partial(expert_kernel, count, experts),
        in_specs=[pl.BlockSpec(memory_space=pltpu.SMEM)] + [whole] * (count + len(weights)),
        out_specs=[whole] * len(out_sizes),
        out_shape=[jax.ShapeDtypeStruct((size, model_width), jnp.bfloat16) for size in out_sizes],
        scratch_shapes=[
            pltpu.VMEM((total, model_width), jnp.bfloat16),
            pltpu.VMEM((total, width), jnp.bfloat16),
        ],
        cost_estimate=pl.CostEstimate(
            flops=6 * total * model_width * width,
            bytes_accessed=6 * model_width * width + 4 * total * model_width,
            transcendentals=total * width,
        ),
        compiler_params=pltpu.CompilerParams(vmem_limit_bytes=16 * 1024 * 1024),
        name="expert_layer",
    )(own_expert, *pieces, *weights)


def across_chips(block, far):
    count = lax.axis_size("expert")
    return lax.ppermute(block, "expert", [(low, low ^ 2 * far) for low in range(count)])


def by_sums(tokens, expert_ids, gate_vals, gate_q, up_q, down_q, gate_scale, up_scale, down_scale):
    token_count, model_width = tokens.shape
    group_count = lax.axis_size("dp")
    pair_count = lax.axis_size("expert") // 2
    expert_count = group_count * pair_count
    own_expert = lax.axis_index("dp") * pair_count + lax.axis_index("expert") // 2
    bits = list(range(group_count.bit_length() - 1))
    orders = (bits, bits[::-1])

    named = expert_ids[:, :, None] == jnp.arange(expert_count, dtype=jnp.int32)[None, None, :]
    weight = jnp.sum(jnp.where(named, gate_vals[:, :, None], 0.0), axis=1)
    high = weight.astype(jnp.bfloat16)
    low = (weight - high.astype(jnp.float32)).astype(jnp.bfloat16)
    extra = -(-2 * expert_count // BLOCK) * BLOCK
    pad = jnp.zeros((token_count, extra - 2 * expert_count), jnp.bfloat16)
    half = token_count // 2
    halves = [slice(0, half), slice(half, token_count)]
    payload = [
        jnp.concatenate([part[rows] for part in (tokens, high, low, pad)], axis=1)
        for rows in halves
    ]

    together = lax.optimization_barrier
    place = jnp.reshape(own_expert, (1,)).astype(jnp.int32)
    place, payload = together((place, payload))
    own = jnp.concatenate(payload, axis=0)
    fars, turns = range(2, pair_count), len(bits)
    steps = [[(0, turn)] for turn in range(turns)]
    for far in fars:
        for turn in range(turns):
            if turn == 0 and far > 2:
                steps[-1].append((far, turn))
            else:
                steps.append([(far, turn)])

    def gather_turn(far, turn):
        blocks = lanes[far]
        arrived = [from_partner(block, "dp", orders[lane][turn]) for lane, block in enumerate(blocks)]
        if turn == turns - 1:
            lanes[far] = [part for pair in zip(blocks, arrived) for part in pair]
            gathered.append(far)
        else:
            lanes[far] = [jnp.concatenate(pair, axis=0) for pair in zip(blocks, arrived)]

    def layer(pieces, sizes):
        return expert_layer(pieces, sizes, place, expert_count, *weights)

    def halved_layer(far):
        return layer(lanes[far], [piece.shape[0] for piece in lanes[far]])

    lanes, outs, gathered, came = {0: payload}, {}, [], {}
    kept_rows = half * group_count // 2
    beside = across_chips(own, 1)
    second = [across_chips(payload[0], 2)]
    for number, step in enumerate(steps):
        for far, turn in step:
            if turn == 0 and far > 0:
                lanes[far] = [came[far][rows] for rows in halves]
                if far + 1 in fars:
                    low = (far + 1) & -(far + 1)
                    block = own if low == far + 1 else came[(far + 1) ^ low]
                    came[far + 1] = across_chips(block, low)
        if number == turns + 1:
            kept, other = lanes[0][0::2], lanes[0][1::2]
            rest = jnp.concatenate([*(block[half:] for block in kept), *other], axis=0)
            rest = across_chips(rest, 1)
        if number > turns and gathered:
            ready = gathered.pop(0)
            outs[ready] = halved_layer(ready)
        for far, turn in step:
            gather_turn(far, turn)
        if number == 0:
            in_own = dequantize_in(gate_q[0], up_q[0], gate_scale[0], up_scale[0])
            down_own = dequantize_down(down_q[0], down_scale[0])
            tied = (lanes, own, payload, beside, second, in_own, down_own)
            lanes, own, payload, beside, second, in_own, down_own = together(tied)
            second.append(across_chips(payload[1], 2))
            in_other = from_partner(in_own, "expert", 0)
        elif number == 1:
            lanes, second, down_own = together((lanes, second, down_own))
            came[2] = jnp.concatenate(second, axis=0)
            down_other = from_partner(down_own, "expert", 0)
        elif number == turns:
            tied = (lanes, came, in_other, down_other)
            lanes, came, in_other, down_other = together(tied)
            weights = (in_own, in_other, down_own, down_other)
        elif number < len(steps) - 1:
            lanes, came, outs = together((lanes, came, outs))
        else:
            lanes, rest, outs = together((lanes, rest, outs))
    final = gathered.pop()
    sizes = [piece.shape[0] for piece in lanes[final]]
    returned, *outs[final] = layer([beside, rest, *lanes[final]], [4 * kept_rows, *sizes])

    def sum_turn(far, turn):
        result = []
        for lane in range(2):
            if turn == turns - 1:
                kept, sent = outs[far][2 * lane : 2 * lane + 2]
            else:
                kept, sent = jnp.split(sums[far][lane], 2, axis=0)
            result.append(added(kept, from_partner(sent, "dp", orders[lane][turn])))
        sums[far] = result

    returned = across_chips(returned, 1)
    sums, merged, parts = {}, {}, []
    for step in steps[:turns - 1:-1]:
        for far, turn in reversed(step):
            sum_turn(far, turn)
        far, turn = step[0] if len(step) == 1 else step[1]
        if turn == 0 and far > 2:
            low = far & -far
            block = jnp.concatenate(sums.pop(far), axis=0)
            block = added(block, merged.pop(far)) if far in merged else block
            block = across_chips(block, low)
            if far == low:
                parts.append([block[rows] for rows in halves])
            else:
                into = far ^ low
                merged[into] = added(merged[into], block) if into in merged else block
    sums, outs, merged, returned = together((sums, outs, merged, returned))
    lower = kept_rows - half
    own_parts = [
        jnp.concatenate([returned[:half], returned[2 * half : 2 * half + lower]], axis=0),
        returned[2 * kept_rows : 3 * kept_rows],
        jnp.concatenate([returned[half : 2 * half], returned[2 * half + lower : 2 * kept_rows]], axis=0),
        returned[3 * kept_rows :],
    ]
    outs[0] = [added(block, part) for block, part in zip(outs[0], own_parts)]
    leaving = sums.pop(2)
    if 2 in merged:
        leaving = [added(block, merged[2][rows]) for block, rows in zip(leaving, halves)]
    back = [across_chips(leaving[0], 2)]
    for turn in range(turns - 1, 0, -1):
        sum_turn(0, turn)
    sums, back, leaving = together((sums, back, leaving))
    back.append(across_chips(leaving[1], 2))
    sum_turn(0, 0)
    result = []
    for lane, rows in enumerate(halves):
        total = tokens[rows].astype(jnp.float32) + sums[0][lane].astype(jnp.float32)
        for part in [back[lane], *(part[lane] for part in parts)]:
            total = total + part.astype(jnp.float32)
        result.append(total.astype(jnp.bfloat16))
    return jnp.concatenate(result, axis=0)


def shards(tokens, expert_ids, *weights):
    expert_count = lax.axis_size("dp") * lax.axis_size("expert") // 2
    token_count, top_count = expert_ids.shape
    capacity = 2 * token_count * top_count // expert_count
    group_count, pair_count = lax.axis_size("dp"), lax.axis_size("expert") // 2
    powers = all(count & (count - 1) == 0 for count in (group_count, pair_count))
    dense = capacity >= token_count and powers and min(group_count, pair_count) >= 4
    plan = by_sums if dense else by_rows
    return plan(tokens, expert_ids, *weights)


def solution(mesh):
    return jax.shard_map(
        shards,
        mesh=mesh,
        in_specs=(
            P(("dp", "expert"), None),
            P(("dp", "expert"), None),
            P(("dp", "expert"), None),
            P("dp", None, "expert"),
            P("dp", None, "expert"),
            P("dp", "expert", None),
            P("dp", None, "expert"),
            P("dp", None, "expert"),
            P("dp", "expert", None),
        ),
        out_specs=P(("dp", "expert"), None),
        check_vma=False,
    )
```

```python
import functools

import jax
import jax.numpy as jnp
from jax import lax
from jax.experimental import pallas as pl
from jax.experimental.pallas import tpu as pltpu
from jax.sharding import PartitionSpec as P

BLOCK = 128


def from_partner(block, axis, bit):
    count = lax.axis_size(axis)
    route = []
    for low in range(count):
        high = low | 1 << bit
        if high != low and high < count:
            route += [(low, high), (high, low)]
    return lax.ppermute(block, axis, route)


def dequantize(quant_vals, block_scale):
    row_count, col_count = quant_vals.shape
    blocked = quant_vals.reshape(row_count // BLOCK, BLOCK, col_count // BLOCK, BLOCK).astype(
        jnp.float32
    )
    scaled = blocked * block_scale[:, None, :, None]
    return scaled.reshape(row_count, col_count).astype(jnp.bfloat16)


def expert_ffn(inputs, w_gate, w_up, w_down):
    gate_part = jnp.dot(inputs, w_gate, preferred_element_type=jnp.float32)
    up_part = jnp.dot(inputs, w_up, preferred_element_type=jnp.float32)
    hidden = (jax.nn.silu(gate_part) * up_part).astype(jnp.bfloat16)
    return jnp.dot(hidden, w_down, preferred_element_type=jnp.float32)


def across_groups(blocks):
    return lax.all_to_all(blocks, "dp", split_axis=1, concat_axis=1, tiled=True)


def across_owners(blocks):
    return lax.all_to_all(blocks, "expert", split_axis=0, concat_axis=0, tiled=True)


def by_rows(tokens, expert_ids, gate_vals, gate_q, up_q, down_q, gate_scale, up_scale, down_scale):
    group_count = lax.axis_size("dp")
    owner_count = lax.axis_size("expert")
    token_count, model_width = tokens.shape
    top_count = expert_ids.shape[1]
    pair_count = owner_count // 2
    expert_count = group_count * pair_count
    capacity = 2 * token_count * top_count // expert_count
    half_cap = capacity // 2
    slot_count = owner_count * group_count * half_cap
    routes = expert_ids.reshape(-1)
    onehot = (routes[:, None] == jnp.arange(expert_count, dtype=jnp.int32)[None, :]).astype(
        jnp.int32
    )
    earlier = jnp.cumsum(onehot, axis=0) - onehot
    route_slot = jnp.sum(earlier * onehot, axis=1)
    route_group = routes // pair_count
    route_pair = routes % pair_count
    route_owner = 2 * route_pair + route_slot // half_cap
    route_place = route_slot % half_cap
    route_index = (route_owner * group_count + route_group) * half_cap + route_place
    chosen = jnp.arange(slot_count, dtype=jnp.int32)[:, None] == route_index[None, :]
    chosen = jnp.any(chosen.reshape(slot_count, token_count, top_count), axis=2).astype(
        jnp.bfloat16
    )
    outgoing = jnp.dot(chosen, tokens, preferred_element_type=jnp.float32).astype(jnp.bfloat16)
    outgoing = outgoing.reshape(owner_count, group_count, half_cap, model_width)
    arrived = across_owners(across_groups(outgoing))
    own_rows = arrived.reshape(-1, model_width)
    row_count = own_rows.shape[0]
    w_gate = dequantize(gate_q[0], gate_scale[0])
    w_up = dequantize(up_q[0], up_scale[0])
    w_down = dequantize(down_q[0], down_scale[0])
    partner_rows = from_partner(own_rows, "expert", 0)
    both_rows = jnp.concatenate([own_rows, partner_rows], axis=0)
    partial_value = expert_ffn(both_rows, w_gate, w_up, w_down)
    returned = from_partner(partial_value[row_count:], "expert", 0)
    expert_out = (partial_value[:row_count] + returned).astype(jnp.bfloat16)
    expert_out = expert_out.reshape(owner_count, group_count, half_cap, model_width)
    returned_rows = across_groups(across_owners(expert_out))
    returned_rows = returned_rows.reshape(slot_count, model_width)
    picked = returned_rows[route_index].reshape(token_count, top_count, model_width)
    weighted = jnp.einsum("tkd,tk->td", picked.astype(jnp.float32), gate_vals)
    mixed = tokens.astype(jnp.float32) + weighted
    return mixed.astype(jnp.bfloat16)


def added(block, arrived):
    return (block.astype(jnp.float32) + arrived.astype(jnp.float32)).astype(jnp.bfloat16)


def scaled(block, scale):
    return (block.astype(jnp.float32) * scale).astype(jnp.bfloat16)


def in_kernel(gate_scales, up_scales, gate_ref, up_ref, out_ref):
    strip, cols = gate_ref.shape
    first = pl.program_id(0) * (strip // BLOCK)
    for row in range(strip // BLOCK):
        rows = slice(row * BLOCK, (row + 1) * BLOCK)
        for col in range(cols // BLOCK):
            at = slice(col * BLOCK, (col + 1) * BLOCK)
            to = 2 * col * BLOCK
            out_ref[rows, to : to + BLOCK] = scaled(gate_ref[rows, at], gate_scales[col, first + row])
            to += BLOCK
            out_ref[rows, to : to + BLOCK] = scaled(up_ref[rows, at], up_scales[col, first + row])


def dequantize_in(gate, up, gate_scales, up_scales):
    rows, cols = gate.shape
    strip = min(rows, 8 * BLOCK)
    block = pl.BlockSpec((strip, cols), lambda i: (i, 0))
    smem = pl.BlockSpec(memory_space=pltpu.SMEM)
    return pl.pallas_call(
        in_kernel,
        grid=(rows // strip,),
        in_specs=[smem, smem, block, block],
        out_specs=pl.BlockSpec((strip, 2 * cols), lambda i: (i, 0)),
        out_shape=jax.ShapeDtypeStruct((rows, 2 * cols), jnp.bfloat16),
        cost_estimate=pl.CostEstimate(
            flops=2 * rows * cols, bytes_accessed=8 * rows * cols, transcendentals=0
        ),
        compiler_params=pltpu.CompilerParams(vmem_limit_bytes=8 * 1024 * 1024),
        name="dequantize_in",
    )(gate_scales.T, up_scales.T, gate, up)


def down_kernel(scales, down_ref, out_ref):
    strip = down_ref.shape[1] // BLOCK
    first = pl.program_id(0) * strip
    for row in range(down_ref.shape[0] // BLOCK):
        rows = slice(row * BLOCK, (row + 1) * BLOCK)
        for col in range(strip):
            cols = slice(col * BLOCK, (col + 1) * BLOCK)
            out_ref[rows, cols] = scaled(down_ref[rows, cols], scales[row, first + col])


def dequantize_down(down, scales):
    rows, cols = down.shape
    strip = min(cols, 8 * BLOCK)
    block = pl.BlockSpec((rows, strip), lambda i: (0, i))
    return pl.pallas_call(
        down_kernel,
        grid=(cols // strip,),
        in_specs=[pl.BlockSpec(memory_space=pltpu.SMEM), block],
        out_specs=block,
        out_shape=jax.ShapeDtypeStruct((rows, cols), jnp.bfloat16),
        cost_estimate=pl.CostEstimate(
            flops=rows * cols, bytes_accessed=4 * rows * cols, transcendentals=0
        ),
        compiler_params=pltpu.CompilerParams(vmem_limit_bytes=8 * 1024 * 1024),
        name="dequantize_down",
    )(scales, down)


def silu(v):
    return v / (1 + jnp.exp(-v))


def expert_kernel(count, experts, own_expert, *refs):
    pieces, refs = refs[:count], refs[count:]
    in_refs, down_refs, refs = refs[:2], refs[2:4], refs[4:]
    outs, (rows, hidden) = refs[:count], refs[count:]
    size, (half, model_width) = pieces[0].shape[0], down_refs[0].shape
    strip = min(4 * BLOCK, model_width)

    weights = []
    for place, piece in enumerate(pieces):
        rows[place * size : (place + 1) * size, :] = piece[:, :model_width]
        marks = piece[:, model_width:].astype(jnp.float32)
        column = lax.broadcasted_iota(jnp.int32, marks.shape, 1)
        chosen = (column == own_expert[0]) | (column == own_expert[0] + experts)
        weights.append(jnp.sum(jnp.where(chosen, marks, 0.0), axis=1, keepdims=True))
    for part, in_ref in enumerate(in_refs):
        for col in range(half // BLOCK):
            at = slice(2 * col * BLOCK, 2 * (col + 1) * BLOCK)
            both = jnp.dot(rows[...], in_ref[:, at], preferred_element_type=jnp.float32)
            value = (silu(both[:, :BLOCK]) * both[:, BLOCK:]).astype(jnp.bfloat16)
            to = part * half + col * BLOCK
            hidden[:, to : to + BLOCK] = value
    for first in range(0, model_width, strip):
        at = slice(first, first + strip)
        value = jnp.dot(hidden[:, :half], down_refs[0][:, at], preferred_element_type=jnp.float32)
        value += jnp.dot(hidden[:, half:], down_refs[1][:, at], preferred_element_type=jnp.float32)
        for place, out in enumerate(outs):
            weighted = value[place * size : (place + 1) * size] * weights[place]
            out[:, at] = weighted.astype(jnp.bfloat16)


def expert_layer(pieces, own_expert, experts, *weights):
    count, size = len(pieces), pieces[0].shape[0]
    model_width, width = weights[0].shape
    total = count * size
    whole = pl.BlockSpec(memory_space=pltpu.VMEM)
    weights = [pltpu.with_memory_space_constraint(weight, pltpu.VMEM) for weight in weights]
    return pl.pallas_call(
        functools.partial(expert_kernel, count, experts),
        in_specs=[pl.BlockSpec(memory_space=pltpu.SMEM)] + [whole] * (count + len(weights)),
        out_specs=[whole] * count,
        out_shape=[jax.ShapeDtypeStruct((size, model_width), jnp.bfloat16)] * count,
        scratch_shapes=[
            pltpu.VMEM((total, model_width), jnp.bfloat16),
            pltpu.VMEM((total, width), jnp.bfloat16),
        ],
        cost_estimate=pl.CostEstimate(
            flops=6 * total * model_width * width,
            bytes_accessed=6 * model_width * width + 4 * total * model_width,
            transcendentals=total * width,
        ),
        compiler_params=pltpu.CompilerParams(vmem_limit_bytes=16 * 1024 * 1024),
        name="expert_layer",
    )(own_expert, *pieces, *weights)


def payload_kernel(expert_count, tokens, ids, vals, *outs):
    token_count, model_width = tokens.shape
    extra = outs[0].shape[1] - model_width
    column = lax.broadcasted_iota(jnp.int32, (token_count, extra), 1)
    weight = jnp.zeros((token_count, extra), jnp.float32)
    for choice in range(ids.shape[1]):
        expert = ids[:, choice : choice + 1]
        named = (column == expert) | (column == expert + expert_count)
        weight += jnp.where(named, vals[:, choice : choice + 1], 0.0)
    high = weight.astype(jnp.bfloat16).astype(jnp.float32)
    marks = jnp.where(column < expert_count, high, weight - high).astype(jnp.bfloat16)
    half = token_count // 2
    for place, out in enumerate(outs):
        rows = slice(place * half, (place + 1) * half)
        out[:, :model_width] = tokens[rows, :]
        out[:, model_width:] = marks[rows]


def build_payload(tokens, ids, vals, expert_count):
    token_count, model_width = tokens.shape
    width = model_width + -(-2 * expert_count // BLOCK) * BLOCK
    whole = pl.BlockSpec(memory_space=pltpu.VMEM)
    return pl.pallas_call(
        functools.partial(payload_kernel, expert_count),
        in_specs=[whole] * 3,
        out_specs=[whole] * 2,
        out_shape=[jax.ShapeDtypeStruct((token_count // 2, width), jnp.bfloat16)] * 2,
        compiler_params=pltpu.CompilerParams(vmem_limit_bytes=4 * 1024 * 1024),
        name="build_payload",
    )(tokens, ids, vals)


def across_chips(block, far):
    count = lax.axis_size("expert")
    return lax.ppermute(block, "expert", [(low, low ^ 2 * far) for low in range(count)])


def by_sums(tokens, expert_ids, gate_vals, gate_q, up_q, down_q, gate_scale, up_scale, down_scale):
    token_count, model_width = tokens.shape
    group_count = lax.axis_size("dp")
    pair_count = lax.axis_size("expert") // 2
    expert_count = group_count * pair_count
    own_expert = lax.axis_index("dp") * pair_count + lax.axis_index("expert") // 2
    bits = list(range(group_count.bit_length() - 1))
    orders = (bits, bits[::-1])

    half = token_count // 2
    halves = [slice(0, half), slice(half, token_count)]
    payload = build_payload(tokens, expert_ids, gate_vals, expert_count)

    together = lax.optimization_barrier
    place = jnp.reshape(own_expert, (1,)).astype(jnp.int32)
    turns = len(bits)
    groups = [(0,), *((far, far + 1) for far in range(1, pair_count - 1, 2)), (pair_count - 1,)]

    def lanes_of(group):
        if len(group) == 2:
            return [came[far] for far in group]
        return [came[group[0]][:half], came[group[0]][half:]]

    def along_z(far):
        low = far & -far
        came[far] = across_chips(came[far ^ low], low)

    def gather_turn(number, turn):
        blocks = lanes[number]
        arrived = [from_partner(block, "dp", orders[lane][turn]) for lane, block in enumerate(blocks)]
        if turn == turns - 1:
            lanes[number] = [part for pair in zip(blocks, arrived) for part in pair]
        else:
            lanes[number] = [jnp.concatenate(pair, axis=0) for pair in zip(blocks, arrived)]

    def layer(number):
        return expert_layer(lanes[number], place, expert_count, *weights)

    place, payload = together((place, payload))
    lanes, outs = {0: payload}, {}
    near = [{far: across_chips(payload[0], far) for far in groups[1]}]
    gather_turn(0, 0)
    in_own = dequantize_in(gate_q[0], up_q[0], gate_scale[0], up_scale[0])
    down_own = dequantize_down(down_q[0], down_scale[0])
    lanes, near, payload, in_own, down_own = together((lanes, near, payload, in_own, down_own))
    in_other = from_partner(in_own, "expert", 0)
    near.append({far: across_chips(payload[1], far) for far in groups[1]})
    for turn in range(1, turns):
        gather_turn(0, turn)
    lanes, near, down_own = together((lanes, near, down_own))
    came = {far: jnp.concatenate([part[far] for part in near], axis=0) for far in groups[1]}
    down_other = from_partner(down_own, "expert", 0)
    lanes[1] = lanes_of(groups[1])
    for number in range(1, len(groups)):
        following = groups[number + 1] if number + 1 < len(groups) else ()
        for turn in range(int(number > 1), turns - 1):
            gather_turn(number, turn)
            if turn == int(number > 1):
                for far in following:
                    along_z(far)
            tied = (lanes, came, outs, in_other, down_other)
            lanes, came, outs, in_other, down_other = together(tied)
        weights = (in_own, in_other, down_own, down_other)
        gather_turn(number, turns - 1)
        if following:
            if turns - 1 == int(number > 1):
                for far in following:
                    along_z(far)
            lanes[number + 1] = lanes_of(following)
            gather_turn(number + 1, 0)
        outs[number - 1] = layer(number - 1)
        lanes, outs, came = together((lanes, outs, came))
    final = len(groups) - 1
    outs[final] = layer(final)

    def sum_turn(number, turn):
        result = []
        for lane in range(2):
            if turn == turns - 1:
                kept, sent = outs[number][2 * lane : 2 * lane + 2]
            else:
                kept, sent = jnp.split(sums[number][lane], 2, axis=0)
            result.append(added(kept, from_partner(sent, "dp", orders[lane][turn])))
        sums[number] = result

    def leave(number):
        group, done = groups[number], sums.pop(number)
        done = done if len(group) == 2 else [jnp.concatenate(done, axis=0)]
        ready = dict(zip(group, done))
        for far in reversed(group):
            block, low = ready[far], far & -far
            if far in merged:
                block = added(block, merged.pop(far))
            if far != low:
                came_back = across_chips(block, low)
                into = far ^ low
                merged[into] = added(merged[into], came_back) if into in merged else came_back
            else:
                whole = across_chips(block, low)
                parts.append([whole[rows] for rows in halves])

    sums, merged, parts = {}, {}, []
    for number in range(final, 0, -1):
        for turn in range(turns - 1 - int(number < final), -1, -1):
            sum_turn(number, turn)
            if turn == 0 and number > 1:
                sum_turn(number - 1, turns - 1)
        leave(number)
    for turn in range(turns - 1, -1, -1):
        sum_turn(0, turn)
    result = []
    for lane, rows in enumerate(halves):
        total = tokens[rows].astype(jnp.float32) + sums[0][lane].astype(jnp.float32)
        for part in parts:
            total = total + part[lane].astype(jnp.float32)
        result.append(total.astype(jnp.bfloat16))
    return jnp.concatenate(result, axis=0)


def shards(tokens, expert_ids, *weights):
    expert_count = lax.axis_size("dp") * lax.axis_size("expert") // 2
    token_count, top_count = expert_ids.shape
    capacity = 2 * token_count * top_count // expert_count
    group_count, pair_count = lax.axis_size("dp"), lax.axis_size("expert") // 2
    powers = all(count & (count - 1) == 0 for count in (group_count, pair_count))
    dense = capacity >= token_count and powers and min(group_count, pair_count) >= 4
    plan = by_sums if dense else by_rows
    return plan(tokens, expert_ids, *weights)


def solution(mesh):
    return jax.shard_map(
        shards,
        mesh=mesh,
        in_specs=(
            P(("dp", "expert"), None),
            P(("dp", "expert"), None),
            P(("dp", "expert"), None),
            P("dp", None, "expert"),
            P("dp", None, "expert"),
            P("dp", "expert", None),
            P("dp", None, "expert"),
            P("dp", None, "expert"),
            P("dp", "expert", None),
        ),
        out_specs=P(("dp", "expert"), None),
        check_vma=False,
    )
```

```python
import functools

import jax
import jax.numpy as jnp
from jax import lax
from jax.experimental import pallas as pl
from jax.experimental.pallas import tpu as pltpu
from jax.sharding import PartitionSpec as P

BLOCK = 128


def from_partner(block, axis, bit):
    count = lax.axis_size(axis)
    route = []
    for low in range(count):
        high = low | 1 << bit
        if high != low and high < count:
            route += [(low, high), (high, low)]
    return lax.ppermute(block, axis, route)


def dequantize(quant_vals, block_scale):
    row_count, col_count = quant_vals.shape
    blocked = quant_vals.reshape(row_count // BLOCK, BLOCK, col_count // BLOCK, BLOCK).astype(
        jnp.float32
    )
    scaled = blocked * block_scale[:, None, :, None]
    return scaled.reshape(row_count, col_count).astype(jnp.bfloat16)


def expert_ffn(inputs, w_gate, w_up, w_down):
    gate_part = jnp.dot(inputs, w_gate, preferred_element_type=jnp.float32)
    up_part = jnp.dot(inputs, w_up, preferred_element_type=jnp.float32)
    hidden = (jax.nn.silu(gate_part) * up_part).astype(jnp.bfloat16)
    return jnp.dot(hidden, w_down, preferred_element_type=jnp.float32)


def across_groups(blocks):
    return lax.all_to_all(blocks, "dp", split_axis=1, concat_axis=1, tiled=True)


def across_owners(blocks):
    return lax.all_to_all(blocks, "expert", split_axis=0, concat_axis=0, tiled=True)


def by_rows(tokens, expert_ids, gate_vals, gate_q, up_q, down_q, gate_scale, up_scale, down_scale):
    group_count = lax.axis_size("dp")
    owner_count = lax.axis_size("expert")
    token_count, model_width = tokens.shape
    top_count = expert_ids.shape[1]
    pair_count = owner_count // 2
    expert_count = group_count * pair_count
    capacity = 2 * token_count * top_count // expert_count
    half_cap = capacity // 2
    slot_count = owner_count * group_count * half_cap
    routes = expert_ids.reshape(-1)
    onehot = (routes[:, None] == jnp.arange(expert_count, dtype=jnp.int32)[None, :]).astype(
        jnp.int32
    )
    earlier = jnp.cumsum(onehot, axis=0) - onehot
    route_slot = jnp.sum(earlier * onehot, axis=1)
    route_group = routes // pair_count
    route_pair = routes % pair_count
    route_owner = 2 * route_pair + route_slot // half_cap
    route_place = route_slot % half_cap
    route_index = (route_owner * group_count + route_group) * half_cap + route_place
    chosen = jnp.arange(slot_count, dtype=jnp.int32)[:, None] == route_index[None, :]
    chosen = jnp.any(chosen.reshape(slot_count, token_count, top_count), axis=2).astype(
        jnp.bfloat16
    )
    outgoing = jnp.dot(chosen, tokens, preferred_element_type=jnp.float32).astype(jnp.bfloat16)
    outgoing = outgoing.reshape(owner_count, group_count, half_cap, model_width)
    arrived = across_owners(across_groups(outgoing))
    own_rows = arrived.reshape(-1, model_width)
    row_count = own_rows.shape[0]
    w_gate = dequantize(gate_q[0], gate_scale[0])
    w_up = dequantize(up_q[0], up_scale[0])
    w_down = dequantize(down_q[0], down_scale[0])
    partner_rows = from_partner(own_rows, "expert", 0)
    both_rows = jnp.concatenate([own_rows, partner_rows], axis=0)
    partial_value = expert_ffn(both_rows, w_gate, w_up, w_down)
    returned = from_partner(partial_value[row_count:], "expert", 0)
    expert_out = (partial_value[:row_count] + returned).astype(jnp.bfloat16)
    expert_out = expert_out.reshape(owner_count, group_count, half_cap, model_width)
    returned_rows = across_groups(across_owners(expert_out))
    returned_rows = returned_rows.reshape(slot_count, model_width)
    picked = returned_rows[route_index].reshape(token_count, top_count, model_width)
    weighted = jnp.einsum("tkd,tk->td", picked.astype(jnp.float32), gate_vals)
    mixed = tokens.astype(jnp.float32) + weighted
    return mixed.astype(jnp.bfloat16)


def added(block, arrived):
    return (block.astype(jnp.float32) + arrived.astype(jnp.float32)).astype(jnp.bfloat16)


def scaled(block, scale):
    return (block.astype(jnp.float32) * scale).astype(jnp.bfloat16)


def in_kernel(gate_scales, up_scales, gate_ref, up_ref, out_ref):
    strip, cols = gate_ref.shape
    first = pl.program_id(0) * (strip // BLOCK)
    for row in range(strip // BLOCK):
        rows = slice(row * BLOCK, (row + 1) * BLOCK)
        for col in range(cols // BLOCK):
            at = slice(col * BLOCK, (col + 1) * BLOCK)
            to = 2 * col * BLOCK
            out_ref[rows, to : to + BLOCK] = scaled(gate_ref[rows, at], gate_scales[col, first + row])
            to += BLOCK
            out_ref[rows, to : to + BLOCK] = scaled(up_ref[rows, at], up_scales[col, first + row])


def dequantize_in(gate, up, gate_scales, up_scales):
    rows, cols = gate.shape
    strip = min(rows, 8 * BLOCK)
    block = pl.BlockSpec((strip, cols), lambda i: (i, 0))
    smem = pl.BlockSpec(memory_space=pltpu.SMEM)
    return pl.pallas_call(
        in_kernel,
        grid=(rows // strip,),
        in_specs=[smem, smem, block, block],
        out_specs=pl.BlockSpec((strip, 2 * cols), lambda i: (i, 0)),
        out_shape=jax.ShapeDtypeStruct((rows, 2 * cols), jnp.bfloat16),
        cost_estimate=pl.CostEstimate(
            flops=2 * rows * cols, bytes_accessed=8 * rows * cols, transcendentals=0
        ),
        compiler_params=pltpu.CompilerParams(vmem_limit_bytes=8 * 1024 * 1024),
        name="dequantize_in",
    )(gate_scales.T, up_scales.T, gate, up)


def down_kernel(scales, down_ref, out_ref):
    strip = down_ref.shape[1] // BLOCK
    first = pl.program_id(0) * strip
    for row in range(down_ref.shape[0] // BLOCK):
        rows = slice(row * BLOCK, (row + 1) * BLOCK)
        for col in range(strip):
            cols = slice(col * BLOCK, (col + 1) * BLOCK)
            out_ref[rows, cols] = scaled(down_ref[rows, cols], scales[row, first + col])


def dequantize_down(down, scales):
    rows, cols = down.shape
    strip = min(cols, 8 * BLOCK)
    block = pl.BlockSpec((rows, strip), lambda i: (0, i))
    return pl.pallas_call(
        down_kernel,
        grid=(cols // strip,),
        in_specs=[pl.BlockSpec(memory_space=pltpu.SMEM), block],
        out_specs=block,
        out_shape=jax.ShapeDtypeStruct((rows, cols), jnp.bfloat16),
        cost_estimate=pl.CostEstimate(
            flops=rows * cols, bytes_accessed=4 * rows * cols, transcendentals=0
        ),
        compiler_params=pltpu.CompilerParams(vmem_limit_bytes=8 * 1024 * 1024),
        name="dequantize_down",
    )(scales, down)


def silu(v):
    return v / (1 + jnp.exp(-v))


def expert_kernel(count, experts, own_expert, *refs):
    pieces, refs = refs[:count], refs[count:]
    in_refs, down_refs, refs = refs[:2], refs[2:4], refs[4:]
    outs, (rows, hidden) = refs[:count], refs[count:]
    size, (half, model_width) = pieces[0].shape[0], down_refs[0].shape
    strip = min(4 * BLOCK, model_width)

    weights = []
    for place, piece in enumerate(pieces):
        rows[place * size : (place + 1) * size, :] = piece[:, :model_width]
        marks = piece[:, model_width:].astype(jnp.float32)
        column = lax.broadcasted_iota(jnp.int32, marks.shape, 1)
        chosen = (column == own_expert[0]) | (column == own_expert[0] + experts)
        weights.append(jnp.sum(jnp.where(chosen, marks, 0.0), axis=1, keepdims=True))
    for part, in_ref in enumerate(in_refs):
        for col in range(half // BLOCK):
            at = slice(2 * col * BLOCK, 2 * (col + 1) * BLOCK)
            both = jnp.dot(rows[...], in_ref[:, at], preferred_element_type=jnp.float32)
            value = (silu(both[:, :BLOCK]) * both[:, BLOCK:]).astype(jnp.bfloat16)
            to = part * half + col * BLOCK
            hidden[:, to : to + BLOCK] = value
    for first in range(0, model_width, strip):
        at = slice(first, first + strip)
        value = jnp.dot(hidden[:, :half], down_refs[0][:, at], preferred_element_type=jnp.float32)
        value += jnp.dot(hidden[:, half:], down_refs[1][:, at], preferred_element_type=jnp.float32)
        for place, out in enumerate(outs):
            weighted = value[place * size : (place + 1) * size] * weights[place]
            out[:, at] = weighted.astype(jnp.bfloat16)


def expert_layer(pieces, own_expert, experts, *weights):
    count, size = len(pieces), pieces[0].shape[0]
    model_width, width = weights[0].shape
    total = count * size
    whole = pl.BlockSpec(memory_space=pltpu.VMEM)
    weights = [pltpu.with_memory_space_constraint(weight, pltpu.VMEM) for weight in weights]
    return pl.pallas_call(
        functools.partial(expert_kernel, count, experts),
        in_specs=[pl.BlockSpec(memory_space=pltpu.SMEM)] + [whole] * (count + len(weights)),
        out_specs=[whole] * count,
        out_shape=[jax.ShapeDtypeStruct((size, model_width), jnp.bfloat16)] * count,
        scratch_shapes=[
            pltpu.VMEM((total, model_width), jnp.bfloat16),
            pltpu.VMEM((total, width), jnp.bfloat16),
        ],
        cost_estimate=pl.CostEstimate(
            flops=6 * total * model_width * width,
            bytes_accessed=6 * model_width * width + 4 * total * model_width,
            transcendentals=total * width,
        ),
        compiler_params=pltpu.CompilerParams(vmem_limit_bytes=16 * 1024 * 1024),
        name="expert_layer",
    )(own_expert, *pieces, *weights)


def across_chips(block, far):
    count = lax.axis_size("expert")
    return lax.ppermute(block, "expert", [(low, low ^ 2 * far) for low in range(count)])


def by_sums(tokens, expert_ids, gate_vals, gate_q, up_q, down_q, gate_scale, up_scale, down_scale):
    token_count, model_width = tokens.shape
    group_count = lax.axis_size("dp")
    pair_count = lax.axis_size("expert") // 2
    expert_count = group_count * pair_count
    own_expert = lax.axis_index("dp") * pair_count + lax.axis_index("expert") // 2
    bits = list(range(group_count.bit_length() - 1))
    orders = (bits, bits[::-1])

    named = expert_ids[:, :, None] == jnp.arange(expert_count, dtype=jnp.int32)[None, None, :]
    weight = jnp.sum(jnp.where(named, gate_vals[:, :, None], 0.0), axis=1)
    high = weight.astype(jnp.bfloat16)
    low = (weight - high.astype(jnp.float32)).astype(jnp.bfloat16)
    extra = -(-2 * expert_count // BLOCK) * BLOCK
    pad = jnp.zeros((token_count, extra - 2 * expert_count), jnp.bfloat16)
    half = token_count // 2
    halves = [slice(0, half), slice(half, token_count)]
    payload = [
        jnp.concatenate([part[rows] for part in (tokens, high, low, pad)], axis=1)
        for rows in halves
    ]

    together = lax.optimization_barrier
    place = jnp.reshape(own_expert, (1,)).astype(jnp.int32)
    turns = len(bits)
    groups = [(0,), *((far, far + 1) for far in range(1, pair_count - 1, 2)), (pair_count - 1,)]

    def lanes_of(group):
        if len(group) == 2:
            return [came[far] for far in group]
        return [came[group[0]][:half], came[group[0]][half:]]

    def along_z(far):
        low = far & -far
        came[far] = across_chips(came[far ^ low], low)

    def gather_turn(number, turn):
        blocks = lanes[number]
        arrived = [from_partner(block, "dp", orders[lane][turn]) for lane, block in enumerate(blocks)]
        if turn == turns - 1:
            lanes[number] = [part for pair in zip(blocks, arrived) for part in pair]
        else:
            lanes[number] = [jnp.concatenate(pair, axis=0) for pair in zip(blocks, arrived)]

    def layer(number):
        return expert_layer(lanes[number], place, expert_count, *weights)

    place, payload = together((place, payload))
    lanes, outs = {0: payload}, {}
    came = {0: jnp.concatenate(payload, axis=0)}
    for far in groups[1]:
        along_z(far)
    gather_turn(0, 0)
    in_own = dequantize_in(gate_q[0], up_q[0], gate_scale[0], up_scale[0])
    down_own = dequantize_down(down_q[0], down_scale[0])
    lanes, came, in_own, down_own = together((lanes, came, in_own, down_own))
    in_other = from_partner(in_own, "expert", 0)
    for turn in range(1, turns):
        gather_turn(0, turn)
    lanes, came, down_own = together((lanes, came, down_own))
    down_other = from_partner(down_own, "expert", 0)
    lanes[1] = lanes_of(groups[1])
    for number in range(1, len(groups)):
        following = groups[number + 1] if number + 1 < len(groups) else ()
        for turn in range(int(number > 1), turns - 1):
            gather_turn(number, turn)
            if turn == int(number > 1):
                for far in following:
                    along_z(far)
            tied = (lanes, came, outs, in_other, down_other)
            lanes, came, outs, in_other, down_other = together(tied)
        weights = (in_own, in_other, down_own, down_other)
        gather_turn(number, turns - 1)
        if following:
            if turns - 1 == int(number > 1):
                for far in following:
                    along_z(far)
            lanes[number + 1] = lanes_of(following)
            gather_turn(number + 1, 0)
        outs[number - 1] = layer(number - 1)
        lanes, outs, came = together((lanes, outs, came))
    final = len(groups) - 1
    outs[final] = layer(final)

    def sum_turn(number, turn):
        result = []
        for lane in range(2):
            if turn == turns - 1:
                kept, sent = outs[number][2 * lane : 2 * lane + 2]
            else:
                kept, sent = jnp.split(sums[number][lane], 2, axis=0)
            result.append(added(kept, from_partner(sent, "dp", orders[lane][turn])))
        sums[number] = result

    def leave(number):
        group, done = groups[number], sums.pop(number)
        done = done if len(group) == 2 else [jnp.concatenate(done, axis=0)]
        ready = dict(zip(group, done))
        for far in reversed(group):
            block, low = ready[far], far & -far
            if far in merged:
                block = added(block, merged.pop(far))
            if far != low:
                came_back = across_chips(block, low)
                into = far ^ low
                merged[into] = added(merged[into], came_back) if into in merged else came_back
            else:
                whole = across_chips(block, low)
                parts.append([whole[rows] for rows in halves])

    sums, merged, parts = {}, {}, []
    for number in range(final, 0, -1):
        for turn in range(turns - 1 - int(number < final), -1, -1):
            sum_turn(number, turn)
            if turn == 0 and number > 1:
                sum_turn(number - 1, turns - 1)
        if number > 1:
            leave(number)
        sums, outs = together((sums, outs))
    sums, merged = together((sums, merged))
    leave(1)
    for turn in range(turns - 1, -1, -1):
        sum_turn(0, turn)
    result = []
    for lane, rows in enumerate(halves):
        total = tokens[rows].astype(jnp.float32) + sums[0][lane].astype(jnp.float32)
        for part in parts:
            total = total + part[lane].astype(jnp.float32)
        result.append(total.astype(jnp.bfloat16))
    return jnp.concatenate(result, axis=0)


def shards(tokens, expert_ids, *weights):
    expert_count = lax.axis_size("dp") * lax.axis_size("expert") // 2
    token_count, top_count = expert_ids.shape
    capacity = 2 * token_count * top_count // expert_count
    group_count, pair_count = lax.axis_size("dp"), lax.axis_size("expert") // 2
    powers = all(count & (count - 1) == 0 for count in (group_count, pair_count))
    dense = capacity >= token_count and powers and min(group_count, pair_count) >= 4
    plan = by_sums if dense else by_rows
    return plan(tokens, expert_ids, *weights)


def solution(mesh):
    return jax.shard_map(
        shards,
        mesh=mesh,
        in_specs=(
            P(("dp", "expert"), None),
            P(("dp", "expert"), None),
            P(("dp", "expert"), None),
            P("dp", None, "expert"),
            P("dp", None, "expert"),
            P("dp", "expert", None),
            P("dp", None, "expert"),
            P("dp", None, "expert"),
            P("dp", "expert", None),
        ),
        out_specs=P(("dp", "expert"), None),
        check_vma=False,
    )
```

```python
import functools

import jax
import jax.numpy as jnp
from jax import lax
from jax.experimental import pallas as pl
from jax.experimental.pallas import tpu as pltpu
from jax.sharding import PartitionSpec as P

BLOCK = 128


def from_partner(block, axis, bit):
    count = lax.axis_size(axis)
    route = []
    for low in range(count):
        high = low | 1 << bit
        if high != low and high < count:
            route += [(low, high), (high, low)]
    return lax.ppermute(block, axis, route)


def dequantize(quant_vals, block_scale):
    row_count, col_count = quant_vals.shape
    blocked = quant_vals.reshape(row_count // BLOCK, BLOCK, col_count // BLOCK, BLOCK).astype(
        jnp.float32
    )
    scaled = blocked * block_scale[:, None, :, None]
    return scaled.reshape(row_count, col_count).astype(jnp.bfloat16)


def expert_ffn(inputs, w_gate, w_up, w_down):
    gate_part = jnp.dot(inputs, w_gate, preferred_element_type=jnp.float32)
    up_part = jnp.dot(inputs, w_up, preferred_element_type=jnp.float32)
    hidden = (jax.nn.silu(gate_part) * up_part).astype(jnp.bfloat16)
    return jnp.dot(hidden, w_down, preferred_element_type=jnp.float32)


def across_groups(blocks):
    return lax.all_to_all(blocks, "dp", split_axis=1, concat_axis=1, tiled=True)


def across_owners(blocks):
    return lax.all_to_all(blocks, "expert", split_axis=0, concat_axis=0, tiled=True)


def by_rows(tokens, expert_ids, gate_vals, gate_q, up_q, down_q, gate_scale, up_scale, down_scale):
    group_count = lax.axis_size("dp")
    owner_count = lax.axis_size("expert")
    token_count, model_width = tokens.shape
    top_count = expert_ids.shape[1]
    pair_count = owner_count // 2
    expert_count = group_count * pair_count
    capacity = 2 * token_count * top_count // expert_count
    half_cap = capacity // 2
    slot_count = owner_count * group_count * half_cap
    routes = expert_ids.reshape(-1)
    onehot = (routes[:, None] == jnp.arange(expert_count, dtype=jnp.int32)[None, :]).astype(
        jnp.int32
    )
    earlier = jnp.cumsum(onehot, axis=0) - onehot
    route_slot = jnp.sum(earlier * onehot, axis=1)
    route_group = routes // pair_count
    route_pair = routes % pair_count
    route_owner = 2 * route_pair + route_slot // half_cap
    route_place = route_slot % half_cap
    route_index = (route_owner * group_count + route_group) * half_cap + route_place
    chosen = jnp.arange(slot_count, dtype=jnp.int32)[:, None] == route_index[None, :]
    chosen = jnp.any(chosen.reshape(slot_count, token_count, top_count), axis=2).astype(
        jnp.bfloat16
    )
    outgoing = jnp.dot(chosen, tokens, preferred_element_type=jnp.float32).astype(jnp.bfloat16)
    outgoing = outgoing.reshape(owner_count, group_count, half_cap, model_width)
    arrived = across_owners(across_groups(outgoing))
    own_rows = arrived.reshape(-1, model_width)
    row_count = own_rows.shape[0]
    w_gate = dequantize(gate_q[0], gate_scale[0])
    w_up = dequantize(up_q[0], up_scale[0])
    w_down = dequantize(down_q[0], down_scale[0])
    partner_rows = from_partner(own_rows, "expert", 0)
    both_rows = jnp.concatenate([own_rows, partner_rows], axis=0)
    partial_value = expert_ffn(both_rows, w_gate, w_up, w_down)
    returned = from_partner(partial_value[row_count:], "expert", 0)
    expert_out = (partial_value[:row_count] + returned).astype(jnp.bfloat16)
    expert_out = expert_out.reshape(owner_count, group_count, half_cap, model_width)
    returned_rows = across_groups(across_owners(expert_out))
    returned_rows = returned_rows.reshape(slot_count, model_width)
    picked = returned_rows[route_index].reshape(token_count, top_count, model_width)
    weighted = jnp.einsum("tkd,tk->td", picked.astype(jnp.float32), gate_vals)
    mixed = tokens.astype(jnp.float32) + weighted
    return mixed.astype(jnp.bfloat16)


def added(block, arrived):
    return (block.astype(jnp.float32) + arrived.astype(jnp.float32)).astype(jnp.bfloat16)


def scaled(block, scale):
    return (block.astype(jnp.float32) * scale).astype(jnp.bfloat16)


def dequantize_kernel(gate_scales, up_scales, down_scales, gate, up, down, in_out, down_out, *scratch):
    gate_raw, up_raw, down_raw, in_sems, down_sems = scratch
    rows, cols = gate.shape
    chunks, down_chunks = in_sems.shape[1], down_sems.shape[0]
    depth, down_depth = rows // chunks, down.shape[0] // down_chunks

    def in_copy(part, chunk):
        source, target = ((gate, gate_raw), (up, up_raw))[part]
        at = pl.ds(pl.multiple_of(chunk * depth, depth), depth)
        return pltpu.make_async_copy(source.at[at], target.at[at], in_sems.at[part, chunk])

    def down_copy(chunk):
        at = pl.ds(pl.multiple_of(chunk * down_depth, down_depth), down_depth)
        return pltpu.make_async_copy(down.at[at], down_raw.at[at], down_sems.at[chunk])

    for chunk in range(chunks):
        for part in range(2):
            in_copy(part, chunk).start()
    for chunk in range(down_chunks):
        down_copy(chunk).start()

    @pl.loop(0, chunks)
    def _(chunk):
        in_copy(0, chunk).wait()
        in_copy(1, chunk).wait()
        for block in range(depth // BLOCK):
            row = chunk * (depth // BLOCK) + block
            at = pl.ds(pl.multiple_of(row * BLOCK, BLOCK), BLOCK)
            for col in range(cols // BLOCK):
                from_cols = slice(col * BLOCK, (col + 1) * BLOCK)
                to = 2 * col * BLOCK
                value = scaled(gate_raw[at, from_cols], gate_scales[col, row])
                in_out[at, to : to + BLOCK] = value
                to += BLOCK
                value = scaled(up_raw[at, from_cols], up_scales[col, row])
                in_out[at, to : to + BLOCK] = value

    @pl.loop(0, down_chunks)
    def _(chunk):
        down_copy(chunk).wait()
        for block in range(down_depth // BLOCK):
            row = chunk * (down_depth // BLOCK) + block
            at = pl.ds(pl.multiple_of(row * BLOCK, BLOCK), BLOCK)
            for col in range(down.shape[1] // BLOCK):
                cols_at = slice(col * BLOCK, (col + 1) * BLOCK)
                down_out[at, cols_at] = scaled(down_raw[at, cols_at], down_scales[row, col])


def dequantize_half(quants, scales):
    rows, cols = quants[0].shape
    chunks, down_chunks = max(1, rows // (4 * BLOCK)), max(1, cols // BLOCK)
    quants = [pltpu.with_memory_space_constraint(quant, pltpu.HBM) for quant in quants]
    whole = pl.BlockSpec(memory_space=pltpu.VMEM)
    return pl.pallas_call(
        dequantize_kernel,
        in_specs=[pl.BlockSpec(memory_space=pltpu.SMEM)] * 3 + [pl.BlockSpec(memory_space=pl.ANY)] * 3,
        out_specs=[whole] * 2,
        out_shape=[
            jax.ShapeDtypeStruct((rows, 2 * cols), jnp.bfloat16),
            jax.ShapeDtypeStruct(quants[2].shape, jnp.bfloat16),
        ],
        scratch_shapes=[
            *(pltpu.VMEM(quant.shape, jnp.bfloat16) for quant in quants),
            pltpu.SemaphoreType.DMA((2, chunks)),
            pltpu.SemaphoreType.DMA((down_chunks,)),
        ],
        cost_estimate=pl.CostEstimate(
            flops=3 * rows * cols, bytes_accessed=12 * rows * cols, transcendentals=0
        ),
        compiler_params=pltpu.CompilerParams(vmem_limit_bytes=24 * 1024 * 1024),
        name="dequantize_half",
    )(*scales, *quants)


def silu(v):
    return v / (1 + jnp.exp(-v))


def expert_kernel(count, experts, own_expert, *refs):
    pieces, refs = refs[:count], refs[count:]
    in_refs, down_refs, refs = refs[:2], refs[2:4], refs[4:]
    outs, (rows, hidden) = refs[:count], refs[count:]
    size, (half, model_width) = pieces[0].shape[0], down_refs[0].shape
    strip = min(4 * BLOCK, model_width)

    weights = []
    for place, piece in enumerate(pieces):
        rows[place * size : (place + 1) * size, :] = piece[:, :model_width]
        marks = piece[:, model_width:].astype(jnp.float32)
        column = lax.broadcasted_iota(jnp.int32, marks.shape, 1)
        chosen = (column == own_expert[0]) | (column == own_expert[0] + experts)
        weights.append(jnp.sum(jnp.where(chosen, marks, 0.0), axis=1, keepdims=True))
    for part, in_ref in enumerate(in_refs):
        for col in range(half // BLOCK):
            at = slice(2 * col * BLOCK, 2 * (col + 1) * BLOCK)
            both = jnp.dot(rows[...], in_ref[:, at], preferred_element_type=jnp.float32)
            value = (silu(both[:, :BLOCK]) * both[:, BLOCK:]).astype(jnp.bfloat16)
            to = part * half + col * BLOCK
            hidden[:, to : to + BLOCK] = value
    for first in range(0, model_width, strip):
        at = slice(first, first + strip)
        value = jnp.dot(hidden[:, :half], down_refs[0][:, at], preferred_element_type=jnp.float32)
        value += jnp.dot(hidden[:, half:], down_refs[1][:, at], preferred_element_type=jnp.float32)
        for place, out in enumerate(outs):
            weighted = value[place * size : (place + 1) * size] * weights[place]
            out[:, at] = weighted.astype(jnp.bfloat16)


def expert_layer(pieces, own_expert, experts, *weights):
    count, size = len(pieces), pieces[0].shape[0]
    model_width, width = weights[0].shape
    total = count * size
    whole = pl.BlockSpec(memory_space=pltpu.VMEM)
    weights = [pltpu.with_memory_space_constraint(weight, pltpu.VMEM) for weight in weights]
    return pl.pallas_call(
        functools.partial(expert_kernel, count, experts),
        in_specs=[pl.BlockSpec(memory_space=pltpu.SMEM)] + [whole] * (count + len(weights)),
        out_specs=[whole] * count,
        out_shape=[jax.ShapeDtypeStruct((size, model_width), jnp.bfloat16)] * count,
        scratch_shapes=[
            pltpu.VMEM((total, model_width), jnp.bfloat16),
            pltpu.VMEM((total, width), jnp.bfloat16),
        ],
        cost_estimate=pl.CostEstimate(
            flops=6 * total * model_width * width,
            bytes_accessed=6 * model_width * width + 4 * total * model_width,
            transcendentals=total * width,
        ),
        compiler_params=pltpu.CompilerParams(vmem_limit_bytes=16 * 1024 * 1024),
        name="expert_layer",
    )(own_expert, *pieces, *weights)


def across_chips(block, far):
    count = lax.axis_size("expert")
    return lax.ppermute(block, "expert", [(low, low ^ 2 * far) for low in range(count)])


def by_sums(tokens, expert_ids, gate_vals, gate_q, up_q, down_q, gate_scale, up_scale, down_scale):
    token_count, model_width = tokens.shape
    group_count = lax.axis_size("dp")
    pair_count = lax.axis_size("expert") // 2
    expert_count = group_count * pair_count
    own_expert = lax.axis_index("dp") * pair_count + lax.axis_index("expert") // 2
    bits = list(range(group_count.bit_length() - 1))
    orders = (bits, bits[::-1])

    named = expert_ids[:, :, None] == jnp.arange(expert_count, dtype=jnp.int32)[None, None, :]
    weight = jnp.sum(jnp.where(named, gate_vals[:, :, None], 0.0), axis=1)
    high = weight.astype(jnp.bfloat16)
    low = (weight - high.astype(jnp.float32)).astype(jnp.bfloat16)
    extra = -(-2 * expert_count // BLOCK) * BLOCK
    pad = jnp.zeros((token_count, extra - 2 * expert_count), jnp.bfloat16)
    half = token_count // 2
    halves = [slice(0, half), slice(half, token_count)]
    payload = [
        jnp.concatenate([part[rows] for part in (tokens, high, low, pad)], axis=1)
        for rows in halves
    ]

    together = lax.optimization_barrier
    place = jnp.reshape(own_expert, (1,)).astype(jnp.int32)
    turns = len(bits)
    groups = [(0,), *((far, far + 1) for far in range(1, pair_count - 1, 2)), (pair_count - 1,)]

    def lanes_of(group):
        if len(group) == 2:
            return [came[far] for far in group]
        return [came[group[0]][:half], came[group[0]][half:]]

    def along_z(far):
        low = far & -far
        came[far] = across_chips(came[far ^ low], low)

    def gather_turn(number, turn):
        blocks = lanes[number]
        arrived = [from_partner(block, "dp", orders[lane][turn]) for lane, block in enumerate(blocks)]
        if turn == turns - 1:
            lanes[number] = [part for pair in zip(blocks, arrived) for part in pair]
        else:
            lanes[number] = [jnp.concatenate(pair, axis=0) for pair in zip(blocks, arrived)]

    def layer(number):
        return expert_layer(lanes[number], place, expert_count, *weights)

    place, payload = together((place, payload))
    lanes, outs = {0: payload}, {}
    near = [{far: across_chips(payload[0], far) for far in groups[1]}]
    gather_turn(0, 0)
    in_own, down_own = dequantize_half(
        (gate_q[0], up_q[0], down_q[0]), (gate_scale[0].T, up_scale[0].T, down_scale[0])
    )
    lanes, near, payload, in_own, down_own = together((lanes, near, payload, in_own, down_own))
    in_other = from_partner(in_own, "expert", 0)
    near.append({far: across_chips(payload[1], far) for far in groups[1]})
    for turn in range(1, turns):
        gather_turn(0, turn)
    lanes, near, down_own = together((lanes, near, down_own))
    came = {far: jnp.concatenate([part[far] for part in near], axis=0) for far in groups[1]}
    down_other = from_partner(down_own, "expert", 0)
    lanes[1] = lanes_of(groups[1])
    for number in range(1, len(groups)):
        following = groups[number + 1] if number + 1 < len(groups) else ()
        for turn in range(int(number > 1), turns - 1):
            gather_turn(number, turn)
            if turn == int(number > 1):
                for far in following:
                    along_z(far)
            tied = (lanes, came, outs, in_other, down_other)
            lanes, came, outs, in_other, down_other = together(tied)
        weights = (in_own, in_other, down_own, down_other)
        gather_turn(number, turns - 1)
        if following:
            if turns - 1 == int(number > 1):
                for far in following:
                    along_z(far)
            lanes[number + 1] = lanes_of(following)
            gather_turn(number + 1, 0)
        outs[number - 1] = layer(number - 1)
        if number + 2 != len(groups):
            lanes, outs, came = together((lanes, outs, came))
    final = len(groups) - 1
    outs[final] = layer(final)

    def sum_turn(number, turn):
        result = []
        for lane in range(2):
            if turn == turns - 1:
                kept, sent = outs[number][2 * lane : 2 * lane + 2]
            else:
                kept, sent = jnp.split(sums[number][lane], 2, axis=0)
            result.append(added(kept, from_partner(sent, "dp", orders[lane][turn])))
        sums[number] = result

    def leave(number):
        group, done = groups[number], sums.pop(number)
        done = done if len(group) == 2 else [jnp.concatenate(done, axis=0)]
        ready = dict(zip(group, done))
        for far in reversed(group):
            block, low = ready[far], far & -far
            if far in merged:
                block = added(block, merged.pop(far))
            if far != low:
                came_back = across_chips(block, low)
                into = far ^ low
                merged[into] = added(merged[into], came_back) if into in merged else came_back
            else:
                whole = across_chips(block, low)
                parts.append([whole[rows] for rows in halves])

    sums, merged, parts = {}, {}, []
    for number in range(final, 0, -1):
        for turn in range(turns - 1 - int(number < final), -1, -1):
            sum_turn(number, turn)
            if turn == 0 and number > 1:
                sum_turn(number - 1, turns - 1)
        if number > 1:
            leave(number)
        sums, outs = together((sums, outs))
    sums, merged = together((sums, merged))
    leave(1)
    for turn in range(turns - 1, -1, -1):
        sum_turn(0, turn)
    result = []
    for lane, rows in enumerate(halves):
        total = tokens[rows].astype(jnp.float32) + sums[0][lane].astype(jnp.float32)
        for part in parts:
            total = total + part[lane].astype(jnp.float32)
        result.append(total.astype(jnp.bfloat16))
    return jnp.concatenate(result, axis=0)


def shards(tokens, expert_ids, *weights):
    expert_count = lax.axis_size("dp") * lax.axis_size("expert") // 2
    token_count, top_count = expert_ids.shape
    capacity = 2 * token_count * top_count // expert_count
    group_count, pair_count = lax.axis_size("dp"), lax.axis_size("expert") // 2
    powers = all(count & (count - 1) == 0 for count in (group_count, pair_count))
    dense = capacity >= token_count and powers and min(group_count, pair_count) >= 4
    plan = by_sums if dense else by_rows
    return plan(tokens, expert_ids, *weights)


def solution(mesh):
    return jax.shard_map(
        shards,
        mesh=mesh,
        in_specs=(
            P(("dp", "expert"), None),
            P(("dp", "expert"), None),
            P(("dp", "expert"), None),
            P("dp", None, "expert"),
            P("dp", None, "expert"),
            P("dp", "expert", None),
            P("dp", None, "expert"),
            P("dp", None, "expert"),
            P("dp", "expert", None),
        ),
        out_specs=P(("dp", "expert"), None),
        check_vma=False,
    )
```

```python
import functools

import jax
import jax.numpy as jnp
from jax import lax
from jax.experimental import pallas as pl
from jax.experimental.pallas import tpu as pltpu
from jax.sharding import PartitionSpec as P

BLOCK = 128


def from_partner(block, axis, bit):
    count = lax.axis_size(axis)
    route = []
    for low in range(count):
        high = low | 1 << bit
        if high != low and high < count:
            route += [(low, high), (high, low)]
    return lax.ppermute(block, axis, route)


def dequantize(quant_vals, block_scale):
    row_count, col_count = quant_vals.shape
    blocked = quant_vals.reshape(row_count // BLOCK, BLOCK, col_count // BLOCK, BLOCK).astype(
        jnp.float32
    )
    scaled = blocked * block_scale[:, None, :, None]
    return scaled.reshape(row_count, col_count).astype(jnp.bfloat16)


def expert_ffn(inputs, w_gate, w_up, w_down):
    gate_part = jnp.dot(inputs, w_gate, preferred_element_type=jnp.float32)
    up_part = jnp.dot(inputs, w_up, preferred_element_type=jnp.float32)
    hidden = (jax.nn.silu(gate_part) * up_part).astype(jnp.bfloat16)
    return jnp.dot(hidden, w_down, preferred_element_type=jnp.float32)


def across_groups(blocks):
    return lax.all_to_all(blocks, "dp", split_axis=1, concat_axis=1, tiled=True)


def across_owners(blocks):
    return lax.all_to_all(blocks, "expert", split_axis=0, concat_axis=0, tiled=True)


def by_rows(tokens, expert_ids, gate_vals, gate_q, up_q, down_q, gate_scale, up_scale, down_scale):
    group_count = lax.axis_size("dp")
    owner_count = lax.axis_size("expert")
    token_count, model_width = tokens.shape
    top_count = expert_ids.shape[1]
    pair_count = owner_count // 2
    expert_count = group_count * pair_count
    capacity = 2 * token_count * top_count // expert_count
    half_cap = capacity // 2
    slot_count = owner_count * group_count * half_cap
    routes = expert_ids.reshape(-1)
    onehot = (routes[:, None] == jnp.arange(expert_count, dtype=jnp.int32)[None, :]).astype(
        jnp.int32
    )
    earlier = jnp.cumsum(onehot, axis=0) - onehot
    route_slot = jnp.sum(earlier * onehot, axis=1)
    route_group = routes // pair_count
    route_pair = routes % pair_count
    route_owner = 2 * route_pair + route_slot // half_cap
    route_place = route_slot % half_cap
    route_index = (route_owner * group_count + route_group) * half_cap + route_place
    chosen = jnp.arange(slot_count, dtype=jnp.int32)[:, None] == route_index[None, :]
    chosen = jnp.any(chosen.reshape(slot_count, token_count, top_count), axis=2).astype(
        jnp.bfloat16
    )
    outgoing = jnp.dot(chosen, tokens, preferred_element_type=jnp.float32).astype(jnp.bfloat16)
    outgoing = outgoing.reshape(owner_count, group_count, half_cap, model_width)
    arrived = across_owners(across_groups(outgoing))
    own_rows = arrived.reshape(-1, model_width)
    row_count = own_rows.shape[0]
    w_gate = dequantize(gate_q[0], gate_scale[0])
    w_up = dequantize(up_q[0], up_scale[0])
    w_down = dequantize(down_q[0], down_scale[0])
    partner_rows = from_partner(own_rows, "expert", 0)
    both_rows = jnp.concatenate([own_rows, partner_rows], axis=0)
    partial_value = expert_ffn(both_rows, w_gate, w_up, w_down)
    returned = from_partner(partial_value[row_count:], "expert", 0)
    expert_out = (partial_value[:row_count] + returned).astype(jnp.bfloat16)
    expert_out = expert_out.reshape(owner_count, group_count, half_cap, model_width)
    returned_rows = across_groups(across_owners(expert_out))
    returned_rows = returned_rows.reshape(slot_count, model_width)
    picked = returned_rows[route_index].reshape(token_count, top_count, model_width)
    weighted = jnp.einsum("tkd,tk->td", picked.astype(jnp.float32), gate_vals)
    mixed = tokens.astype(jnp.float32) + weighted
    return mixed.astype(jnp.bfloat16)


def added(block, arrived):
    return (block.astype(jnp.float32) + arrived.astype(jnp.float32)).astype(jnp.bfloat16)


def scaled(block, scale):
    return (block.astype(jnp.float32) * scale).astype(jnp.bfloat16)


def dequantize_kernel(gate_scales, up_scales, down_scales, gate, up, down, in_out, down_out, *scratch):
    gate_raw, up_raw, down_raw, in_sems, down_sems = scratch
    rows, cols = gate.shape
    chunks, down_chunks = in_sems.shape[1], down_sems.shape[0]
    depth, down_depth = rows // chunks, down.shape[0] // down_chunks

    def in_copy(part, chunk):
        source, target = ((gate, gate_raw), (up, up_raw))[part]
        at = pl.ds(pl.multiple_of(chunk * depth, depth), depth)
        return pltpu.make_async_copy(source.at[at], target.at[at], in_sems.at[part, chunk])

    def down_copy(chunk):
        at = pl.ds(pl.multiple_of(chunk * down_depth, down_depth), down_depth)
        return pltpu.make_async_copy(down.at[at], down_raw.at[at], down_sems.at[chunk])

    for chunk in range(chunks):
        for part in range(2):
            in_copy(part, chunk).start()
    for chunk in range(down_chunks):
        down_copy(chunk).start()

    @pl.loop(0, chunks)
    def _(chunk):
        in_copy(0, chunk).wait()
        in_copy(1, chunk).wait()
        for block in range(depth // BLOCK):
            row = chunk * (depth // BLOCK) + block
            at = pl.ds(pl.multiple_of(row * BLOCK, BLOCK), BLOCK)
            for col in range(cols // BLOCK):
                from_cols = slice(col * BLOCK, (col + 1) * BLOCK)
                to = 2 * col * BLOCK
                value = scaled(gate_raw[at, from_cols], gate_scales[col, row])
                in_out[at, to : to + BLOCK] = value
                to += BLOCK
                value = scaled(up_raw[at, from_cols], up_scales[col, row])
                in_out[at, to : to + BLOCK] = value

    @pl.loop(0, down_chunks)
    def _(chunk):
        down_copy(chunk).wait()
        for block in range(down_depth // BLOCK):
            row = chunk * (down_depth // BLOCK) + block
            at = pl.ds(pl.multiple_of(row * BLOCK, BLOCK), BLOCK)
            for col in range(down.shape[1] // BLOCK):
                cols_at = slice(col * BLOCK, (col + 1) * BLOCK)
                down_out[at, cols_at] = scaled(down_raw[at, cols_at], down_scales[row, col])


def dequantize_half(quants, scales):
    rows, cols = quants[0].shape
    chunks, down_chunks = max(1, rows // (4 * BLOCK)), max(1, cols // BLOCK)
    quants = [pltpu.with_memory_space_constraint(quant, pltpu.HBM) for quant in quants]
    whole = pl.BlockSpec(memory_space=pltpu.VMEM)
    return pl.pallas_call(
        dequantize_kernel,
        in_specs=[pl.BlockSpec(memory_space=pltpu.SMEM)] * 3 + [pl.BlockSpec(memory_space=pl.ANY)] * 3,
        out_specs=[whole] * 2,
        out_shape=[
            jax.ShapeDtypeStruct((rows, 2 * cols), jnp.bfloat16),
            jax.ShapeDtypeStruct(quants[2].shape, jnp.bfloat16),
        ],
        scratch_shapes=[
            *(pltpu.VMEM(quant.shape, jnp.bfloat16) for quant in quants),
            pltpu.SemaphoreType.DMA((2, chunks)),
            pltpu.SemaphoreType.DMA((down_chunks,)),
        ],
        cost_estimate=pl.CostEstimate(
            flops=3 * rows * cols, bytes_accessed=12 * rows * cols, transcendentals=0
        ),
        compiler_params=pltpu.CompilerParams(vmem_limit_bytes=24 * 1024 * 1024),
        name="dequantize_half",
    )(*scales, *quants)


def silu(v):
    return v / (1 + jnp.exp(-v))


def expert_kernel(count, experts, own_expert, *refs):
    pieces, refs = refs[:count], refs[count:]
    in_refs, down_refs, refs = refs[:2], refs[2:4], refs[4:]
    outs, (rows, hidden) = refs[:count], refs[count:]
    size, (half, model_width) = pieces[0].shape[0], down_refs[0].shape
    strip = min(4 * BLOCK, model_width)

    weights = []
    for place, piece in enumerate(pieces):
        rows[place * size : (place + 1) * size, :] = piece[:, :model_width]
        marks = piece[:, model_width:].astype(jnp.float32)
        column = lax.broadcasted_iota(jnp.int32, marks.shape, 1)
        chosen = (column == own_expert[0]) | (column == own_expert[0] + experts)
        weights.append(jnp.sum(jnp.where(chosen, marks, 0.0), axis=1, keepdims=True))
    for part, in_ref in enumerate(in_refs):
        for col in range(half // BLOCK):
            at = slice(2 * col * BLOCK, 2 * (col + 1) * BLOCK)
            both = jnp.dot(rows[...], in_ref[:, at], preferred_element_type=jnp.float32)
            value = (silu(both[:, :BLOCK]) * both[:, BLOCK:]).astype(jnp.bfloat16)
            to = part * half + col * BLOCK
            hidden[:, to : to + BLOCK] = value
    for first in range(0, model_width, strip):
        at = slice(first, first + strip)
        value = jnp.dot(hidden[:, :half], down_refs[0][:, at], preferred_element_type=jnp.float32)
        value += jnp.dot(hidden[:, half:], down_refs[1][:, at], preferred_element_type=jnp.float32)
        for place, out in enumerate(outs):
            weighted = value[place * size : (place + 1) * size] * weights[place]
            out[:, at] = weighted.astype(jnp.bfloat16)


def expert_layer(pieces, own_expert, experts, *weights):
    count, size = len(pieces), pieces[0].shape[0]
    model_width, width = weights[0].shape
    total = count * size
    whole = pl.BlockSpec(memory_space=pltpu.VMEM)
    weights = [pltpu.with_memory_space_constraint(weight, pltpu.VMEM) for weight in weights]
    return pl.pallas_call(
        functools.partial(expert_kernel, count, experts),
        in_specs=[pl.BlockSpec(memory_space=pltpu.SMEM)] + [whole] * (count + len(weights)),
        out_specs=[whole] * count,
        out_shape=[jax.ShapeDtypeStruct((size, model_width), jnp.bfloat16)] * count,
        scratch_shapes=[
            pltpu.VMEM((total, model_width), jnp.bfloat16),
            pltpu.VMEM((total, width), jnp.bfloat16),
        ],
        cost_estimate=pl.CostEstimate(
            flops=6 * total * model_width * width,
            bytes_accessed=6 * model_width * width + 4 * total * model_width,
            transcendentals=total * width,
        ),
        compiler_params=pltpu.CompilerParams(vmem_limit_bytes=16 * 1024 * 1024),
        name="expert_layer",
    )(own_expert, *pieces, *weights)


def across_chips(block, far):
    count = lax.axis_size("expert")
    return lax.ppermute(block, "expert", [(low, low ^ 2 * far) for low in range(count)])


def by_sums(tokens, expert_ids, gate_vals, gate_q, up_q, down_q, gate_scale, up_scale, down_scale):
    token_count, model_width = tokens.shape
    group_count = lax.axis_size("dp")
    pair_count = lax.axis_size("expert") // 2
    expert_count = group_count * pair_count
    own_expert = lax.axis_index("dp") * pair_count + lax.axis_index("expert") // 2
    bits = list(range(group_count.bit_length() - 1))
    orders = (bits, bits[::-1])

    named = expert_ids[:, :, None] == jnp.arange(expert_count, dtype=jnp.int32)[None, None, :]
    weight = jnp.sum(jnp.where(named, gate_vals[:, :, None], 0.0), axis=1)
    high = weight.astype(jnp.bfloat16)
    low = (weight - high.astype(jnp.float32)).astype(jnp.bfloat16)
    extra = -(-2 * expert_count // BLOCK) * BLOCK
    pad = jnp.zeros((token_count, extra - 2 * expert_count), jnp.bfloat16)
    half = token_count // 2
    halves = [slice(0, half), slice(half, token_count)]
    payload = [
        jnp.concatenate([part[rows] for part in (tokens, high, low, pad)], axis=1)
        for rows in halves
    ]

    together = lax.optimization_barrier
    place = jnp.reshape(own_expert, (1,)).astype(jnp.int32)
    turns = len(bits)
    groups = [(0,), *((far, far + 1) for far in range(1, pair_count - 1, 2)), (pair_count - 1,)]

    def lanes_of(group):
        if len(group) == 2:
            return [came[far] for far in group]
        return [came[group[0]][:half], came[group[0]][half:]]

    def along_z(far):
        low = far & -far
        came[far] = across_chips(came[far ^ low], low)

    def gather_turn(number, turn):
        blocks = lanes[number]
        arrived = [from_partner(block, "dp", orders[lane][turn]) for lane, block in enumerate(blocks)]
        if turn == turns - 1:
            lanes[number] = [part for pair in zip(blocks, arrived) for part in pair]
        else:
            lanes[number] = [jnp.concatenate(pair, axis=0) for pair in zip(blocks, arrived)]

    def layer(number):
        return expert_layer(lanes[number], place, expert_count, *weights)

    place, payload = together((place, payload))
    lanes, outs = {0: payload}, {}
    near = [{far: across_chips(payload[0], far) for far in groups[1]}]
    gather_turn(0, 0)
    in_own, down_own = dequantize_half(
        (gate_q[0], up_q[0], down_q[0]), (gate_scale[0].T, up_scale[0].T, down_scale[0])
    )
    lanes, near, payload, in_own, down_own = together((lanes, near, payload, in_own, down_own))
    in_other = from_partner(in_own, "expert", 0)
    near.append({far: across_chips(payload[1], far) for far in groups[1]})
    for turn in range(1, turns):
        gather_turn(0, turn)
    lanes, near, down_own = together((lanes, near, down_own))
    came = {far: jnp.concatenate([part[far] for part in near], axis=0) for far in groups[1]}
    down_other = from_partner(down_own, "expert", 0)
    lanes[1] = lanes_of(groups[1])
    for number in range(1, len(groups)):
        following = groups[number + 1] if number + 1 < len(groups) else ()
        for turn in range(int(number > 1), turns - 1):
            gather_turn(number, turn)
            if turn == int(number > 1):
                for far in following:
                    along_z(far)
            tied = (lanes, came, outs, in_other, down_other)
            lanes, came, outs, in_other, down_other = together(tied)
        weights = (in_own, in_other, down_own, down_other)
        gather_turn(number, turns - 1)
        if following:
            if turns - 1 == int(number > 1):
                for far in following:
                    along_z(far)
            lanes[number + 1] = lanes_of(following)
            gather_turn(number + 1, 0)
        if number + 1 == len(groups):
            break
        outs[number - 1] = layer(number - 1)
        if number + 2 != len(groups):
            lanes, outs, came = together((lanes, outs, came))
    final = len(groups) - 1
    sums, merged, parts = {}, {}, []

    def sum_turn(number, turn):
        result = []
        for lane in range(2):
            if turn == turns - 1:
                kept, sent = outs[number][2 * lane : 2 * lane + 2]
            else:
                kept, sent = jnp.split(sums[number][lane], 2, axis=0)
            result.append(added(kept, from_partner(sent, "dp", orders[lane][turn])))
        sums[number] = result

    def leave(number):
        group, done = groups[number], sums.pop(number)
        done = done if len(group) == 2 else [jnp.concatenate(done, axis=0)]
        ready = dict(zip(group, done))
        for far in reversed(group):
            block, low = ready[far], far & -far
            if far in merged:
                block = added(block, merged.pop(far))
            if far != low:
                came_back = across_chips(block, low)
                into = far ^ low
                merged[into] = added(merged[into], came_back) if into in merged else came_back
            else:
                whole = across_chips(block, low)
                parts.append([whole[rows] for rows in halves])

    lanes, outs = together((lanes, outs))
    sum_turn(0, turns - 1)
    outs[final - 1] = layer(final - 1)
    lanes, outs, sums = together((lanes, outs, sums))
    outs[final] = layer(final)
    for number in range(final, 0, -1):
        for turn in range(turns - 1 - int(number < final), -1, -1):
            sum_turn(number, turn)
            if turn == 0 and number > 1:
                sum_turn(number - 1, turns - 1)
        if number > 1:
            leave(number)
        sums, outs = together((sums, outs))
    leave(1)
    for turn in range(turns - 2, -1, -1):
        sum_turn(0, turn)
    result = []
    for lane, rows in enumerate(halves):
        total = tokens[rows].astype(jnp.float32) + sums[0][lane].astype(jnp.float32)
        for part in parts:
            total = total + part[lane].astype(jnp.float32)
        result.append(total.astype(jnp.bfloat16))
    return jnp.concatenate(result, axis=0)


def shards(tokens, expert_ids, *weights):
    expert_count = lax.axis_size("dp") * lax.axis_size("expert") // 2
    token_count, top_count = expert_ids.shape
    capacity = 2 * token_count * top_count // expert_count
    group_count, pair_count = lax.axis_size("dp"), lax.axis_size("expert") // 2
    powers = all(count & (count - 1) == 0 for count in (group_count, pair_count))
    dense = capacity >= token_count and powers and min(group_count, pair_count) >= 4
    plan = by_sums if dense else by_rows
    return plan(tokens, expert_ids, *weights)


def solution(mesh):
    return jax.shard_map(
        shards,
        mesh=mesh,
        in_specs=(
            P(("dp", "expert"), None),
            P(("dp", "expert"), None),
            P(("dp", "expert"), None),
            P("dp", None, "expert"),
            P("dp", None, "expert"),
            P("dp", "expert", None),
            P("dp", None, "expert"),
            P("dp", None, "expert"),
            P("dp", "expert", None),
        ),
        out_specs=P(("dp", "expert"), None),
        check_vma=False,
    )
```

```python
import functools

import jax
import jax.numpy as jnp
from jax import lax
from jax.experimental import pallas as pl
from jax.experimental.pallas import tpu as pltpu
from jax.sharding import PartitionSpec as P

BLOCK = 128


def from_partner(block, axis, bit):
    count = lax.axis_size(axis)
    route = []
    for low in range(count):
        high = low | 1 << bit
        if high != low and high < count:
            route += [(low, high), (high, low)]
    return lax.ppermute(block, axis, route)


def dequantize(quant_vals, block_scale):
    row_count, col_count = quant_vals.shape
    blocked = quant_vals.reshape(row_count // BLOCK, BLOCK, col_count // BLOCK, BLOCK).astype(
        jnp.float32
    )
    scaled = blocked * block_scale[:, None, :, None]
    return scaled.reshape(row_count, col_count).astype(jnp.bfloat16)


def expert_ffn(inputs, w_gate, w_up, w_down):
    gate_part = jnp.dot(inputs, w_gate, preferred_element_type=jnp.float32)
    up_part = jnp.dot(inputs, w_up, preferred_element_type=jnp.float32)
    hidden = (jax.nn.silu(gate_part) * up_part).astype(jnp.bfloat16)
    return jnp.dot(hidden, w_down, preferred_element_type=jnp.float32)


def across_groups(blocks):
    return lax.all_to_all(blocks, "dp", split_axis=1, concat_axis=1, tiled=True)


def across_owners(blocks):
    return lax.all_to_all(blocks, "expert", split_axis=0, concat_axis=0, tiled=True)


def by_rows(tokens, expert_ids, gate_vals, gate_q, up_q, down_q, gate_scale, up_scale, down_scale):
    group_count = lax.axis_size("dp")
    owner_count = lax.axis_size("expert")
    token_count, model_width = tokens.shape
    top_count = expert_ids.shape[1]
    pair_count = owner_count // 2
    expert_count = group_count * pair_count
    capacity = 2 * token_count * top_count // expert_count
    half_cap = capacity // 2
    slot_count = owner_count * group_count * half_cap
    routes = expert_ids.reshape(-1)
    onehot = (routes[:, None] == jnp.arange(expert_count, dtype=jnp.int32)[None, :]).astype(
        jnp.int32
    )
    earlier = jnp.cumsum(onehot, axis=0) - onehot
    route_slot = jnp.sum(earlier * onehot, axis=1)
    route_group = routes // pair_count
    route_pair = routes % pair_count
    route_owner = 2 * route_pair + route_slot // half_cap
    route_place = route_slot % half_cap
    route_index = (route_owner * group_count + route_group) * half_cap + route_place
    chosen = jnp.arange(slot_count, dtype=jnp.int32)[:, None] == route_index[None, :]
    chosen = jnp.any(chosen.reshape(slot_count, token_count, top_count), axis=2).astype(
        jnp.bfloat16
    )
    outgoing = jnp.dot(chosen, tokens, preferred_element_type=jnp.float32).astype(jnp.bfloat16)
    outgoing = outgoing.reshape(owner_count, group_count, half_cap, model_width)
    arrived = across_owners(across_groups(outgoing))
    own_rows = arrived.reshape(-1, model_width)
    row_count = own_rows.shape[0]
    w_gate = dequantize(gate_q[0], gate_scale[0])
    w_up = dequantize(up_q[0], up_scale[0])
    w_down = dequantize(down_q[0], down_scale[0])
    partner_rows = from_partner(own_rows, "expert", 0)
    both_rows = jnp.concatenate([own_rows, partner_rows], axis=0)
    partial_value = expert_ffn(both_rows, w_gate, w_up, w_down)
    returned = from_partner(partial_value[row_count:], "expert", 0)
    expert_out = (partial_value[:row_count] + returned).astype(jnp.bfloat16)
    expert_out = expert_out.reshape(owner_count, group_count, half_cap, model_width)
    returned_rows = across_groups(across_owners(expert_out))
    returned_rows = returned_rows.reshape(slot_count, model_width)
    picked = returned_rows[route_index].reshape(token_count, top_count, model_width)
    weighted = jnp.einsum("tkd,tk->td", picked.astype(jnp.float32), gate_vals)
    mixed = tokens.astype(jnp.float32) + weighted
    return mixed.astype(jnp.bfloat16)


def added(block, arrived):
    return (block.astype(jnp.float32) + arrived.astype(jnp.float32)).astype(jnp.bfloat16)


def scaled(block, scale):
    return (block.astype(jnp.float32) * scale).astype(jnp.bfloat16)


def chunk_copies(sources, targets, sems):
    chunks = sems.shape[1]
    depth = sources[0].shape[0] // chunks

    def copy(part, chunk):
        at = pl.ds(pl.multiple_of(chunk * depth, depth), depth)
        return pltpu.make_async_copy(sources[part].at[at], targets[part].at[at], sems.at[part, chunk])

    for chunk in range(chunks):
        for part in range(len(sources)):
            copy(part, chunk).start()
    return copy


def in_kernel(gate_scales, up_scales, gate, up, out, gate_raw, up_raw, sems):
    rows, cols = gate.shape
    chunks = sems.shape[1]
    strip = rows // chunks // BLOCK
    copy = chunk_copies((gate, up), (gate_raw, up_raw), sems)

    @pl.loop(0, chunks)
    def _(chunk):
        copy(0, chunk).wait()
        copy(1, chunk).wait()
        for block in range(strip):
            row = chunk * strip + block
            at = pl.ds(pl.multiple_of(row * BLOCK, BLOCK), BLOCK)
            for col in range(cols // BLOCK):
                source, to = slice(col * BLOCK, (col + 1) * BLOCK), 2 * col * BLOCK
                out[at, to : to + BLOCK] = scaled(gate_raw[at, source], gate_scales[col, row])
                to += BLOCK
                out[at, to : to + BLOCK] = scaled(up_raw[at, source], up_scales[col, row])


def down_kernel(scales, down, out, raw, sems):
    chunks = sems.shape[1]
    strip = down.shape[0] // chunks // BLOCK
    copy = chunk_copies((down,), (raw,), sems)

    @pl.loop(0, chunks)
    def _(chunk):
        copy(0, chunk).wait()
        for block in range(strip):
            row = chunk * strip + block
            at = pl.ds(pl.multiple_of(row * BLOCK, BLOCK), BLOCK)
            for col in range(down.shape[1] // BLOCK):
                cols = slice(col * BLOCK, (col + 1) * BLOCK)
                out[at, cols] = scaled(raw[at, cols], scales[row, col])


def dequantize_call(kernel, name, quants, scales, width, chunks):
    rows, cols = quants[0].shape
    quants = [pltpu.with_memory_space_constraint(quant, pltpu.HBM) for quant in quants]
    return pl.pallas_call(
        kernel,
        in_specs=[pl.BlockSpec(memory_space=pltpu.SMEM)] * len(scales)
        + [pl.BlockSpec(memory_space=pl.ANY)] * len(quants),
        out_specs=pl.BlockSpec(memory_space=pltpu.VMEM),
        out_shape=jax.ShapeDtypeStruct((rows, width), jnp.bfloat16),
        scratch_shapes=[
            *(pltpu.VMEM(quant.shape, jnp.bfloat16) for quant in quants),
            pltpu.SemaphoreType.DMA((len(quants), chunks)),
        ],
        cost_estimate=pl.CostEstimate(
            flops=rows * width, bytes_accessed=4 * rows * width, transcendentals=0
        ),
        compiler_params=pltpu.CompilerParams(vmem_limit_bytes=16 * 1024 * 1024),
        name=name,
    )(*scales, *quants)


def dequantize_in(gate, up, gate_scales, up_scales):
    rows, cols = gate.shape
    chunks = max(1, rows // (4 * BLOCK))
    scales = (gate_scales, up_scales)
    return dequantize_call(in_kernel, "dequantize_in", (gate, up), scales, 2 * cols, chunks)


def dequantize_down(down, scales):
    rows, cols = down.shape
    return dequantize_call(down_kernel, "dequantize_down", (down,), (scales,), cols, rows // BLOCK)


def silu(v):
    return v / (1 + jnp.exp(-v))


def expert_kernel(count, experts, own_expert, *refs):
    pieces, refs = refs[:count], refs[count:]
    in_refs, down_refs, refs = refs[:2], refs[2:4], refs[4:]
    outs, (rows, hidden) = refs[:count], refs[count:]
    size, (half, model_width) = pieces[0].shape[0], down_refs[0].shape
    strip = min(4 * BLOCK, model_width)

    weights = []
    for place, piece in enumerate(pieces):
        rows[place * size : (place + 1) * size, :] = piece[:, :model_width]
        marks = piece[:, model_width:].astype(jnp.float32)
        column = lax.broadcasted_iota(jnp.int32, marks.shape, 1)
        chosen = (column == own_expert[0]) | (column == own_expert[0] + experts)
        weights.append(jnp.sum(jnp.where(chosen, marks, 0.0), axis=1, keepdims=True))
    for part, in_ref in enumerate(in_refs):
        for col in range(half // BLOCK):
            at = slice(2 * col * BLOCK, 2 * (col + 1) * BLOCK)
            both = jnp.dot(rows[...], in_ref[:, at], preferred_element_type=jnp.float32)
            value = (silu(both[:, :BLOCK]) * both[:, BLOCK:]).astype(jnp.bfloat16)
            to = part * half + col * BLOCK
            hidden[:, to : to + BLOCK] = value
    for first in range(0, model_width, strip):
        at = slice(first, first + strip)
        value = jnp.dot(hidden[:, :half], down_refs[0][:, at], preferred_element_type=jnp.float32)
        value += jnp.dot(hidden[:, half:], down_refs[1][:, at], preferred_element_type=jnp.float32)
        for place, out in enumerate(outs):
            weighted = value[place * size : (place + 1) * size] * weights[place]
            out[:, at] = weighted.astype(jnp.bfloat16)


def expert_layer(pieces, own_expert, experts, *weights):
    count, size = len(pieces), pieces[0].shape[0]
    model_width, width = weights[0].shape
    total = count * size
    whole = pl.BlockSpec(memory_space=pltpu.VMEM)
    weights = [pltpu.with_memory_space_constraint(weight, pltpu.VMEM) for weight in weights]
    return pl.pallas_call(
        functools.partial(expert_kernel, count, experts),
        in_specs=[pl.BlockSpec(memory_space=pltpu.SMEM)] + [whole] * (count + len(weights)),
        out_specs=[whole] * count,
        out_shape=[jax.ShapeDtypeStruct((size, model_width), jnp.bfloat16)] * count,
        scratch_shapes=[
            pltpu.VMEM((total, model_width), jnp.bfloat16),
            pltpu.VMEM((total, width), jnp.bfloat16),
        ],
        cost_estimate=pl.CostEstimate(
            flops=6 * total * model_width * width,
            bytes_accessed=6 * model_width * width + 4 * total * model_width,
            transcendentals=total * width,
        ),
        compiler_params=pltpu.CompilerParams(vmem_limit_bytes=16 * 1024 * 1024),
        name="expert_layer",
    )(own_expert, *pieces, *weights)


def across_chips(block, far):
    count = lax.axis_size("expert")
    return lax.ppermute(block, "expert", [(low, low ^ 2 * far) for low in range(count)])


def by_sums(tokens, expert_ids, gate_vals, gate_q, up_q, down_q, gate_scale, up_scale, down_scale):
    token_count, model_width = tokens.shape
    group_count = lax.axis_size("dp")
    pair_count = lax.axis_size("expert") // 2
    expert_count = group_count * pair_count
    own_expert = lax.axis_index("dp") * pair_count + lax.axis_index("expert") // 2
    bits = list(range(group_count.bit_length() - 1))
    orders = (bits, bits[::-1])

    named = expert_ids[:, :, None] == jnp.arange(expert_count, dtype=jnp.int32)[None, None, :]
    weight = jnp.sum(jnp.where(named, gate_vals[:, :, None], 0.0), axis=1)
    high = weight.astype(jnp.bfloat16)
    low = (weight - high.astype(jnp.float32)).astype(jnp.bfloat16)
    extra = -(-2 * expert_count // BLOCK) * BLOCK
    pad = jnp.zeros((token_count, extra - 2 * expert_count), jnp.bfloat16)
    half = token_count // 2
    halves = [slice(0, half), slice(half, token_count)]
    payload = [
        jnp.concatenate([part[rows] for part in (tokens, high, low, pad)], axis=1)
        for rows in halves
    ]

    together = lax.optimization_barrier
    place = jnp.reshape(own_expert, (1,)).astype(jnp.int32)
    turns = len(bits)
    groups = [(0,), *((far, far + 1) for far in range(1, pair_count - 1, 2)), (pair_count - 1,)]

    def lanes_of(group):
        if len(group) == 2:
            return [came[far] for far in group]
        return [came[group[0]][:half], came[group[0]][half:]]

    def along_z(far):
        low = far & -far
        came[far] = across_chips(came[far ^ low], low)

    def gather_turn(number, turn):
        blocks = lanes[number]
        arrived = [from_partner(block, "dp", orders[lane][turn]) for lane, block in enumerate(blocks)]
        if turn == turns - 1:
            lanes[number] = [part for pair in zip(blocks, arrived) for part in pair]
        else:
            lanes[number] = [jnp.concatenate(pair, axis=0) for pair in zip(blocks, arrived)]

    def layer(number):
        return expert_layer(lanes[number], place, expert_count, *weights)

    place, payload = together((place, payload))
    lanes, outs = {0: payload}, {}
    near = [{far: across_chips(payload[0], far) for far in groups[1]}]
    gather_turn(0, 0)
    in_own = dequantize_in(gate_q[0], up_q[0], gate_scale[0].T, up_scale[0].T)
    lanes, near, payload, in_own, down_own = together((lanes, near, payload, in_own, down_q[0]))
    in_other = from_partner(in_own, "expert", 0)
    down_own = dequantize_down(down_own, down_scale[0])
    near.append({far: across_chips(payload[1], far) for far in groups[1]})
    for turn in range(1, turns):
        gather_turn(0, turn)
    lanes, near, down_own = together((lanes, near, down_own))
    came = {far: jnp.concatenate([part[far] for part in near], axis=0) for far in groups[1]}
    down_other = from_partner(down_own, "expert", 0)
    lanes[1] = lanes_of(groups[1])
    for number in range(1, len(groups)):
        following = groups[number + 1] if number + 1 < len(groups) else ()
        for turn in range(int(number > 1), turns - 1):
            gather_turn(number, turn)
            if turn == int(number > 1):
                for far in following:
                    along_z(far)
            tied = (lanes, came, outs, in_other, down_other)
            lanes, came, outs, in_other, down_other = together(tied)
        weights = (in_own, in_other, down_own, down_other)
        gather_turn(number, turns - 1)
        if following:
            if turns - 1 == int(number > 1):
                for far in following:
                    along_z(far)
            lanes[number + 1] = lanes_of(following)
            gather_turn(number + 1, 0)
        if number + 1 == len(groups):
            break
        outs[number - 1] = layer(number - 1)
        if number + 2 != len(groups):
            lanes, outs, came = together((lanes, outs, came))
    final = len(groups) - 1
    sums, merged, parts = {}, {}, []

    def sum_turn(number, turn):
        result = []
        for lane in range(2):
            if turn == turns - 1:
                kept, sent = outs[number][2 * lane : 2 * lane + 2]
            else:
                kept, sent = jnp.split(sums[number][lane], 2, axis=0)
            result.append(added(kept, from_partner(sent, "dp", orders[lane][turn])))
        sums[number] = result

    def leave(number):
        group, done = groups[number], sums.pop(number)
        done = done if len(group) == 2 else [jnp.concatenate(done, axis=0)]
        ready = dict(zip(group, done))
        for far in reversed(group):
            block, low = ready[far], far & -far
            if far in merged:
                block = added(block, merged.pop(far))
            if far != low:
                came_back = across_chips(block, low)
                into = far ^ low
                merged[into] = added(merged[into], came_back) if into in merged else came_back
            else:
                whole = across_chips(block, low)
                parts.append([whole[rows] for rows in halves])

    lanes[final - 1], outs = together((lanes[final - 1], outs))
    sum_turn(0, turns - 1)
    outs[final - 1] = layer(final - 1)
    lanes, outs, sums = together((lanes, outs, sums))
    outs[final] = layer(final)
    for number in range(final, 0, -1):
        for turn in range(turns - 1 - int(number < final), -1, -1):
            sum_turn(number, turn)
            if turn == 0 and number > 1:
                sum_turn(number - 1, turns - 1)
        if number > 1:
            leave(number)
        sums, outs = together((sums, outs))
    leave(1)
    for turn in range(turns - 2, -1, -1):
        sum_turn(0, turn)
    result = []
    for lane, rows in enumerate(halves):
        total = tokens[rows].astype(jnp.float32) + sums[0][lane].astype(jnp.float32)
        for part in parts:
            total = total + part[lane].astype(jnp.float32)
        result.append(total.astype(jnp.bfloat16))
    return jnp.concatenate(result, axis=0)


def shards(tokens, expert_ids, *weights):
    expert_count = lax.axis_size("dp") * lax.axis_size("expert") // 2
    token_count, top_count = expert_ids.shape
    capacity = 2 * token_count * top_count // expert_count
    group_count, pair_count = lax.axis_size("dp"), lax.axis_size("expert") // 2
    powers = all(count & (count - 1) == 0 for count in (group_count, pair_count))
    dense = capacity >= token_count and powers and min(group_count, pair_count) >= 4
    plan = by_sums if dense else by_rows
    return plan(tokens, expert_ids, *weights)


def solution(mesh):
    return jax.shard_map(
        shards,
        mesh=mesh,
        in_specs=(
            P(("dp", "expert"), None),
            P(("dp", "expert"), None),
            P(("dp", "expert"), None),
            P("dp", None, "expert"),
            P("dp", None, "expert"),
            P("dp", "expert", None),
            P("dp", None, "expert"),
            P("dp", None, "expert"),
            P("dp", "expert", None),
        ),
        out_specs=P(("dp", "expert"), None),
        check_vma=False,
    )
```

```python
import functools

import jax
import jax.numpy as jnp
from jax import lax
from jax.experimental import pallas as pl
from jax.experimental.pallas import tpu as pltpu
from jax.sharding import PartitionSpec as P

BLOCK = 128


def from_partner(block, axis, bit):
    count = lax.axis_size(axis)
    route = []
    for low in range(count):
        high = low | 1 << bit
        if high != low and high < count:
            route += [(low, high), (high, low)]
    return lax.ppermute(block, axis, route)


def dequantize(quant_vals, block_scale):
    row_count, col_count = quant_vals.shape
    blocked = quant_vals.reshape(row_count // BLOCK, BLOCK, col_count // BLOCK, BLOCK).astype(
        jnp.float32
    )
    scaled = blocked * block_scale[:, None, :, None]
    return scaled.reshape(row_count, col_count).astype(jnp.bfloat16)


def expert_ffn(inputs, w_gate, w_up, w_down):
    gate_part = jnp.dot(inputs, w_gate, preferred_element_type=jnp.float32)
    up_part = jnp.dot(inputs, w_up, preferred_element_type=jnp.float32)
    hidden = (jax.nn.silu(gate_part) * up_part).astype(jnp.bfloat16)
    return jnp.dot(hidden, w_down, preferred_element_type=jnp.float32)


def across_groups(blocks):
    return lax.all_to_all(blocks, "dp", split_axis=1, concat_axis=1, tiled=True)


def across_owners(blocks):
    return lax.all_to_all(blocks, "expert", split_axis=0, concat_axis=0, tiled=True)


def by_rows(tokens, expert_ids, gate_vals, gate_q, up_q, down_q, gate_scale, up_scale, down_scale):
    group_count = lax.axis_size("dp")
    owner_count = lax.axis_size("expert")
    token_count, model_width = tokens.shape
    top_count = expert_ids.shape[1]
    pair_count = owner_count // 2
    expert_count = group_count * pair_count
    capacity = 2 * token_count * top_count // expert_count
    half_cap = capacity // 2
    slot_count = owner_count * group_count * half_cap
    routes = expert_ids.reshape(-1)
    onehot = (routes[:, None] == jnp.arange(expert_count, dtype=jnp.int32)[None, :]).astype(
        jnp.int32
    )
    earlier = jnp.cumsum(onehot, axis=0) - onehot
    route_slot = jnp.sum(earlier * onehot, axis=1)
    route_group = routes // pair_count
    route_pair = routes % pair_count
    route_owner = 2 * route_pair + route_slot // half_cap
    route_place = route_slot % half_cap
    route_index = (route_owner * group_count + route_group) * half_cap + route_place
    chosen = jnp.arange(slot_count, dtype=jnp.int32)[:, None] == route_index[None, :]
    chosen = jnp.any(chosen.reshape(slot_count, token_count, top_count), axis=2).astype(
        jnp.bfloat16
    )
    outgoing = jnp.dot(chosen, tokens, preferred_element_type=jnp.float32).astype(jnp.bfloat16)
    outgoing = outgoing.reshape(owner_count, group_count, half_cap, model_width)
    arrived = across_owners(across_groups(outgoing))
    own_rows = arrived.reshape(-1, model_width)
    row_count = own_rows.shape[0]
    w_gate = dequantize(gate_q[0], gate_scale[0])
    w_up = dequantize(up_q[0], up_scale[0])
    w_down = dequantize(down_q[0], down_scale[0])
    partner_rows = from_partner(own_rows, "expert", 0)
    both_rows = jnp.concatenate([own_rows, partner_rows], axis=0)
    partial_value = expert_ffn(both_rows, w_gate, w_up, w_down)
    returned = from_partner(partial_value[row_count:], "expert", 0)
    expert_out = (partial_value[:row_count] + returned).astype(jnp.bfloat16)
    expert_out = expert_out.reshape(owner_count, group_count, half_cap, model_width)
    returned_rows = across_groups(across_owners(expert_out))
    returned_rows = returned_rows.reshape(slot_count, model_width)
    picked = returned_rows[route_index].reshape(token_count, top_count, model_width)
    weighted = jnp.einsum("tkd,tk->td", picked.astype(jnp.float32), gate_vals)
    mixed = tokens.astype(jnp.float32) + weighted
    return mixed.astype(jnp.bfloat16)


def added(block, arrived):
    return (block.astype(jnp.float32) + arrived.astype(jnp.float32)).astype(jnp.bfloat16)


def scaled(block, scale):
    return (block.astype(jnp.float32) * scale).astype(jnp.bfloat16)


def chunk_copies(sources, targets, sems):
    chunks = sems.shape[1]
    depth = sources[0].shape[0] // chunks

    def copy(part, chunk):
        at = pl.ds(pl.multiple_of(chunk * depth, depth), depth)
        return pltpu.make_async_copy(sources[part].at[at], targets[part].at[at], sems.at[part, chunk])

    for chunk in range(chunks):
        for part in range(len(sources)):
            copy(part, chunk).start()
    return copy


def in_kernel(gate_scales, up_scales, gate, up, out, gate_raw, up_raw, sems):
    rows, cols = gate.shape
    chunks = sems.shape[1]
    strip = rows // chunks // BLOCK
    copy = chunk_copies((gate, up), (gate_raw, up_raw), sems)

    @pl.loop(0, chunks)
    def _(chunk):
        copy(0, chunk).wait()
        copy(1, chunk).wait()
        for block in range(strip):
            row = chunk * strip + block
            at = pl.ds(pl.multiple_of(row * BLOCK, BLOCK), BLOCK)
            for col in range(cols // BLOCK):
                source, to = slice(col * BLOCK, (col + 1) * BLOCK), 2 * col * BLOCK
                out[at, to : to + BLOCK] = scaled(gate_raw[at, source], gate_scales[col, row])
                to += BLOCK
                out[at, to : to + BLOCK] = scaled(up_raw[at, source], up_scales[col, row])


def down_kernel(scales, down, out, raw, sems):
    chunks = sems.shape[1]
    strip = down.shape[0] // chunks // BLOCK
    copy = chunk_copies((down,), (raw,), sems)

    @pl.loop(0, chunks)
    def _(chunk):
        copy(0, chunk).wait()
        for block in range(strip):
            row = chunk * strip + block
            at = pl.ds(pl.multiple_of(row * BLOCK, BLOCK), BLOCK)
            for col in range(down.shape[1] // BLOCK):
                cols = slice(col * BLOCK, (col + 1) * BLOCK)
                out[at, cols] = scaled(raw[at, cols], scales[row, col])


def dequantize_call(kernel, name, quants, scales, width, chunks):
    rows, cols = quants[0].shape
    quants = [pltpu.with_memory_space_constraint(quant, pltpu.HBM) for quant in quants]
    return pl.pallas_call(
        kernel,
        in_specs=[pl.BlockSpec(memory_space=pltpu.SMEM)] * len(scales)
        + [pl.BlockSpec(memory_space=pl.ANY)] * len(quants),
        out_specs=pl.BlockSpec(memory_space=pltpu.VMEM),
        out_shape=jax.ShapeDtypeStruct((rows, width), jnp.bfloat16),
        scratch_shapes=[
            *(pltpu.VMEM(quant.shape, jnp.bfloat16) for quant in quants),
            pltpu.SemaphoreType.DMA((len(quants), chunks)),
        ],
        cost_estimate=pl.CostEstimate(
            flops=rows * width, bytes_accessed=4 * rows * width, transcendentals=0
        ),
        compiler_params=pltpu.CompilerParams(vmem_limit_bytes=16 * 1024 * 1024),
        name=name,
    )(*scales, *quants)


def dequantize_in(gate, up, gate_scales, up_scales):
    rows, cols = gate.shape
    chunks = max(1, rows // (4 * BLOCK))
    scales = (gate_scales, up_scales)
    return dequantize_call(in_kernel, "dequantize_in", (gate, up), scales, 2 * cols, chunks)


def dequantize_down(down, scales):
    rows, cols = down.shape
    return dequantize_call(down_kernel, "dequantize_down", (down,), (scales,), cols, rows // BLOCK)


def silu(v):
    return v / (1 + jnp.exp(-v))


def expert_kernel(count, experts, own_expert, *refs):
    pieces, refs = refs[:count], refs[count:]
    in_refs, down_refs, refs = refs[:2], refs[2:4], refs[4:]
    outs, (rows, hidden) = refs[:count], refs[count:]
    size, (half, model_width) = pieces[0].shape[0], down_refs[0].shape
    strip = min(4 * BLOCK, model_width)

    weights = []
    for place, piece in enumerate(pieces):
        rows[place * size : (place + 1) * size, :] = piece[:, :model_width]
        marks = piece[:, model_width:].astype(jnp.float32)
        column = lax.broadcasted_iota(jnp.int32, marks.shape, 1)
        chosen = (column == own_expert[0]) | (column == own_expert[0] + experts)
        weights.append(jnp.sum(jnp.where(chosen, marks, 0.0), axis=1, keepdims=True))
    for part, in_ref in enumerate(in_refs):
        for col in range(half // BLOCK):
            at = slice(2 * col * BLOCK, 2 * (col + 1) * BLOCK)
            both = jnp.dot(rows[...], in_ref[:, at], preferred_element_type=jnp.float32)
            value = (silu(both[:, :BLOCK]) * both[:, BLOCK:]).astype(jnp.bfloat16)
            to = part * half + col * BLOCK
            hidden[:, to : to + BLOCK] = value
    for first in range(0, model_width, strip):
        at = slice(first, first + strip)
        value = jnp.dot(hidden[:, :half], down_refs[0][:, at], preferred_element_type=jnp.float32)
        value += jnp.dot(hidden[:, half:], down_refs[1][:, at], preferred_element_type=jnp.float32)
        for place, out in enumerate(outs):
            weighted = value[place * size : (place + 1) * size] * weights[place]
            out[:, at] = weighted.astype(jnp.bfloat16)


def expert_layer(pieces, own_expert, experts, *weights):
    count, size = len(pieces), pieces[0].shape[0]
    model_width, width = weights[0].shape
    total = count * size
    whole = pl.BlockSpec(memory_space=pltpu.VMEM)
    weights = [pltpu.with_memory_space_constraint(weight, pltpu.VMEM) for weight in weights]
    return pl.pallas_call(
        functools.partial(expert_kernel, count, experts),
        in_specs=[pl.BlockSpec(memory_space=pltpu.SMEM)] + [whole] * (count + len(weights)),
        out_specs=[whole] * count,
        out_shape=[jax.ShapeDtypeStruct((size, model_width), jnp.bfloat16)] * count,
        scratch_shapes=[
            pltpu.VMEM((total, model_width), jnp.bfloat16),
            pltpu.VMEM((total, width), jnp.bfloat16),
        ],
        cost_estimate=pl.CostEstimate(
            flops=6 * total * model_width * width,
            bytes_accessed=6 * model_width * width + 4 * total * model_width,
            transcendentals=total * width,
        ),
        compiler_params=pltpu.CompilerParams(vmem_limit_bytes=16 * 1024 * 1024),
        name="expert_layer",
    )(own_expert, *pieces, *weights)


def across_chips(block, far):
    count = lax.axis_size("expert")
    return lax.ppermute(block, "expert", [(low, low ^ 2 * far) for low in range(count)])


def by_sums(tokens, expert_ids, gate_vals, gate_q, up_q, down_q, gate_scale, up_scale, down_scale):
    token_count, model_width = tokens.shape
    group_count = lax.axis_size("dp")
    pair_count = lax.axis_size("expert") // 2
    expert_count = group_count * pair_count
    own_expert = lax.axis_index("dp") * pair_count + lax.axis_index("expert") // 2
    bits = list(range(group_count.bit_length() - 1))
    orders = (bits, bits[::-1])

    named = expert_ids[:, :, None] == jnp.arange(expert_count, dtype=jnp.int32)[None, None, :]
    weight = jnp.sum(jnp.where(named, gate_vals[:, :, None], 0.0), axis=1)
    high = weight.astype(jnp.bfloat16)
    low = (weight - high.astype(jnp.float32)).astype(jnp.bfloat16)
    extra = -(-2 * expert_count // BLOCK) * BLOCK
    pad = jnp.zeros((token_count, extra - 2 * expert_count), jnp.bfloat16)
    half = token_count // 2
    halves = [slice(0, half), slice(half, token_count)]
    payload = [
        jnp.concatenate([part[rows] for part in (tokens, high, low, pad)], axis=1)
        for rows in halves
    ]

    together = lax.optimization_barrier
    place = jnp.reshape(own_expert, (1,)).astype(jnp.int32)
    turns = len(bits)
    groups = [(0,), *((far, far + 1) for far in range(1, pair_count - 1, 2)), (pair_count - 1,)]

    def lanes_of(group):
        if len(group) == 2:
            return [came[far] for far in group]
        return [came[group[0]][:half], came[group[0]][half:]]

    def along_z(far):
        low = far & -far
        came[far] = across_chips(came[far ^ low], low)

    def gather_turn(number, turn):
        blocks = lanes[number]
        arrived = [from_partner(block, "dp", orders[lane][turn]) for lane, block in enumerate(blocks)]
        if turn == turns - 1:
            lanes[number] = [part for pair in zip(blocks, arrived) for part in pair]
        else:
            lanes[number] = [jnp.concatenate(pair, axis=0) for pair in zip(blocks, arrived)]

    def layer(number):
        return expert_layer(lanes[number], place, expert_count, *weights)

    place, payload = together((place, payload))
    lanes, outs = {0: payload}, {}
    near = [{far: across_chips(payload[0], far) for far in groups[1]}]
    gather_turn(0, 0)
    in_own = dequantize_in(gate_q[0], up_q[0], gate_scale[0].T, up_scale[0].T)
    lanes, near, payload, in_own, down_own = together((lanes, near, payload, in_own, down_q[0]))
    in_other = from_partner(in_own, "expert", 0)
    down_own = dequantize_down(down_own, down_scale[0])
    near.append({far: across_chips(payload[1], far) for far in groups[1]})
    for turn in range(1, turns):
        gather_turn(0, turn)
    lanes, near, down_own = together((lanes, near, down_own))
    came = {far: jnp.concatenate([part[far] for part in near], axis=0) for far in groups[1]}
    down_other = from_partner(down_own, "expert", 0)
    lanes[1] = lanes_of(groups[1])
    for number in range(1, len(groups)):
        following = groups[number + 1] if number + 1 < len(groups) else ()
        for turn in range(int(number > 1), turns - 1):
            gather_turn(number, turn)
            if turn == int(number > 1):
                for far in following:
                    along_z(far)
            tied = (lanes, came, outs, in_other, down_other)
            lanes, came, outs, in_other, down_other = together(tied)
        weights = (in_own, in_other, down_own, down_other)
        gather_turn(number, turns - 1)
        if following:
            if turns - 1 == int(number > 1):
                for far in following:
                    along_z(far)
            lanes[number + 1] = lanes_of(following)
            gather_turn(number + 1, 0)
        if number + 1 == len(groups):
            break
        outs[number - 1] = layer(number - 1)
        if number + 2 != len(groups):
            lanes, outs, came = together((lanes, outs, came))
    final = len(groups) - 1
    sums, merged, parts = {}, {}, []

    def sum_turn(number, turn):
        result = []
        for lane in range(2):
            if turn == turns - 1:
                kept, sent = outs[number][2 * lane : 2 * lane + 2]
            else:
                kept, sent = jnp.split(sums[number][lane], 2, axis=0)
            result.append(added(kept, from_partner(sent, "dp", orders[lane][turn])))
        sums[number] = result

    def leave(number):
        group, done = groups[number], sums.pop(number)
        done = done if len(group) == 2 else [jnp.concatenate(done, axis=0)]
        ready = dict(zip(group, done))
        for far in reversed(group):
            block, low = ready[far], far & -far
            if far in merged:
                block = added(block, merged.pop(far))
            if far != low:
                came_back = across_chips(block, low)
                into = far ^ low
                merged[into] = added(merged[into], came_back) if into in merged else came_back
            else:
                whole = across_chips(block, low)
                parts.append([whole[rows] for rows in halves])

    lanes[final - 1], outs = together((lanes[final - 1], outs))
    sum_turn(0, turns - 1)
    outs[final - 1] = layer(final - 1)
    lanes, outs = together((lanes, outs))
    outs[final] = layer(final)
    outs[final], sums = together((outs[final], sums))
    for number in range(final, 0, -1):
        for turn in range(turns - 1 - int(number < final), -1, -1):
            sum_turn(number, turn)
            if turn == 0 and number > 1:
                sum_turn(number - 1, turns - 1)
        if number > 1:
            sums, outs = together((sums, outs))
            leave(number)
    leave(1)
    for turn in range(turns - 2, -1, -1):
        sum_turn(0, turn)
    result = []
    for lane, rows in enumerate(halves):
        total = tokens[rows].astype(jnp.float32) + sums[0][lane].astype(jnp.float32)
        for part in parts:
            total = total + part[lane].astype(jnp.float32)
        result.append(total.astype(jnp.bfloat16))
    return jnp.concatenate(result, axis=0)


def shards(tokens, expert_ids, *weights):
    expert_count = lax.axis_size("dp") * lax.axis_size("expert") // 2
    token_count, top_count = expert_ids.shape
    capacity = 2 * token_count * top_count // expert_count
    group_count, pair_count = lax.axis_size("dp"), lax.axis_size("expert") // 2
    powers = all(count & (count - 1) == 0 for count in (group_count, pair_count))
    dense = capacity >= token_count and powers and min(group_count, pair_count) >= 4
    plan = by_sums if dense else by_rows
    return plan(tokens, expert_ids, *weights)


def solution(mesh):
    return jax.shard_map(
        shards,
        mesh=mesh,
        in_specs=(
            P(("dp", "expert"), None),
            P(("dp", "expert"), None),
            P(("dp", "expert"), None),
            P("dp", None, "expert"),
            P("dp", None, "expert"),
            P("dp", "expert", None),
            P("dp", None, "expert"),
            P("dp", None, "expert"),
            P("dp", "expert", None),
        ),
        out_specs=P(("dp", "expert"), None),
        check_vma=False,
    )
```

```python
import functools

import jax
import jax.numpy as jnp
from jax import lax
from jax.experimental import pallas as pl
from jax.experimental.pallas import tpu as pltpu
from jax.sharding import PartitionSpec as P

BLOCK = 128


def from_partner(block, axis, bit):
    count = lax.axis_size(axis)
    route = []
    for low in range(count):
        high = low | 1 << bit
        if high != low and high < count:
            route += [(low, high), (high, low)]
    return lax.ppermute(block, axis, route)


def dequantize(quant_vals, block_scale):
    row_count, col_count = quant_vals.shape
    blocked = quant_vals.reshape(row_count // BLOCK, BLOCK, col_count // BLOCK, BLOCK).astype(
        jnp.float32
    )
    scaled = blocked * block_scale[:, None, :, None]
    return scaled.reshape(row_count, col_count).astype(jnp.bfloat16)


def expert_ffn(inputs, w_gate, w_up, w_down):
    gate_part = jnp.dot(inputs, w_gate, preferred_element_type=jnp.float32)
    up_part = jnp.dot(inputs, w_up, preferred_element_type=jnp.float32)
    hidden = (jax.nn.silu(gate_part) * up_part).astype(jnp.bfloat16)
    return jnp.dot(hidden, w_down, preferred_element_type=jnp.float32)


def across_groups(blocks):
    return lax.all_to_all(blocks, "dp", split_axis=1, concat_axis=1, tiled=True)


def across_owners(blocks):
    return lax.all_to_all(blocks, "expert", split_axis=0, concat_axis=0, tiled=True)


def by_rows(tokens, expert_ids, gate_vals, gate_q, up_q, down_q, gate_scale, up_scale, down_scale):
    group_count = lax.axis_size("dp")
    owner_count = lax.axis_size("expert")
    token_count, model_width = tokens.shape
    top_count = expert_ids.shape[1]
    pair_count = owner_count // 2
    expert_count = group_count * pair_count
    capacity = 2 * token_count * top_count // expert_count
    half_cap = capacity // 2
    slot_count = owner_count * group_count * half_cap
    routes = expert_ids.reshape(-1)
    onehot = (routes[:, None] == jnp.arange(expert_count, dtype=jnp.int32)[None, :]).astype(
        jnp.int32
    )
    earlier = jnp.cumsum(onehot, axis=0) - onehot
    route_slot = jnp.sum(earlier * onehot, axis=1)
    route_group = routes // pair_count
    route_pair = routes % pair_count
    route_owner = 2 * route_pair + route_slot // half_cap
    route_place = route_slot % half_cap
    route_index = (route_owner * group_count + route_group) * half_cap + route_place
    chosen = jnp.arange(slot_count, dtype=jnp.int32)[:, None] == route_index[None, :]
    chosen = jnp.any(chosen.reshape(slot_count, token_count, top_count), axis=2).astype(
        jnp.bfloat16
    )
    outgoing = jnp.dot(chosen, tokens, preferred_element_type=jnp.float32).astype(jnp.bfloat16)
    outgoing = outgoing.reshape(owner_count, group_count, half_cap, model_width)
    arrived = across_owners(across_groups(outgoing))
    own_rows = arrived.reshape(-1, model_width)
    row_count = own_rows.shape[0]
    w_gate = dequantize(gate_q[0], gate_scale[0])
    w_up = dequantize(up_q[0], up_scale[0])
    w_down = dequantize(down_q[0], down_scale[0])
    partner_rows = from_partner(own_rows, "expert", 0)
    both_rows = jnp.concatenate([own_rows, partner_rows], axis=0)
    partial_value = expert_ffn(both_rows, w_gate, w_up, w_down)
    returned = from_partner(partial_value[row_count:], "expert", 0)
    expert_out = (partial_value[:row_count] + returned).astype(jnp.bfloat16)
    expert_out = expert_out.reshape(owner_count, group_count, half_cap, model_width)
    returned_rows = across_groups(across_owners(expert_out))
    returned_rows = returned_rows.reshape(slot_count, model_width)
    picked = returned_rows[route_index].reshape(token_count, top_count, model_width)
    weighted = jnp.einsum("tkd,tk->td", picked.astype(jnp.float32), gate_vals)
    mixed = tokens.astype(jnp.float32) + weighted
    return mixed.astype(jnp.bfloat16)


def added(block, arrived):
    return (block.astype(jnp.float32) + arrived.astype(jnp.float32)).astype(jnp.bfloat16)


def scaled(block, scale):
    return (block.astype(jnp.float32) * scale).astype(jnp.bfloat16)


def chunk_copies(sources, targets, sems):
    chunks = sems.shape[1]
    depth = sources[0].shape[0] // chunks

    def copy(part, chunk):
        at = pl.ds(pl.multiple_of(chunk * depth, depth), depth)
        return pltpu.make_async_copy(sources[part].at[at], targets[part].at[at], sems.at[part, chunk])

    for chunk in range(chunks):
        for part in range(len(sources)):
            copy(part, chunk).start()
    return copy


def in_kernel(gate_scales, up_scales, gate, up, out, gate_raw, up_raw, sems):
    rows, cols = gate.shape
    chunks = sems.shape[1]
    strip = rows // chunks // BLOCK
    copy = chunk_copies((gate, up), (gate_raw, up_raw), sems)

    @pl.loop(0, chunks)
    def _(chunk):
        copy(0, chunk).wait()
        copy(1, chunk).wait()
        for block in range(strip):
            row = chunk * strip + block
            at = pl.ds(pl.multiple_of(row * BLOCK, BLOCK), BLOCK)
            for col in range(cols // BLOCK):
                source, to = slice(col * BLOCK, (col + 1) * BLOCK), 2 * col * BLOCK
                out[at, to : to + BLOCK] = scaled(gate_raw[at, source], gate_scales[col, row])
                to += BLOCK
                out[at, to : to + BLOCK] = scaled(up_raw[at, source], up_scales[col, row])


def down_kernel(scales, down, out, raw, sems):
    chunks = sems.shape[1]
    strip = down.shape[0] // chunks // BLOCK
    copy = chunk_copies((down,), (raw,), sems)

    @pl.loop(0, chunks)
    def _(chunk):
        copy(0, chunk).wait()
        for block in range(strip):
            row = chunk * strip + block
            at = pl.ds(pl.multiple_of(row * BLOCK, BLOCK), BLOCK)
            for col in range(down.shape[1] // BLOCK):
                cols = slice(col * BLOCK, (col + 1) * BLOCK)
                out[at, cols] = scaled(raw[at, cols], scales[row, col])


def dequantize_call(kernel, name, quants, scales, width, chunks):
    rows, cols = quants[0].shape
    quants = [pltpu.with_memory_space_constraint(quant, pltpu.HBM) for quant in quants]
    return pl.pallas_call(
        kernel,
        in_specs=[pl.BlockSpec(memory_space=pltpu.SMEM)] * len(scales)
        + [pl.BlockSpec(memory_space=pl.ANY)] * len(quants),
        out_specs=pl.BlockSpec(memory_space=pltpu.VMEM),
        out_shape=jax.ShapeDtypeStruct((rows, width), jnp.bfloat16),
        scratch_shapes=[
            *(pltpu.VMEM(quant.shape, jnp.bfloat16) for quant in quants),
            pltpu.SemaphoreType.DMA((len(quants), chunks)),
        ],
        cost_estimate=pl.CostEstimate(
            flops=rows * width, bytes_accessed=4 * rows * width, transcendentals=0
        ),
        compiler_params=pltpu.CompilerParams(vmem_limit_bytes=16 * 1024 * 1024),
        name=name,
    )(*scales, *quants)


def dequantize_in(gate, up, gate_scales, up_scales):
    rows, cols = gate.shape
    chunks = max(1, rows // (4 * BLOCK))
    scales = (gate_scales, up_scales)
    return dequantize_call(in_kernel, "dequantize_in", (gate, up), scales, 2 * cols, chunks)


def dequantize_down(down, scales):
    rows, cols = down.shape
    return dequantize_call(down_kernel, "dequantize_down", (down,), (scales,), cols, rows // BLOCK)


def silu(v):
    return v / (1 + jnp.exp(-v))


def expert_kernel(count, experts, own_expert, *refs):
    pieces, refs = refs[:count], refs[count:]
    in_refs, down_refs, refs = refs[:2], refs[2:4], refs[4:]
    outs, (rows, hidden) = refs[:count], refs[count:]
    size, (half, model_width) = pieces[0].shape[0], down_refs[0].shape
    strip = min(4 * BLOCK, model_width)

    weights = []
    for place, piece in enumerate(pieces):
        rows[place * size : (place + 1) * size, :] = piece[:, :model_width]
        marks = piece[:, model_width:].astype(jnp.float32)
        column = lax.broadcasted_iota(jnp.int32, marks.shape, 1)
        chosen = (column == own_expert[0]) | (column == own_expert[0] + experts)
        weights.append(jnp.sum(jnp.where(chosen, marks, 0.0), axis=1, keepdims=True))
    for part, in_ref in enumerate(in_refs):
        for col in range(half // BLOCK):
            at = slice(2 * col * BLOCK, 2 * (col + 1) * BLOCK)
            both = jnp.dot(rows[...], in_ref[:, at], preferred_element_type=jnp.float32)
            value = (silu(both[:, :BLOCK]) * both[:, BLOCK:]).astype(jnp.bfloat16)
            to = part * half + col * BLOCK
            hidden[:, to : to + BLOCK] = value
    for first in range(0, model_width, strip):
        at = slice(first, first + strip)
        value = jnp.dot(hidden[:, :half], down_refs[0][:, at], preferred_element_type=jnp.float32)
        value += jnp.dot(hidden[:, half:], down_refs[1][:, at], preferred_element_type=jnp.float32)
        for place, out in enumerate(outs):
            weighted = value[place * size : (place + 1) * size] * weights[place]
            out[:, at] = weighted.astype(jnp.bfloat16)


def expert_layer(pieces, own_expert, experts, *weights):
    count, size = len(pieces), pieces[0].shape[0]
    model_width, width = weights[0].shape
    total = count * size
    whole = pl.BlockSpec(memory_space=pltpu.VMEM)
    weights = [pltpu.with_memory_space_constraint(weight, pltpu.VMEM) for weight in weights]
    return pl.pallas_call(
        functools.partial(expert_kernel, count, experts),
        in_specs=[pl.BlockSpec(memory_space=pltpu.SMEM)] + [whole] * (count + len(weights)),
        out_specs=[whole] * count,
        out_shape=[jax.ShapeDtypeStruct((size, model_width), jnp.bfloat16)] * count,
        scratch_shapes=[
            pltpu.VMEM((total, model_width), jnp.bfloat16),
            pltpu.VMEM((total, width), jnp.bfloat16),
        ],
        cost_estimate=pl.CostEstimate(
            flops=6 * total * model_width * width,
            bytes_accessed=6 * model_width * width + 4 * total * model_width,
            transcendentals=total * width,
        ),
        compiler_params=pltpu.CompilerParams(vmem_limit_bytes=16 * 1024 * 1024),
        name="expert_layer",
    )(own_expert, *pieces, *weights)


def across_chips(block, far):
    count = lax.axis_size("expert")
    return lax.ppermute(block, "expert", [(low, low ^ 2 * far) for low in range(count)])


def by_sums(tokens, expert_ids, gate_vals, gate_q, up_q, down_q, gate_scale, up_scale, down_scale):
    token_count, model_width = tokens.shape
    group_count = lax.axis_size("dp")
    pair_count = lax.axis_size("expert") // 2
    expert_count = group_count * pair_count
    own_expert = lax.axis_index("dp") * pair_count + lax.axis_index("expert") // 2
    bits = list(range(group_count.bit_length() - 1))
    orders = (bits, bits[::-1])

    named = expert_ids[:, :, None] == jnp.arange(expert_count, dtype=jnp.int32)[None, None, :]
    weight = jnp.sum(jnp.where(named, gate_vals[:, :, None], 0.0), axis=1)
    high = weight.astype(jnp.bfloat16)
    low = (weight - high.astype(jnp.float32)).astype(jnp.bfloat16)
    extra = -(-2 * expert_count // BLOCK) * BLOCK
    pad = jnp.zeros((token_count, extra - 2 * expert_count), jnp.bfloat16)
    half = token_count // 2
    halves = [slice(0, half), slice(half, token_count)]
    payload = [
        jnp.concatenate([part[rows] for part in (tokens, high, low, pad)], axis=1)
        for rows in halves
    ]

    together = lax.optimization_barrier
    place = jnp.reshape(own_expert, (1,)).astype(jnp.int32)
    turns = len(bits)
    groups = [(0,), *((far, far + 1) for far in range(1, pair_count - 1, 2)), (pair_count - 1,)]

    def lanes_of(group):
        if len(group) == 2:
            return [came[far] for far in group]
        return [came[group[0]][:half], came[group[0]][half:]]

    def along_z(far):
        low = far & -far
        came[far] = across_chips(came[far ^ low], low)

    def gather_turn(number, turn):
        blocks = lanes[number]
        arrived = [from_partner(block, "dp", orders[lane][turn]) for lane, block in enumerate(blocks)]
        if turn == turns - 1:
            lanes[number] = [part for pair in zip(blocks, arrived) for part in pair]
        else:
            lanes[number] = [jnp.concatenate(pair, axis=0) for pair in zip(blocks, arrived)]

    def layer(number):
        return expert_layer(lanes[number], place, expert_count, *weights)

    place, payload = together((place, payload))
    lanes, outs = {0: payload}, {}
    near = [{far: across_chips(payload[0], far) for far in groups[1]}]
    gather_turn(0, 0)
    in_own = dequantize_in(gate_q[0], up_q[0], gate_scale[0].T, up_scale[0].T)
    lanes, near, payload, in_own, down_own = together((lanes, near, payload, in_own, down_q[0]))
    in_other = from_partner(in_own, "expert", 0)
    down_own = dequantize_down(down_own, down_scale[0])
    near.append({far: across_chips(payload[1], far) for far in groups[1]})
    for turn in range(1, turns):
        gather_turn(0, turn)
    lanes, near, down_own = together((lanes, near, down_own))
    came = {far: jnp.concatenate([part[far] for part in near], axis=0) for far in groups[1]}
    down_other = from_partner(down_own, "expert", 0)
    lanes[1] = lanes_of(groups[1])
    for number in range(1, len(groups)):
        following = groups[number + 1] if number + 1 < len(groups) else ()
        for turn in range(int(number > 1), turns - 1):
            gather_turn(number, turn)
            if turn == int(number > 1):
                for far in following:
                    along_z(far)
            tied = (lanes, came, outs, in_other, down_other)
            lanes, came, outs, in_other, down_other = together(tied)
        weights = (in_own, in_other, down_own, down_other)
        gather_turn(number, turns - 1)
        if following:
            if turns - 1 == int(number > 1):
                for far in following:
                    along_z(far)
            lanes[number + 1] = lanes_of(following)
            gather_turn(number + 1, 0)
        if number + 1 == len(groups):
            break
        outs[number - 1] = layer(number - 1)
        if number + 2 != len(groups):
            lanes, outs, came = together((lanes, outs, came))
    final = len(groups) - 1
    sums, merged, parts = {}, {}, []

    def sum_turn(number, turn):
        result = []
        for lane in range(2):
            if turn == turns - 1:
                kept, sent = outs[number][2 * lane : 2 * lane + 2]
            else:
                kept, sent = jnp.split(sums[number][lane], 2, axis=0)
            result.append(added(kept, from_partner(sent, "dp", orders[lane][turn])))
        sums[number] = result

    def leave(number):
        group, done = groups[number], sums.pop(number)
        done = done if len(group) == 2 else [jnp.concatenate(done, axis=0)]
        ready = dict(zip(group, done))
        for far in reversed(group):
            block, low = ready[far], far & -far
            if far in merged:
                block = added(block, merged.pop(far))
            if far != low:
                came_back = across_chips(block, low)
                into = far ^ low
                merged[into] = added(merged[into], came_back) if into in merged else came_back
            else:
                whole = across_chips(block, low)
                parts.append([whole[rows] for rows in halves])

    lanes[final - 1], outs = together((lanes[final - 1], outs))
    sum_turn(0, turns - 1)
    outs[final - 1] = layer(final - 1)
    lanes, outs = together((lanes, outs))
    outs[final] = layer(final)
    outs[final], sums = together((outs[final], sums))
    for number in range(final, 0, -1):
        first = turns - 1 if number == final else turns - 2
        for turn in range(first, -1, -1):
            sum_turn(number, turn)
            if turn == first and number > 1:
                sum_turn(number - 1, turns - 1)
                sums = together(sums)
        if number > 1:
            leave(number)
    leave(1)
    for turn in range(turns - 2, -1, -1):
        sum_turn(0, turn)
    result = []
    for lane, rows in enumerate(halves):
        total = tokens[rows].astype(jnp.float32) + sums[0][lane].astype(jnp.float32)
        for part in parts:
            total = total + part[lane].astype(jnp.float32)
        result.append(total.astype(jnp.bfloat16))
    return jnp.concatenate(result, axis=0)


def shards(tokens, expert_ids, *weights):
    expert_count = lax.axis_size("dp") * lax.axis_size("expert") // 2
    token_count, top_count = expert_ids.shape
    capacity = 2 * token_count * top_count // expert_count
    group_count, pair_count = lax.axis_size("dp"), lax.axis_size("expert") // 2
    powers = all(count & (count - 1) == 0 for count in (group_count, pair_count))
    dense = capacity >= token_count and powers and min(group_count, pair_count) >= 4
    plan = by_sums if dense else by_rows
    return plan(tokens, expert_ids, *weights)


def solution(mesh):
    return jax.shard_map(
        shards,
        mesh=mesh,
        in_specs=(
            P(("dp", "expert"), None),
            P(("dp", "expert"), None),
            P(("dp", "expert"), None),
            P("dp", None, "expert"),
            P("dp", None, "expert"),
            P("dp", "expert", None),
            P("dp", None, "expert"),
            P("dp", None, "expert"),
            P("dp", "expert", None),
        ),
        out_specs=P(("dp", "expert"), None),
        check_vma=False,
    )
```

```python
import functools

import jax
import jax.numpy as jnp
from jax import lax
from jax.experimental import pallas as pl
from jax.experimental.pallas import tpu as pltpu
from jax.sharding import PartitionSpec as P

BLOCK = 128


def from_partner(block, axis, bit):
    count = lax.axis_size(axis)
    route = []
    for low in range(count):
        high = low | 1 << bit
        if high != low and high < count:
            route += [(low, high), (high, low)]
    return lax.ppermute(block, axis, route)


def dequantize(quant_vals, block_scale):
    row_count, col_count = quant_vals.shape
    blocked = quant_vals.reshape(row_count // BLOCK, BLOCK, col_count // BLOCK, BLOCK).astype(
        jnp.float32
    )
    scaled = blocked * block_scale[:, None, :, None]
    return scaled.reshape(row_count, col_count).astype(jnp.bfloat16)


def expert_ffn(inputs, w_gate, w_up, w_down):
    gate_part = jnp.dot(inputs, w_gate, preferred_element_type=jnp.float32)
    up_part = jnp.dot(inputs, w_up, preferred_element_type=jnp.float32)
    hidden = (jax.nn.silu(gate_part) * up_part).astype(jnp.bfloat16)
    return jnp.dot(hidden, w_down, preferred_element_type=jnp.float32)


def across_groups(blocks):
    return lax.all_to_all(blocks, "dp", split_axis=1, concat_axis=1, tiled=True)


def across_owners(blocks):
    return lax.all_to_all(blocks, "expert", split_axis=0, concat_axis=0, tiled=True)


def by_rows(tokens, expert_ids, gate_vals, gate_q, up_q, down_q, gate_scale, up_scale, down_scale):
    group_count = lax.axis_size("dp")
    owner_count = lax.axis_size("expert")
    token_count, model_width = tokens.shape
    top_count = expert_ids.shape[1]
    pair_count = owner_count // 2
    expert_count = group_count * pair_count
    capacity = 2 * token_count * top_count // expert_count
    half_cap = capacity // 2
    slot_count = owner_count * group_count * half_cap
    routes = expert_ids.reshape(-1)
    onehot = (routes[:, None] == jnp.arange(expert_count, dtype=jnp.int32)[None, :]).astype(
        jnp.int32
    )
    earlier = jnp.cumsum(onehot, axis=0) - onehot
    route_slot = jnp.sum(earlier * onehot, axis=1)
    route_group = routes // pair_count
    route_pair = routes % pair_count
    route_owner = 2 * route_pair + route_slot // half_cap
    route_place = route_slot % half_cap
    route_index = (route_owner * group_count + route_group) * half_cap + route_place
    chosen = jnp.arange(slot_count, dtype=jnp.int32)[:, None] == route_index[None, :]
    chosen = jnp.any(chosen.reshape(slot_count, token_count, top_count), axis=2).astype(
        jnp.bfloat16
    )
    outgoing = jnp.dot(chosen, tokens, preferred_element_type=jnp.float32).astype(jnp.bfloat16)
    outgoing = outgoing.reshape(owner_count, group_count, half_cap, model_width)
    arrived = across_owners(across_groups(outgoing))
    own_rows = arrived.reshape(-1, model_width)
    row_count = own_rows.shape[0]
    w_gate = dequantize(gate_q[0], gate_scale[0])
    w_up = dequantize(up_q[0], up_scale[0])
    w_down = dequantize(down_q[0], down_scale[0])
    partner_rows = from_partner(own_rows, "expert", 0)
    both_rows = jnp.concatenate([own_rows, partner_rows], axis=0)
    partial_value = expert_ffn(both_rows, w_gate, w_up, w_down)
    returned = from_partner(partial_value[row_count:], "expert", 0)
    expert_out = (partial_value[:row_count] + returned).astype(jnp.bfloat16)
    expert_out = expert_out.reshape(owner_count, group_count, half_cap, model_width)
    returned_rows = across_groups(across_owners(expert_out))
    returned_rows = returned_rows.reshape(slot_count, model_width)
    picked = returned_rows[route_index].reshape(token_count, top_count, model_width)
    weighted = jnp.einsum("tkd,tk->td", picked.astype(jnp.float32), gate_vals)
    mixed = tokens.astype(jnp.float32) + weighted
    return mixed.astype(jnp.bfloat16)


def added(block, arrived):
    return (block.astype(jnp.float32) + arrived.astype(jnp.float32)).astype(jnp.bfloat16)


def scaled(block, scale):
    return (block.astype(jnp.float32) * scale).astype(jnp.bfloat16)


def chunk_copies(sources, targets, sems):
    chunks = sems.shape[1]
    depth = sources[0].shape[0] // chunks

    def copy(part, chunk):
        at = pl.ds(pl.multiple_of(chunk * depth, depth), depth)
        return pltpu.make_async_copy(sources[part].at[at], targets[part].at[at], sems.at[part, chunk])

    for chunk in range(chunks):
        for part in range(len(sources)):
            copy(part, chunk).start()
    return copy


def in_kernel(gate_scales, up_scales, gate, up, out, gate_raw, up_raw, sems):
    rows, cols = gate.shape
    chunks = sems.shape[1]
    strip = rows // chunks // BLOCK
    copy = chunk_copies((gate, up), (gate_raw, up_raw), sems)

    @pl.loop(0, chunks)
    def _(chunk):
        copy(0, chunk).wait()
        copy(1, chunk).wait()
        for block in range(strip):
            row = chunk * strip + block
            at = pl.ds(pl.multiple_of(row * BLOCK, BLOCK), BLOCK)
            for col in range(cols // BLOCK):
                source, to = slice(col * BLOCK, (col + 1) * BLOCK), 2 * col * BLOCK
                out[at, to : to + BLOCK] = scaled(gate_raw[at, source], gate_scales[col, row])
                to += BLOCK
                out[at, to : to + BLOCK] = scaled(up_raw[at, source], up_scales[col, row])


def down_kernel(scales, down, out, raw, sems):
    chunks = sems.shape[1]
    strip = down.shape[0] // chunks // BLOCK
    copy = chunk_copies((down,), (raw,), sems)

    @pl.loop(0, chunks)
    def _(chunk):
        copy(0, chunk).wait()
        for block in range(strip):
            row = chunk * strip + block
            at = pl.ds(pl.multiple_of(row * BLOCK, BLOCK), BLOCK)
            for col in range(down.shape[1] // BLOCK):
                cols = slice(col * BLOCK, (col + 1) * BLOCK)
                out[at, cols] = scaled(raw[at, cols], scales[row, col])


def dequantize_call(kernel, name, quants, scales, width, chunks):
    rows, cols = quants[0].shape
    quants = [pltpu.with_memory_space_constraint(quant, pltpu.HBM) for quant in quants]
    return pl.pallas_call(
        kernel,
        in_specs=[pl.BlockSpec(memory_space=pltpu.SMEM)] * len(scales)
        + [pl.BlockSpec(memory_space=pl.ANY)] * len(quants),
        out_specs=pl.BlockSpec(memory_space=pltpu.VMEM),
        out_shape=jax.ShapeDtypeStruct((rows, width), jnp.bfloat16),
        scratch_shapes=[
            *(pltpu.VMEM(quant.shape, jnp.bfloat16) for quant in quants),
            pltpu.SemaphoreType.DMA((len(quants), chunks)),
        ],
        cost_estimate=pl.CostEstimate(
            flops=rows * width, bytes_accessed=4 * rows * width, transcendentals=0
        ),
        compiler_params=pltpu.CompilerParams(vmem_limit_bytes=16 * 1024 * 1024),
        name=name,
    )(*scales, *quants)


def dequantize_in(gate, up, gate_scales, up_scales):
    rows, cols = gate.shape
    chunks = max(1, rows // (4 * BLOCK))
    scales = (gate_scales, up_scales)
    return dequantize_call(in_kernel, "dequantize_in", (gate, up), scales, 2 * cols, chunks)


def dequantize_down(down, scales):
    rows, cols = down.shape
    return dequantize_call(down_kernel, "dequantize_down", (down,), (scales,), cols, rows // BLOCK)


def silu(v):
    return v / (1 + jnp.exp(-v))


def expert_kernel(count, experts, own_expert, *refs):
    pieces, refs = refs[:count], refs[count:]
    in_refs, down_refs, refs = refs[:2], refs[2:4], refs[4:]
    outs, (rows, hidden) = refs[:count], refs[count:]
    size, (half, model_width) = pieces[0].shape[0], down_refs[0].shape
    strip = min(4 * BLOCK, model_width)

    weights = []
    for place, piece in enumerate(pieces):
        rows[place * size : (place + 1) * size, :] = piece[:, :model_width]
        marks = piece[:, model_width:].astype(jnp.float32)
        column = lax.broadcasted_iota(jnp.int32, marks.shape, 1)
        chosen = (column == own_expert[0]) | (column == own_expert[0] + experts)
        weights.append(jnp.sum(jnp.where(chosen, marks, 0.0), axis=1, keepdims=True))
    for part, in_ref in enumerate(in_refs):
        for col in range(half // BLOCK):
            at = slice(2 * col * BLOCK, 2 * (col + 1) * BLOCK)
            both = jnp.dot(rows[...], in_ref[:, at], preferred_element_type=jnp.float32)
            value = (silu(both[:, :BLOCK]) * both[:, BLOCK:]).astype(jnp.bfloat16)
            to = part * half + col * BLOCK
            hidden[:, to : to + BLOCK] = value
    for first in range(0, model_width, strip):
        at = slice(first, first + strip)
        value = jnp.dot(hidden[:, :half], down_refs[0][:, at], preferred_element_type=jnp.float32)
        value += jnp.dot(hidden[:, half:], down_refs[1][:, at], preferred_element_type=jnp.float32)
        for place, out in enumerate(outs):
            weighted = value[place * size : (place + 1) * size] * weights[place]
            out[:, at] = weighted.astype(jnp.bfloat16)


def expert_layer(pieces, own_expert, experts, *weights):
    count, size = len(pieces), pieces[0].shape[0]
    model_width, width = weights[0].shape
    total = count * size
    whole = pl.BlockSpec(memory_space=pltpu.VMEM)
    weights = [pltpu.with_memory_space_constraint(weight, pltpu.VMEM) for weight in weights]
    return pl.pallas_call(
        functools.partial(expert_kernel, count, experts),
        in_specs=[pl.BlockSpec(memory_space=pltpu.SMEM)] + [whole] * (count + len(weights)),
        out_specs=[whole] * count,
        out_shape=[jax.ShapeDtypeStruct((size, model_width), jnp.bfloat16)] * count,
        scratch_shapes=[
            pltpu.VMEM((total, model_width), jnp.bfloat16),
            pltpu.VMEM((total, width), jnp.bfloat16),
        ],
        cost_estimate=pl.CostEstimate(
            flops=6 * total * model_width * width,
            bytes_accessed=6 * model_width * width + 4 * total * model_width,
            transcendentals=total * width,
        ),
        compiler_params=pltpu.CompilerParams(vmem_limit_bytes=16 * 1024 * 1024),
        name="expert_layer",
    )(own_expert, *pieces, *weights)


def across_chips(block, far):
    count = lax.axis_size("expert")
    return lax.ppermute(block, "expert", [(low, low ^ 2 * far) for low in range(count)])


def by_sums(tokens, expert_ids, gate_vals, gate_q, up_q, down_q, gate_scale, up_scale, down_scale):
    token_count, model_width = tokens.shape
    group_count = lax.axis_size("dp")
    pair_count = lax.axis_size("expert") // 2
    expert_count = group_count * pair_count
    own_expert = lax.axis_index("dp") * pair_count + lax.axis_index("expert") // 2
    bits = list(range(group_count.bit_length() - 1))
    orders = (bits, bits[::-1])

    named = expert_ids[:, :, None] == jnp.arange(expert_count, dtype=jnp.int32)[None, None, :]
    weight = jnp.sum(jnp.where(named, gate_vals[:, :, None], 0.0), axis=1)
    high = weight.astype(jnp.bfloat16)
    low = (weight - high.astype(jnp.float32)).astype(jnp.bfloat16)
    extra = -(-2 * expert_count // BLOCK) * BLOCK
    pad = jnp.zeros((token_count, extra - 2 * expert_count), jnp.bfloat16)
    half = token_count // 2
    halves = [slice(0, half), slice(half, token_count)]
    payload = [
        jnp.concatenate([part[rows] for part in (tokens, high, low, pad)], axis=1)
        for rows in halves
    ]

    together = lax.optimization_barrier
    place = jnp.reshape(own_expert, (1,)).astype(jnp.int32)
    turns = len(bits)
    groups = [(0,), *((far, far + 1) for far in range(1, pair_count - 1, 2)), (pair_count - 1,)]

    def lanes_of(group):
        if len(group) == 2:
            return [came[far] for far in group]
        return [came[group[0]][:half], came[group[0]][half:]]

    def along_z(far):
        low = far & -far
        came[far] = across_chips(came[far ^ low], low)

    def gather_turn(number, turn):
        blocks = lanes[number]
        arrived = [from_partner(block, "dp", orders[lane][turn]) for lane, block in enumerate(blocks)]
        if turn == turns - 1:
            lanes[number] = [part for pair in zip(blocks, arrived) for part in pair]
        else:
            lanes[number] = [jnp.concatenate(pair, axis=0) for pair in zip(blocks, arrived)]

    def layer(number):
        return expert_layer(lanes[number], place, expert_count, *weights)

    place, payload = together((place, payload))
    lanes, outs = {0: payload}, {}
    near = [{far: across_chips(payload[0], far) for far in groups[1]}]
    gather_turn(0, 0)
    in_own = dequantize_in(gate_q[0], up_q[0], gate_scale[0].T, up_scale[0].T)
    lanes, near, payload, in_own, down_own = together((lanes, near, payload, in_own, down_q[0]))
    in_other = from_partner(in_own, "expert", 0)
    down_own = dequantize_down(down_own, down_scale[0])
    near.append({far: across_chips(payload[1], far) for far in groups[1]})
    for turn in range(1, turns):
        gather_turn(0, turn)
    lanes, near, down_own = together((lanes, near, down_own))
    came = {far: jnp.concatenate([part[far] for part in near], axis=0) for far in groups[1]}
    down_other = from_partner(down_own, "expert", 0)
    lanes[1] = lanes_of(groups[1])
    for number in range(1, len(groups)):
        following = groups[number + 1] if number + 1 < len(groups) else ()
        for turn in range(int(number > 1), turns - 1):
            gather_turn(number, turn)
            if turn == int(number > 1):
                for far in following:
                    along_z(far)
            tied = (lanes, came, outs, in_other, down_other)
            lanes, came, outs, in_other, down_other = together(tied)
        weights = (in_own, in_other, down_own, down_other)
        gather_turn(number, turns - 1)
        if following:
            if turns - 1 == int(number > 1):
                for far in following:
                    along_z(far)
            lanes[number + 1] = lanes_of(following)
            gather_turn(number + 1, 0)
        if number + 1 == len(groups):
            break
        outs[number - 1] = layer(number - 1)
        if number + 2 != len(groups):
            lanes, outs, came = together((lanes, outs, came))
    final = len(groups) - 1
    sums, merged, parts = {}, {}, []

    def sum_turn(number, turn):
        result = []
        for lane in range(2):
            if turn == turns - 1:
                kept, sent = outs[number][2 * lane : 2 * lane + 2]
            else:
                kept, sent = jnp.split(sums[number][lane], 2, axis=0)
            result.append(added(kept, from_partner(sent, "dp", orders[lane][turn])))
        sums[number] = result

    def leave(number):
        group, done = groups[number], sums.pop(number)
        done = done if len(group) == 2 else [jnp.concatenate(done, axis=0)]
        ready = dict(zip(group, done))
        for far in reversed(group):
            block, low = ready[far], far & -far
            if far in merged:
                block = added(block, merged.pop(far))
            if far != low:
                came_back = across_chips(block, low)
                into = far ^ low
                merged[into] = added(merged[into], came_back) if into in merged else came_back
            else:
                whole = across_chips(block, low)
                parts.append([whole[rows] for rows in halves])

    lanes[final - 1], outs = together((lanes[final - 1], outs))
    sum_turn(0, turns - 1)
    outs[final - 1] = layer(final - 1)
    lanes, outs, sums[0][0] = together((lanes, outs, sums[0][0]))
    outs[final] = layer(final)
    for number in range(final, 0, -1):
        for turn in range(turns - 1 - int(number < final), -1, -1):
            sum_turn(number, turn)
            if turn == 0 and number > 1:
                sum_turn(number - 1, turns - 1)
        if number > 1:
            leave(number)
        sums, outs = together((sums, outs))
    leave(1)
    for turn in range(turns - 2, -1, -1):
        sum_turn(0, turn)
    result = []
    for lane, rows in enumerate(halves):
        total = tokens[rows].astype(jnp.float32) + sums[0][lane].astype(jnp.float32)
        for part in parts:
            total = total + part[lane].astype(jnp.float32)
        result.append(total.astype(jnp.bfloat16))
    return jnp.concatenate(result, axis=0)


def shards(tokens, expert_ids, *weights):
    expert_count = lax.axis_size("dp") * lax.axis_size("expert") // 2
    token_count, top_count = expert_ids.shape
    capacity = 2 * token_count * top_count // expert_count
    group_count, pair_count = lax.axis_size("dp"), lax.axis_size("expert") // 2
    powers = all(count & (count - 1) == 0 for count in (group_count, pair_count))
    dense = capacity >= token_count and powers and min(group_count, pair_count) >= 4
    plan = by_sums if dense else by_rows
    return plan(tokens, expert_ids, *weights)


def solution(mesh):
    return jax.shard_map(
        shards,
        mesh=mesh,
        in_specs=(
            P(("dp", "expert"), None),
            P(("dp", "expert"), None),
            P(("dp", "expert"), None),
            P("dp", None, "expert"),
            P("dp", None, "expert"),
            P("dp", "expert", None),
            P("dp", None, "expert"),
            P("dp", None, "expert"),
            P("dp", "expert", None),
        ),
        out_specs=P(("dp", "expert"), None),
        check_vma=False,
    )
```

```python
import functools

import jax
import jax.numpy as jnp
from jax import lax
from jax.experimental import pallas as pl
from jax.experimental.pallas import tpu as pltpu
from jax.sharding import PartitionSpec as P

BLOCK = 128


def from_partner(block, axis, bit):
    count = lax.axis_size(axis)
    route = []
    for low in range(count):
        high = low | 1 << bit
        if high != low and high < count:
            route += [(low, high), (high, low)]
    return lax.ppermute(block, axis, route)


def dequantize(quant_vals, block_scale):
    row_count, col_count = quant_vals.shape
    blocked = quant_vals.reshape(row_count // BLOCK, BLOCK, col_count // BLOCK, BLOCK).astype(
        jnp.float32
    )
    scaled = blocked * block_scale[:, None, :, None]
    return scaled.reshape(row_count, col_count).astype(jnp.bfloat16)


def expert_ffn(inputs, w_gate, w_up, w_down):
    gate_part = jnp.dot(inputs, w_gate, preferred_element_type=jnp.float32)
    up_part = jnp.dot(inputs, w_up, preferred_element_type=jnp.float32)
    hidden = (jax.nn.silu(gate_part) * up_part).astype(jnp.bfloat16)
    return jnp.dot(hidden, w_down, preferred_element_type=jnp.float32)


def across_groups(blocks):
    return lax.all_to_all(blocks, "dp", split_axis=1, concat_axis=1, tiled=True)


def across_owners(blocks):
    return lax.all_to_all(blocks, "expert", split_axis=0, concat_axis=0, tiled=True)


def by_rows(tokens, expert_ids, gate_vals, gate_q, up_q, down_q, gate_scale, up_scale, down_scale):
    group_count = lax.axis_size("dp")
    owner_count = lax.axis_size("expert")
    token_count, model_width = tokens.shape
    top_count = expert_ids.shape[1]
    pair_count = owner_count // 2
    expert_count = group_count * pair_count
    capacity = 2 * token_count * top_count // expert_count
    half_cap = capacity // 2
    slot_count = owner_count * group_count * half_cap
    routes = expert_ids.reshape(-1)
    onehot = (routes[:, None] == jnp.arange(expert_count, dtype=jnp.int32)[None, :]).astype(
        jnp.int32
    )
    earlier = jnp.cumsum(onehot, axis=0) - onehot
    route_slot = jnp.sum(earlier * onehot, axis=1)
    route_group = routes // pair_count
    route_pair = routes % pair_count
    route_owner = 2 * route_pair + route_slot // half_cap
    route_place = route_slot % half_cap
    route_index = (route_owner * group_count + route_group) * half_cap + route_place
    chosen = jnp.arange(slot_count, dtype=jnp.int32)[:, None] == route_index[None, :]
    chosen = jnp.any(chosen.reshape(slot_count, token_count, top_count), axis=2).astype(
        jnp.bfloat16
    )
    outgoing = jnp.dot(chosen, tokens, preferred_element_type=jnp.float32).astype(jnp.bfloat16)
    outgoing = outgoing.reshape(owner_count, group_count, half_cap, model_width)
    arrived = across_owners(across_groups(outgoing))
    own_rows = arrived.reshape(-1, model_width)
    row_count = own_rows.shape[0]
    w_gate = dequantize(gate_q[0], gate_scale[0])
    w_up = dequantize(up_q[0], up_scale[0])
    w_down = dequantize(down_q[0], down_scale[0])
    partner_rows = from_partner(own_rows, "expert", 0)
    both_rows = jnp.concatenate([own_rows, partner_rows], axis=0)
    partial_value = expert_ffn(both_rows, w_gate, w_up, w_down)
    returned = from_partner(partial_value[row_count:], "expert", 0)
    expert_out = (partial_value[:row_count] + returned).astype(jnp.bfloat16)
    expert_out = expert_out.reshape(owner_count, group_count, half_cap, model_width)
    returned_rows = across_groups(across_owners(expert_out))
    returned_rows = returned_rows.reshape(slot_count, model_width)
    picked = returned_rows[route_index].reshape(token_count, top_count, model_width)
    weighted = jnp.einsum("tkd,tk->td", picked.astype(jnp.float32), gate_vals)
    mixed = tokens.astype(jnp.float32) + weighted
    return mixed.astype(jnp.bfloat16)


def added(block, arrived):
    return (block.astype(jnp.float32) + arrived.astype(jnp.float32)).astype(jnp.bfloat16)


def scaled(block, scale):
    return (block.astype(jnp.float32) * scale).astype(jnp.bfloat16)


def chunk_copies(sources, targets, sems):
    chunks = sems.shape[1]
    depth = sources[0].shape[0] // chunks

    def copy(part, chunk):
        at = pl.ds(pl.multiple_of(chunk * depth, depth), depth)
        return pltpu.make_async_copy(sources[part].at[at], targets[part].at[at], sems.at[part, chunk])

    for chunk in range(chunks):
        for part in range(len(sources)):
            copy(part, chunk).start()
    return copy


def in_kernel(gate_scales, up_scales, gate, up, out, gate_raw, up_raw, sems):
    rows, cols = gate.shape
    chunks = sems.shape[1]
    strip = rows // chunks // BLOCK
    copy = chunk_copies((gate, up), (gate_raw, up_raw), sems)

    @pl.loop(0, chunks)
    def _(chunk):
        copy(0, chunk).wait()
        copy(1, chunk).wait()
        for block in range(strip):
            row = chunk * strip + block
            at = pl.ds(pl.multiple_of(row * BLOCK, BLOCK), BLOCK)
            for col in range(cols // BLOCK):
                source, to = slice(col * BLOCK, (col + 1) * BLOCK), 2 * col * BLOCK
                out[at, to : to + BLOCK] = scaled(gate_raw[at, source], gate_scales[col, row])
                to += BLOCK
                out[at, to : to + BLOCK] = scaled(up_raw[at, source], up_scales[col, row])


def down_kernel(scales, down, out, raw, sems):
    chunks = sems.shape[1]
    strip = down.shape[0] // chunks // BLOCK
    copy = chunk_copies((down,), (raw,), sems)

    @pl.loop(0, chunks)
    def _(chunk):
        copy(0, chunk).wait()
        for block in range(strip):
            row = chunk * strip + block
            at = pl.ds(pl.multiple_of(row * BLOCK, BLOCK), BLOCK)
            for col in range(down.shape[1] // BLOCK):
                cols = slice(col * BLOCK, (col + 1) * BLOCK)
                out[at, cols] = scaled(raw[at, cols], scales[row, col])


def dequantize_call(kernel, name, quants, scales, width, chunks):
    rows, cols = quants[0].shape
    quants = [pltpu.with_memory_space_constraint(quant, pltpu.HBM) for quant in quants]
    return pl.pallas_call(
        kernel,
        in_specs=[pl.BlockSpec(memory_space=pltpu.SMEM)] * len(scales)
        + [pl.BlockSpec(memory_space=pl.ANY)] * len(quants),
        out_specs=pl.BlockSpec(memory_space=pltpu.VMEM),
        out_shape=jax.ShapeDtypeStruct((rows, width), jnp.bfloat16),
        scratch_shapes=[
            *(pltpu.VMEM(quant.shape, jnp.bfloat16) for quant in quants),
            pltpu.SemaphoreType.DMA((len(quants), chunks)),
        ],
        cost_estimate=pl.CostEstimate(
            flops=rows * width, bytes_accessed=4 * rows * width, transcendentals=0
        ),
        compiler_params=pltpu.CompilerParams(vmem_limit_bytes=16 * 1024 * 1024),
        name=name,
    )(*scales, *quants)


def dequantize_in(gate, up, gate_scales, up_scales):
    rows, cols = gate.shape
    chunks = max(1, rows // (4 * BLOCK))
    scales = (gate_scales, up_scales)
    return dequantize_call(in_kernel, "dequantize_in", (gate, up), scales, 2 * cols, chunks)


def dequantize_down(down, scales):
    rows, cols = down.shape
    return dequantize_call(down_kernel, "dequantize_down", (down,), (scales,), cols, rows // BLOCK)


def silu(v):
    return v / (1 + jnp.exp(-v))


def expert_kernel(count, experts, own_expert, *refs):
    pieces, refs = refs[:count], refs[count:]
    in_refs, down_refs, refs = refs[:2], refs[2:4], refs[4:]
    outs, (rows, hidden) = refs[:count], refs[count:]
    size, (half, model_width) = pieces[0].shape[0], down_refs[0].shape
    strip = min(4 * BLOCK, model_width)

    weights = []
    for place, piece in enumerate(pieces):
        rows[place * size : (place + 1) * size, :] = piece[:, :model_width]
        marks = piece[:, model_width:].astype(jnp.float32)
        column = lax.broadcasted_iota(jnp.int32, marks.shape, 1)
        chosen = (column == own_expert[0]) | (column == own_expert[0] + experts)
        weights.append(jnp.sum(jnp.where(chosen, marks, 0.0), axis=1, keepdims=True))
    for part, in_ref in enumerate(in_refs):
        for col in range(half // BLOCK):
            at = slice(2 * col * BLOCK, 2 * (col + 1) * BLOCK)
            both = jnp.dot(rows[...], in_ref[:, at], preferred_element_type=jnp.float32)
            value = (silu(both[:, :BLOCK]) * both[:, BLOCK:]).astype(jnp.bfloat16)
            to = part * half + col * BLOCK
            hidden[:, to : to + BLOCK] = value
    for first in range(0, model_width, strip):
        at = slice(first, first + strip)
        value = jnp.dot(hidden[:, :half], down_refs[0][:, at], preferred_element_type=jnp.float32)
        value += jnp.dot(hidden[:, half:], down_refs[1][:, at], preferred_element_type=jnp.float32)
        for place, out in enumerate(outs):
            weighted = value[place * size : (place + 1) * size] * weights[place]
            out[:, at] = weighted.astype(jnp.bfloat16)


def expert_layer(pieces, own_expert, experts, *weights):
    count, size = len(pieces), pieces[0].shape[0]
    model_width, width = weights[0].shape
    total = count * size
    whole = pl.BlockSpec(memory_space=pltpu.VMEM)
    weights = [pltpu.with_memory_space_constraint(weight, pltpu.VMEM) for weight in weights]
    return pl.pallas_call(
        functools.partial(expert_kernel, count, experts),
        in_specs=[pl.BlockSpec(memory_space=pltpu.SMEM)] + [whole] * (count + len(weights)),
        out_specs=[whole] * count,
        out_shape=[jax.ShapeDtypeStruct((size, model_width), jnp.bfloat16)] * count,
        scratch_shapes=[
            pltpu.VMEM((total, model_width), jnp.bfloat16),
            pltpu.VMEM((total, width), jnp.bfloat16),
        ],
        cost_estimate=pl.CostEstimate(
            flops=6 * total * model_width * width,
            bytes_accessed=6 * model_width * width + 4 * total * model_width,
            transcendentals=total * width,
        ),
        compiler_params=pltpu.CompilerParams(vmem_limit_bytes=16 * 1024 * 1024),
        name="expert_layer",
    )(own_expert, *pieces, *weights)


def across_chips(block, far):
    count = lax.axis_size("expert")
    return lax.ppermute(block, "expert", [(low, low ^ 2 * far) for low in range(count)])


def by_sums(tokens, expert_ids, gate_vals, gate_q, up_q, down_q, gate_scale, up_scale, down_scale):
    token_count, model_width = tokens.shape
    group_count = lax.axis_size("dp")
    pair_count = lax.axis_size("expert") // 2
    expert_count = group_count * pair_count
    own_expert = lax.axis_index("dp") * pair_count + lax.axis_index("expert") // 2
    bits = list(range(group_count.bit_length() - 1))
    orders = (bits, bits[::-1])

    named = expert_ids[:, :, None] == jnp.arange(expert_count, dtype=jnp.int32)[None, None, :]
    weight = jnp.sum(jnp.where(named, gate_vals[:, :, None], 0.0), axis=1)
    high = weight.astype(jnp.bfloat16)
    low = (weight - high.astype(jnp.float32)).astype(jnp.bfloat16)
    extra = -(-2 * expert_count // BLOCK) * BLOCK
    pad = jnp.zeros((token_count, extra - 2 * expert_count), jnp.bfloat16)
    half = token_count // 2
    halves = [slice(0, half), slice(half, token_count)]
    payload = [
        jnp.concatenate([part[rows] for part in (tokens, high, low, pad)], axis=1)
        for rows in halves
    ]

    together = lax.optimization_barrier
    place = jnp.reshape(own_expert, (1,)).astype(jnp.int32)
    turns = len(bits)
    groups = [(0,), *((far, far + 1) for far in range(1, pair_count - 1, 2)), (pair_count - 1,)]

    def lanes_of(group):
        if len(group) == 2:
            return [came[far] for far in group]
        return [came[group[0]][:half], came[group[0]][half:]]

    def along_z(far):
        low = far & -far
        came[far] = across_chips(came[far ^ low], low)

    def gather_turn(number, turn):
        blocks = lanes[number]
        arrived = [from_partner(block, "dp", orders[lane][turn]) for lane, block in enumerate(blocks)]
        if turn == turns - 1:
            lanes[number] = [part for pair in zip(blocks, arrived) for part in pair]
        else:
            lanes[number] = [jnp.concatenate(pair, axis=0) for pair in zip(blocks, arrived)]

    def layer(number):
        return expert_layer(lanes[number], place, expert_count, *weights)

    place, payload = together((place, payload))
    lanes, outs = {0: payload}, {}
    near = [{far: across_chips(payload[0], far) for far in groups[1]}]
    gather_turn(0, 0)
    in_own = dequantize_in(gate_q[0], up_q[0], gate_scale[0].T, up_scale[0].T)
    lanes, near, payload, in_own, down_own = together((lanes, near, payload, in_own, down_q[0]))
    in_other = from_partner(in_own, "expert", 0)
    down_own = dequantize_down(down_own, down_scale[0])
    near.append({far: across_chips(payload[1], far) for far in groups[1]})
    for turn in range(1, turns):
        gather_turn(0, turn)
    lanes, near, down_own = together((lanes, near, down_own))
    came = {far: jnp.concatenate([part[far] for part in near], axis=0) for far in groups[1]}
    down_other = from_partner(down_own, "expert", 0)
    lanes[1] = lanes_of(groups[1])
    for number in range(1, len(groups)):
        following = groups[number + 1] if number + 1 < len(groups) else ()
        for turn in range(int(number > 1), turns - 1):
            gather_turn(number, turn)
            if turn == int(number > 1):
                for far in following:
                    along_z(far)
            tied = (lanes, came, outs, in_other, down_other)
            lanes, came, outs, in_other, down_other = together(tied)
        weights = (in_own, in_other, down_own, down_other)
        gather_turn(number, turns - 1)
        if following:
            if turns - 1 == int(number > 1):
                for far in following:
                    along_z(far)
            lanes[number + 1] = lanes_of(following)
            gather_turn(number + 1, 0)
        if number + 1 == len(groups):
            break
        outs[number - 1] = layer(number - 1)
        if number + 2 != len(groups):
            lanes, outs, came = together((lanes, outs, came))
    final = len(groups) - 1
    sums, merged, parts = {}, {}, []

    def sum_turn(number, turn):
        result = []
        for lane in range(2):
            if turn == turns - 1:
                kept, sent = outs[number][2 * lane : 2 * lane + 2]
            else:
                kept, sent = jnp.split(sums[number][lane], 2, axis=0)
            result.append(added(kept, from_partner(sent, "dp", orders[lane][turn])))
        sums[number] = result

    def leave(number):
        group, done = groups[number], sums.pop(number)
        done = done if len(group) == 2 else [jnp.concatenate(done, axis=0)]
        ready = dict(zip(group, done))
        for far in reversed(group):
            block, low = ready[far], far & -far
            if far in merged:
                block = added(block, merged.pop(far))
            if far != low:
                came_back = across_chips(block, low)
                into = far ^ low
                merged[into] = added(merged[into], came_back) if into in merged else came_back
            else:
                whole = across_chips(block, low)
                parts.append([whole[rows] for rows in halves])

    sum_turn(0, turns - 1)
    outs[final - 1] = layer(final - 1)
    lanes, outs, sums = together((lanes, outs, sums))
    outs[final] = layer(final)
    for number in range(final, 0, -1):
        for turn in range(turns - 1 - int(number < final), -1, -1):
            sum_turn(number, turn)
            if turn == 0 and number > 1:
                sum_turn(number - 1, turns - 1)
        if number > 1:
            leave(number)
        sums, outs = together((sums, outs))
    leave(1)
    for turn in range(turns - 2, -1, -1):
        sum_turn(0, turn)
    result = []
    for lane, rows in enumerate(halves):
        total = tokens[rows].astype(jnp.float32) + sums[0][lane].astype(jnp.float32)
        for part in parts:
            total = total + part[lane].astype(jnp.float32)
        result.append(total.astype(jnp.bfloat16))
    return jnp.concatenate(result, axis=0)


def shards(tokens, expert_ids, *weights):
    expert_count = lax.axis_size("dp") * lax.axis_size("expert") // 2
    token_count, top_count = expert_ids.shape
    capacity = 2 * token_count * top_count // expert_count
    group_count, pair_count = lax.axis_size("dp"), lax.axis_size("expert") // 2
    powers = all(count & (count - 1) == 0 for count in (group_count, pair_count))
    dense = capacity >= token_count and powers and min(group_count, pair_count) >= 4
    plan = by_sums if dense else by_rows
    return plan(tokens, expert_ids, *weights)


def solution(mesh):
    return jax.shard_map(
        shards,
        mesh=mesh,
        in_specs=(
            P(("dp", "expert"), None),
            P(("dp", "expert"), None),
            P(("dp", "expert"), None),
            P("dp", None, "expert"),
            P("dp", None, "expert"),
            P("dp", "expert", None),
            P("dp", None, "expert"),
            P("dp", None, "expert"),
            P("dp", "expert", None),
        ),
        out_specs=P(("dp", "expert"), None),
        check_vma=False,
    )
```

```python
import functools

import jax
import jax.numpy as jnp
from jax import lax
from jax.experimental import pallas as pl
from jax.experimental.pallas import tpu as pltpu
from jax.sharding import PartitionSpec as P

BLOCK = 128


def from_partner(block, axis, bit):
    count = lax.axis_size(axis)
    route = []
    for low in range(count):
        high = low | 1 << bit
        if high != low and high < count:
            route += [(low, high), (high, low)]
    return lax.ppermute(block, axis, route)


def dequantize(quant_vals, block_scale):
    row_count, col_count = quant_vals.shape
    blocked = quant_vals.reshape(row_count // BLOCK, BLOCK, col_count // BLOCK, BLOCK).astype(
        jnp.float32
    )
    scaled = blocked * block_scale[:, None, :, None]
    return scaled.reshape(row_count, col_count).astype(jnp.bfloat16)


def expert_ffn(inputs, w_gate, w_up, w_down):
    gate_part = jnp.dot(inputs, w_gate, preferred_element_type=jnp.float32)
    up_part = jnp.dot(inputs, w_up, preferred_element_type=jnp.float32)
    hidden = (jax.nn.silu(gate_part) * up_part).astype(jnp.bfloat16)
    return jnp.dot(hidden, w_down, preferred_element_type=jnp.float32)


def across_groups(blocks):
    return lax.all_to_all(blocks, "dp", split_axis=1, concat_axis=1, tiled=True)


def across_owners(blocks):
    return lax.all_to_all(blocks, "expert", split_axis=0, concat_axis=0, tiled=True)


def by_rows(tokens, expert_ids, gate_vals, gate_q, up_q, down_q, gate_scale, up_scale, down_scale):
    group_count = lax.axis_size("dp")
    owner_count = lax.axis_size("expert")
    token_count, model_width = tokens.shape
    top_count = expert_ids.shape[1]
    pair_count = owner_count // 2
    expert_count = group_count * pair_count
    capacity = 2 * token_count * top_count // expert_count
    half_cap = capacity // 2
    slot_count = owner_count * group_count * half_cap
    routes = expert_ids.reshape(-1)
    onehot = (routes[:, None] == jnp.arange(expert_count, dtype=jnp.int32)[None, :]).astype(
        jnp.int32
    )
    earlier = jnp.cumsum(onehot, axis=0) - onehot
    route_slot = jnp.sum(earlier * onehot, axis=1)
    route_group = routes // pair_count
    route_pair = routes % pair_count
    route_owner = 2 * route_pair + route_slot // half_cap
    route_place = route_slot % half_cap
    route_index = (route_owner * group_count + route_group) * half_cap + route_place
    chosen = jnp.arange(slot_count, dtype=jnp.int32)[:, None] == route_index[None, :]
    chosen = jnp.any(chosen.reshape(slot_count, token_count, top_count), axis=2).astype(
        jnp.bfloat16
    )
    outgoing = jnp.dot(chosen, tokens, preferred_element_type=jnp.float32).astype(jnp.bfloat16)
    outgoing = outgoing.reshape(owner_count, group_count, half_cap, model_width)
    arrived = across_owners(across_groups(outgoing))
    own_rows = arrived.reshape(-1, model_width)
    row_count = own_rows.shape[0]
    w_gate = dequantize(gate_q[0], gate_scale[0])
    w_up = dequantize(up_q[0], up_scale[0])
    w_down = dequantize(down_q[0], down_scale[0])
    partner_rows = from_partner(own_rows, "expert", 0)
    both_rows = jnp.concatenate([own_rows, partner_rows], axis=0)
    partial_value = expert_ffn(both_rows, w_gate, w_up, w_down)
    returned = from_partner(partial_value[row_count:], "expert", 0)
    expert_out = (partial_value[:row_count] + returned).astype(jnp.bfloat16)
    expert_out = expert_out.reshape(owner_count, group_count, half_cap, model_width)
    returned_rows = across_groups(across_owners(expert_out))
    returned_rows = returned_rows.reshape(slot_count, model_width)
    picked = returned_rows[route_index].reshape(token_count, top_count, model_width)
    weighted = jnp.einsum("tkd,tk->td", picked.astype(jnp.float32), gate_vals)
    mixed = tokens.astype(jnp.float32) + weighted
    return mixed.astype(jnp.bfloat16)


def added(block, arrived):
    return (block.astype(jnp.float32) + arrived.astype(jnp.float32)).astype(jnp.bfloat16)


def scaled(block, scale):
    return (block.astype(jnp.float32) * scale).astype(jnp.bfloat16)


def chunk_copies(sources, targets, sems):
    chunks = sems.shape[1]
    depth = sources[0].shape[0] // chunks

    def copy(part, chunk):
        at = pl.ds(pl.multiple_of(chunk * depth, depth), depth)
        return pltpu.make_async_copy(sources[part].at[at], targets[part].at[at], sems.at[part, chunk])

    for chunk in range(chunks):
        for part in range(len(sources)):
            copy(part, chunk).start()
    return copy


def in_kernel(gate_scales, up_scales, gate, up, out, gate_raw, up_raw, sems):
    rows, cols = gate.shape
    chunks = sems.shape[1]
    strip = rows // chunks // BLOCK
    copy = chunk_copies((gate, up), (gate_raw, up_raw), sems)

    @pl.loop(0, chunks)
    def _(chunk):
        copy(0, chunk).wait()
        copy(1, chunk).wait()
        for block in range(strip):
            row = chunk * strip + block
            at = pl.ds(pl.multiple_of(row * BLOCK, BLOCK), BLOCK)
            for col in range(cols // BLOCK):
                source, to = slice(col * BLOCK, (col + 1) * BLOCK), 2 * col * BLOCK
                out[at, to : to + BLOCK] = scaled(gate_raw[at, source], gate_scales[col, row])
                to += BLOCK
                out[at, to : to + BLOCK] = scaled(up_raw[at, source], up_scales[col, row])


def down_kernel(scales, down, out, raw, sems):
    chunks = sems.shape[1]
    strip = down.shape[0] // chunks // BLOCK
    copy = chunk_copies((down,), (raw,), sems)

    @pl.loop(0, chunks)
    def _(chunk):
        copy(0, chunk).wait()
        for block in range(strip):
            row = chunk * strip + block
            at = pl.ds(pl.multiple_of(row * BLOCK, BLOCK), BLOCK)
            for col in range(down.shape[1] // BLOCK):
                cols = slice(col * BLOCK, (col + 1) * BLOCK)
                out[at, cols] = scaled(raw[at, cols], scales[row, col])


def dequantize_call(kernel, name, quants, scales, width, chunks):
    rows, cols = quants[0].shape
    quants = [pltpu.with_memory_space_constraint(quant, pltpu.HBM) for quant in quants]
    return pl.pallas_call(
        kernel,
        in_specs=[pl.BlockSpec(memory_space=pltpu.SMEM)] * len(scales)
        + [pl.BlockSpec(memory_space=pl.ANY)] * len(quants),
        out_specs=pl.BlockSpec(memory_space=pltpu.VMEM),
        out_shape=jax.ShapeDtypeStruct((rows, width), jnp.bfloat16),
        scratch_shapes=[
            *(pltpu.VMEM(quant.shape, jnp.bfloat16) for quant in quants),
            pltpu.SemaphoreType.DMA((len(quants), chunks)),
        ],
        cost_estimate=pl.CostEstimate(
            flops=rows * width, bytes_accessed=4 * rows * width, transcendentals=0
        ),
        compiler_params=pltpu.CompilerParams(vmem_limit_bytes=16 * 1024 * 1024),
        name=name,
    )(*scales, *quants)


def dequantize_in(gate, up, gate_scales, up_scales):
    rows, cols = gate.shape
    chunks = max(1, rows // (4 * BLOCK))
    scales = (gate_scales, up_scales)
    return dequantize_call(in_kernel, "dequantize_in", (gate, up), scales, 2 * cols, chunks)


def dequantize_down(down, scales):
    rows, cols = down.shape
    return dequantize_call(down_kernel, "dequantize_down", (down,), (scales,), cols, rows // BLOCK)


def silu(v):
    return v / (1 + jnp.exp(-v))


def expert_kernel(count, experts, own_expert, *refs):
    pieces, refs = refs[:count], refs[count:]
    in_refs, down_refs, refs = refs[:2], refs[2:4], refs[4:]
    outs, (rows, hidden) = refs[:count], refs[count:]
    size, (half, model_width) = pieces[0].shape[0], down_refs[0].shape
    strip = min(4 * BLOCK, model_width)

    weights = []
    for place, piece in enumerate(pieces):
        rows[place * size : (place + 1) * size, :] = piece[:, :model_width]
        marks = piece[:, model_width:].astype(jnp.float32)
        column = lax.broadcasted_iota(jnp.int32, marks.shape, 1)
        chosen = (column == own_expert[0]) | (column == own_expert[0] + experts)
        weights.append(jnp.sum(jnp.where(chosen, marks, 0.0), axis=1, keepdims=True))
    for part, in_ref in enumerate(in_refs):
        for col in range(half // BLOCK):
            at = slice(2 * col * BLOCK, 2 * (col + 1) * BLOCK)
            both = jnp.dot(rows[...], in_ref[:, at], preferred_element_type=jnp.float32)
            value = (silu(both[:, :BLOCK]) * both[:, BLOCK:]).astype(jnp.bfloat16)
            to = part * half + col * BLOCK
            hidden[:, to : to + BLOCK] = value
    for first in range(0, model_width, strip):
        at = slice(first, first + strip)
        value = jnp.dot(hidden[:, :half], down_refs[0][:, at], preferred_element_type=jnp.float32)
        value += jnp.dot(hidden[:, half:], down_refs[1][:, at], preferred_element_type=jnp.float32)
        for place, out in enumerate(outs):
            weighted = value[place * size : (place + 1) * size] * weights[place]
            out[:, at] = weighted.astype(jnp.bfloat16)


def expert_layer(pieces, own_expert, experts, *weights):
    count, size = len(pieces), pieces[0].shape[0]
    model_width, width = weights[0].shape
    total = count * size
    whole = pl.BlockSpec(memory_space=pltpu.VMEM)
    weights = [pltpu.with_memory_space_constraint(weight, pltpu.VMEM) for weight in weights]
    return pl.pallas_call(
        functools.partial(expert_kernel, count, experts),
        in_specs=[pl.BlockSpec(memory_space=pltpu.SMEM)] + [whole] * (count + len(weights)),
        out_specs=[whole] * count,
        out_shape=[jax.ShapeDtypeStruct((size, model_width), jnp.bfloat16)] * count,
        scratch_shapes=[
            pltpu.VMEM((total, model_width), jnp.bfloat16),
            pltpu.VMEM((total, width), jnp.bfloat16),
        ],
        cost_estimate=pl.CostEstimate(
            flops=6 * total * model_width * width,
            bytes_accessed=6 * model_width * width + 4 * total * model_width,
            transcendentals=total * width,
        ),
        compiler_params=pltpu.CompilerParams(vmem_limit_bytes=16 * 1024 * 1024),
        name="expert_layer",
    )(own_expert, *pieces, *weights)


def across_chips(block, far):
    count = lax.axis_size("expert")
    return lax.ppermute(block, "expert", [(low, low ^ 2 * far) for low in range(count)])


def by_sums(tokens, expert_ids, gate_vals, gate_q, up_q, down_q, gate_scale, up_scale, down_scale):
    token_count, model_width = tokens.shape
    group_count = lax.axis_size("dp")
    pair_count = lax.axis_size("expert") // 2
    expert_count = group_count * pair_count
    own_expert = lax.axis_index("dp") * pair_count + lax.axis_index("expert") // 2
    bits = list(range(group_count.bit_length() - 1))
    orders = (bits, bits[::-1])

    named = expert_ids[:, :, None] == jnp.arange(expert_count, dtype=jnp.int32)[None, None, :]
    weight = jnp.sum(jnp.where(named, gate_vals[:, :, None], 0.0), axis=1)
    high = weight.astype(jnp.bfloat16)
    low = (weight - high.astype(jnp.float32)).astype(jnp.bfloat16)
    extra = -(-2 * expert_count // BLOCK) * BLOCK
    pad = jnp.zeros((token_count, extra - 2 * expert_count), jnp.bfloat16)
    half = token_count // 2
    halves = [slice(0, half), slice(half, token_count)]
    payload = [
        jnp.concatenate([part[rows] for part in (tokens, high, low, pad)], axis=1)
        for rows in halves
    ]

    together = lax.optimization_barrier
    place = jnp.reshape(own_expert, (1,)).astype(jnp.int32)
    turns = len(bits)
    groups = [(0,), *((far, far + 1) for far in range(1, pair_count - 1, 2)), (pair_count - 1,)]

    def lanes_of(group):
        if len(group) == 2:
            return [came[far] for far in group]
        return [came[group[0]][:half], came[group[0]][half:]]

    def along_z(far):
        low = far & -far
        came[far] = across_chips(came[far ^ low], low)

    def gather_turn(number, turn):
        blocks = lanes[number]
        arrived = [from_partner(block, "dp", orders[lane][turn]) for lane, block in enumerate(blocks)]
        if turn == turns - 1:
            lanes[number] = [part for pair in zip(blocks, arrived) for part in pair]
        else:
            lanes[number] = [jnp.concatenate(pair, axis=0) for pair in zip(blocks, arrived)]

    def layer(number):
        return expert_layer(lanes[number], place, expert_count, *weights)

    place, payload = together((place, payload))
    lanes, outs = {0: payload}, {}
    near = [{far: across_chips(payload[0], far) for far in groups[1]}]
    gather_turn(0, 0)
    in_own = dequantize_in(gate_q[0], up_q[0], gate_scale[0].T, up_scale[0].T)
    lanes, near, payload, in_own, down_own = together((lanes, near, payload, in_own, down_q[0]))
    in_other = from_partner(in_own, "expert", 0)
    down_own = dequantize_down(down_own, down_scale[0])
    near.append({far: across_chips(payload[1], far) for far in groups[1]})
    for turn in range(1, turns):
        gather_turn(0, turn)
    lanes, near, down_own = together((lanes, near, down_own))
    came = {far: jnp.concatenate([part[far] for part in near], axis=0) for far in groups[1]}
    down_other = from_partner(down_own, "expert", 0)
    lanes[1] = lanes_of(groups[1])
    for number in range(1, len(groups)):
        following = groups[number + 1] if number + 1 < len(groups) else ()
        for turn in range(int(number > 1), turns - 1):
            gather_turn(number, turn)
            if turn == int(number > 1):
                for far in following:
                    along_z(far)
            tied = (lanes, came, outs, in_other, down_other)
            lanes, came, outs, in_other, down_other = together(tied)
        weights = (in_own, in_other, down_own, down_other)
        gather_turn(number, turns - 1)
        if following:
            if turns - 1 == int(number > 1):
                for far in following:
                    along_z(far)
            lanes[number + 1] = lanes_of(following)
            gather_turn(number + 1, 0)
        if number + 1 == len(groups):
            break
        outs[number - 1] = layer(number - 1)
        if number + 2 != len(groups):
            lanes, outs, came = together((lanes, outs, came))
    final = len(groups) - 1
    sums, merged, parts = {}, {}, []

    def sum_turn(number, turn):
        result = []
        for lane in range(2):
            if turn == turns - 1:
                kept, sent = outs[number][2 * lane : 2 * lane + 2]
            else:
                kept, sent = jnp.split(sums[number][lane], 2, axis=0)
            result.append(added(kept, from_partner(sent, "dp", orders[lane][turn])))
        sums[number] = result

    def leave(number):
        group, done = groups[number], sums.pop(number)
        done = done if len(group) == 2 else [jnp.concatenate(done, axis=0)]
        ready = dict(zip(group, done))
        for far in reversed(group):
            block, low = ready[far], far & -far
            if far in merged:
                block = added(block, merged.pop(far))
            if far != low:
                came_back = across_chips(block, low)
                into = far ^ low
                merged[into] = added(merged[into], came_back) if into in merged else came_back
            else:
                whole = across_chips(block, low)
                parts.append([whole[rows] for rows in halves])

    lanes[final - 1], outs = together((lanes[final - 1], outs))
    sum_turn(0, turns - 1)
    outs[final - 1] = layer(final - 1)
    lanes, outs, sums = together((lanes, outs, sums))
    outs[final] = layer(final)
    for number in range(final, 0, -1):
        for turn in range(turns - 1 - int(number < final), -1, -1):
            sum_turn(number, turn)
            if turn == turns - 1:
                sums[number], outs[number - 1] = together((sums[number], outs[number - 1]))
            if turn == 0 and number > 1:
                sum_turn(number - 1, turns - 1)
        if number > 1:
            leave(number)
        sums, outs, merged = together((sums, outs, merged))
    leave(1)
    for turn in range(turns - 2, -1, -1):
        sum_turn(0, turn)
    result = []
    for lane, rows in enumerate(halves):
        total = tokens[rows].astype(jnp.float32) + sums[0][lane].astype(jnp.float32)
        for part in parts:
            total = total + part[lane].astype(jnp.float32)
        result.append(total.astype(jnp.bfloat16))
    return jnp.concatenate(result, axis=0)


def shards(tokens, expert_ids, *weights):
    expert_count = lax.axis_size("dp") * lax.axis_size("expert") // 2
    token_count, top_count = expert_ids.shape
    capacity = 2 * token_count * top_count // expert_count
    group_count, pair_count = lax.axis_size("dp"), lax.axis_size("expert") // 2
    powers = all(count & (count - 1) == 0 for count in (group_count, pair_count))
    dense = capacity >= token_count and powers and min(group_count, pair_count) >= 4
    plan = by_sums if dense else by_rows
    return plan(tokens, expert_ids, *weights)


def solution(mesh):
    return jax.shard_map(
        shards,
        mesh=mesh,
        in_specs=(
            P(("dp", "expert"), None),
            P(("dp", "expert"), None),
            P(("dp", "expert"), None),
            P("dp", None, "expert"),
            P("dp", None, "expert"),
            P("dp", "expert", None),
            P("dp", None, "expert"),
            P("dp", None, "expert"),
            P("dp", "expert", None),
        ),
        out_specs=P(("dp", "expert"), None),
        check_vma=False,
    )
```
